256 devices in a mesh: dp: 32 (over z_lo, x, core), mp: 8 (over y, z_hi).
Axes of the slice: x: 4, y: 4, z: 8 (z_hi: 2, z_lo: 4; z = z_hi * 4 + z_lo), core: 2. Of those that a mesh axis runs over, the one named last changes fastest.
Arguments:
- attn_out: bfloat16 [2, 4096, 4096], P(None, 'dp', 'mp'), may hold values from -24 to 24
- residual: bfloat16 [2, 4096, 4096], P(None, 'dp', 'mp'), may hold values from -24 to 24
- o_weight: bfloat16 [4096, 4096], P('mp'), may hold values from -0.09375 to 0.09375
- norm_gain: float32 [4096], P('mp'), may hold values from 0.1 to 1.9
- positive: int32 [4096], P('dp'), may hold values from 0 to 4095, each once
Outputs:
- pair_loss: float32 [4096], P('dp')
- resid_grad: float32 [2, 4096, 4096], P(None, 'dp', 'mp')
- attn_grad: float32 [2, 4096, 4096], P(None, 'dp', 'mp')
- weight_grad: float32 [4096, 4096], P('mp', 'dp')
The draws below stay inside these ranges and needn't reach their ends.
Inputs may be any that keep to these rules, and one draw needn't show every extreme that they name: Each response is the positive of exactly one query.
All inputs are finite; a program needn't handle non-finite values.
Results may differ from the reference program's by a relative error of at most 0.0041.
Values may be sent and summed in bfloat16 or wider, within the bound.
A program may use at most 64 MiB of HBM per device.

```python
import jax
import jax.numpy as jnp
from jax import lax

D = 4096
PAIRS = 4096


def draw_attn_out(key, part):
    key = jax.random.fold_in(key, 11)
    values = jax.random.normal(key, (2, PAIRS, D), jnp.float32)
    return jnp.clip(values, -6.0, 6.0).astype(jnp.bfloat16)


def draw_residual(key, part):
    key = jax.random.fold_in(key, 23)
    values = jax.random.normal(key, (2, PAIRS, D), jnp.float32)
    return jnp.clip(values, -6.0, 6.0).astype(jnp.bfloat16)


def levels(rng, extent, pieces, least, top_value):
    gain = 1.0
    for position, parts in pieces:
        draws = jax.random.uniform(jax.random.fold_in(jax.random.fold_in(rng, 6), position), (parts,), jnp.float32, least / len(pieces), top_value / len(pieces))
        gain = gain * jnp.repeat(jnp.exp(draws), extent[position] // parts).reshape((-1,) + (1,) * (len(extent) - 1 - position))
    return gain


def bell_draw(stream_key, shape, scale, most, cuts=(), kind=jnp.bfloat16):
    gain = levels(stream_key, shape, cuts, -0.22, 0.18) if cuts else 1.0
    values = jax.random.normal(stream_key, shape, jnp.float32) * scale * gain
    return jnp.minimum(jnp.maximum(values, -most), most).astype(kind)


def setup_inputs(seed: int = 0) -> dict:
    arg_keys = jax.random.split(jax.random.key(seed), 6)
    return {
        "attn_out": draw_attn_out(jax.random.fold_in(arg_keys[5], 71), 0),
        "residual": draw_residual(jax.random.fold_in(arg_keys[5], 71), 0),
        "o_weight": bell_draw(arg_keys[2], (D, D), D ** -0.5, 0.09375, ((0, 8),)),
        "norm_gain": jnp.clip(1.0 + 0.18 * jax.random.normal(arg_keys[3], (D,), jnp.float32), 0.1, 1.9),
        "positive": jax.random.permutation(arg_keys[4], PAIRS).astype(jnp.int32),
    }


LOGIT_SCALE = 50.0
EPS = 1e-06

def reference(attn_out, residual, o_weight, norm_gain, positive):
    attn_rows = attn_out.reshape(2 * PAIRS, D)
    projected = jnp.dot(attn_rows, o_weight, preferred_element_type=jnp.float32)
    scaled = (residual.reshape(2 * PAIRS, D).astype(jnp.float32) + projected) * norm_gain
    inverse = lax.rsqrt(lax.optimization_barrier(jnp.sum(scaled * scaled, axis=1)) + EPS)
    embedded = (scaled * inverse[:, None]).astype(jnp.bfloat16)
    queries = embedded[:PAIRS]
    answers = embedded[PAIRS:]
    logits = LOGIT_SCALE * lax.dot_general(queries, answers, (((1,), (1,)), ((), ())), preferred_element_type=jnp.float32)
    row_top = lax.optimization_barrier(jnp.max(logits, axis=1))
    log_total = row_top + jnp.log(lax.optimization_barrier(jnp.sum(jnp.exp(logits - row_top[:, None]), axis=1)))
    is_positive = positive[:, None] == jnp.arange(PAIRS, dtype=jnp.int32)[None, :]
    pair_loss = log_total - lax.optimization_barrier(jnp.sum(jnp.where(is_positive, logits, 0.0), axis=1))
    score_grad = (LOGIT_SCALE * (jnp.exp(logits - log_total[:, None]) - is_positive.astype(jnp.float32))).astype(jnp.bfloat16)
    grad_queries = jnp.dot(score_grad, answers, preferred_element_type=jnp.float32)
    grad_answers = lax.dot_general(score_grad, queries, (((0,), (0,)), ((), ())), preferred_element_type=jnp.float32)
    grad_embedded = jnp.concatenate([grad_queries, grad_answers], axis=0)
    radial = lax.optimization_barrier(jnp.sum(grad_embedded * scaled, axis=1))
    grad_scaled = inverse[:, None] * grad_embedded - (inverse * inverse * inverse * radial)[:, None] * scaled
    resid_grad = norm_gain * grad_scaled
    grad_wire = resid_grad.astype(jnp.bfloat16)
    attn_grad = lax.dot_general(grad_wire, o_weight, (((1,), (1,)), ((), ())), preferred_element_type=jnp.float32)
    weight_grad = lax.dot_general(attn_rows, grad_wire, (((0,), (0,)), ((), ())), preferred_element_type=jnp.float32)
    return (pair_loss, resid_grad.reshape(2, PAIRS, D), attn_grad.reshape(2, PAIRS, D), weight_grad)
```

```python
import jax
import jax.numpy as jnp
from jax import lax
from jax.sharding import PartitionSpec as P
from jax.experimental import pallas as pl
from jax.experimental.pallas import tpu as pltpu

LOGIT_SCALE = 50.0
EPS = 1e-06
F32 = jnp.float32
BF16 = jnp.bfloat16
MESH = pl.DeviceIdType.MESH
WIRE = BF16

STAGES = dict(
    y1=6, z1=1, ss=7, qx=3, ps=3, ax=3, az=3, ac=4, ly=6, lz=1, tx=3, pl=7,
    sz=1, sy=6, gc=4, gz=3, gq=3, rq=7, ra=7, gh=2, gy=12, gx=24, wc=4, wz=3,
)
BASE = {}
COUNT = 0
for _name, _n in STAGES.items():
    BASE[_name] = COUNT
    COUNT += _n


def nt(a, b):
    return lax.dot_general(a, b, (((1,), (1,)), ((), ())), preferred_element_type=F32)


def tn(a, b):
    return lax.dot_general(a, b, (((0,), (0,)), ((), ())), preferred_element_type=F32)


def nn(a, b):
    return lax.dot_general(a, b, (((1,), (0,)), ((), ())), preferred_element_type=F32)


def to_row(col):
    n = col.shape[0]
    return jnp.broadcast_to(col, (n, 128)).T[0:8]


def to_col(row):
    n = row.shape[1]
    return jnp.broadcast_to(row, (128, n)).T[:, 0:1]


def rows(start, size, unit=None):
    return pl.ds(pl.multiple_of(start, unit or size), size)


def kernel(
    a_ref, r_ref, w_ref, gain_ref, pos_ref,
    loss_ref, rg_ref, ag_ref, wg_ref,
    ys, yr, own, zs, zr, sc, inv_s, ssb,
    qx, aa, px, pt, lg, lr, lzs, lzr, eb, txb, lossb,
    sa, gap, gcr, gzs, gzr, gqs, gqr, ge, rb,
    gg, gx, ax, tb, tcr, wzs, wzr,
    send, recv,
):
    dp = lax.axis_index("dp")
    mp = lax.axis_index("mp")
    core, x, zl = dp % 2, (dp // 2) % 4, dp // 8
    y, zh = mp // 2, mp % 2
    j = mp
    pending = []

    def dev(core=core, x=x, zl=zl, y=y, zh=zh):
        return ((zl * 4 + x) * 2 + core, y * 2 + zh)

    def copy(stage, k, src, dst, to):
        return pltpu.make_async_remote_copy(
            src_ref=src, dst_ref=dst,
            send_sem=send.at[BASE[stage] + k], recv_sem=recv.at[BASE[stage] + k],
            device_id=to, device_id_type=MESH,
        )

    def go(*args):
        c = copy(*args)
        c.start()
        pending.append(c)

    def got(stage, k, dst):
        copy(stage, k, dst, dst, dev(core=1 - core)).wait_recv()

    def ring(v, d):
        return (v + d) % 4

    others = [(d, e) for d in (2, 1, 3, 0) for e in (1, 0) if (d, e) != (0, 0)]

    barrier = pltpu.get_barrier_semaphore()
    peers = [dev(y=ring(y, d), zh=(zh + e) % 2) for d, e in others]
    peers += [dev(x=ring(x, d)) for d in (1, 2, 3)]
    peers += [dev(zl=ring(zl, d)) for d in (1, 2, 3)]
    peers += [dev(core=1 - core)]
    for p in peers:
        pl.semaphore_signal(barrier, inc=1, device_id=p, device_id_type=MESH)

    def wcols(yy, e):
        return w_ref[:, rows(yy * 1024 + e * 512, 512)]

    for er in (0, 1):
        e = (1 - zh) if er == 0 else zh
        for d in (2, 1, 3):
            ys[er * 3 + d - 1] = nn(a_ref[...], wcols(ring(y, d), e)).astype(WIRE)
    px[x] = jnp.broadcast_to(pos_ref[...], (8, 128))
    pl.semaphore_wait(barrier, len(peers))
    for er in (0, 1):
        for d in (2, 1, 3):
            s = er * 3 + d - 1
            go("y1", s, ys.at[s], yr.at[s], dev(y=ring(y, d)))
    for d in (2, 1, 3):
        go("ps", d - 1, px.at[x], px.at[x], dev(x=ring(x, d)))
        go("ax", d - 1, a_ref, ax.at[rows(x * 256, 256)], dev(x=ring(x, d)))
    ax[rows(x * 256, 256), :] = a_ref[...]
    own[0] = nn(a_ref[...], wcols(y, 1 - zh))
    own[1] = nn(a_ref[...], wcols(y, zh))
    for d in (1, 3, 2):
        got("y1", d - 1, yr.at[d - 1])
    zs[...] = (
        own[0] + yr[0].astype(F32) + yr[1].astype(F32) + yr[2].astype(F32)
    ).astype(WIRE)
    go("z1", 0, zs, zr, dev(zh=1 - zh))
    for d in (1, 3, 2):
        got("y1", 3 + d - 1, yr.at[3 + d - 1])
    own[1] = own[1] + yr[3].astype(F32) + yr[4].astype(F32) + yr[5].astype(F32)
    got("z1", 0, zr)
    scaled = (r_ref[...].astype(F32) + (own[1] + zr[...].astype(F32))) * gain_ref[...]
    sc[...] = scaled

    ssb[0] = to_row(jnp.sum(scaled * scaled, axis=1, keepdims=True))
    for d, e in others:
        k = d * 2 + e
        go("ss", k - 1, ssb.at[0], ssb.at[k], dev(y=ring(y, d), zh=(zh + e) % 2))
    for d, e in others[::-1]:
        k = d * 2 + e
        got("ss", k - 1, ssb.at[k])
    total = ssb[0]
    for k in range(1, 8):
        total = total + ssb[k]
    inv = to_col(lax.rsqrt(total[0:1] + EPS))
    inv_s[...] = jnp.broadcast_to(inv, (256, 128))

    emb = (sc[...] * inv).astype(BF16)
    a_at = rows((zl * 2 + core) * 128, 128)
    aa[a_at, :] = emb[128:256]
    for d in (2, 1, 3):
        go("az", d - 1, aa.at[a_at], aa.at[a_at], dev(zl=ring(zl, d)))
    q_at = rows(x * 128, 128)
    qx[q_at, :] = emb[0:128]
    for d in (2, 1, 3):
        go("qx", d - 1, qx.at[q_at], qx.at[q_at], dev(x=ring(x, d)))
    go("ac", 0, aa.at[a_at], aa.at[a_at], dev(core=1 - core))
    for d in (1, 3, 2):
        got("qx", d - 1, qx.at[rows(ring(x, -d) * 128, 128)])

    for t in (0, 1, 3, 2):
        zz = ring(zl, -t)
        if t:
            at = rows((zz * 2 + core) * 128, 128)
            got("az", t - 1, aa.at[at])
            go("ac", t, aa.at[at], aa.at[at], dev(core=1 - core))
        got("ac", t, aa.at[rows((zz * 2 + 1 - core) * 128, 128)])
        lg[:, rows(zz * 256, 256)] = nt(qx[...], aa[rows(zz * 256, 256), :])

    def block(yy, e):
        return rows((yy * 2 + e) * 64, 64)

    for er in (0, 1):
        e = (1 - zh) if er == 0 else zh
        for d in (2, 1, 3):
            s = er * 3 + d - 1
            go("ly", s, lg.at[block(ring(y, d), e)], lr.at[s], dev(y=ring(y, d)))
    for d in (1, 3, 2):
        got("ly", d - 1, lr.at[d - 1])
    lzs[...] = lg[block(y, 1 - zh), :] + lr[0] + lr[1] + lr[2]
    go("lz", 0, lzs, lzr, dev(zh=1 - zh))
    for d in (1, 3, 2):
        got("ps", d - 1, px.at[ring(x, -d)])
    pt[...] = jnp.broadcast_to(px[y].astype(F32)[0:1], (128, 128)).T
    for d in (1, 3, 2):
        got("ly", 3 + d - 1, lr.at[3 + d - 1])
    eb[...] = lg[block(y, zh), :] + lr[3] + lr[4] + lr[5]
    got("lz", 0, lzr)
    logits = LOGIT_SCALE * (eb[...] + lzr[...])

    cols = lax.broadcasted_iota(jnp.int32, (64, 1024), 1)
    answer = (cols // 256) * 1024 + x * 256 + cols % 256
    positive = pt[rows(zh * 64, 64), 0:1].astype(jnp.int32)
    hit = answer == positive
    ex = jnp.exp(logits)
    eb[...] = ex
    sums = jnp.concatenate(
        [
            jnp.sum(ex, axis=1, keepdims=True),
            jnp.sum(jnp.where(hit, logits, 0.0), axis=1, keepdims=True),
        ],
        axis=0,
    )
    txb[0] = to_row(sums)
    for d in (2, 1, 3):
        go("tx", d - 1, txb.at[0], txb.at[d], dev(x=ring(x, d)))
    for d in (1, 3, 2):
        got("tx", d - 1, txb.at[d])
    totals = txb[0] + txb[1] + txb[2] + txb[3]
    col = to_col(totals[0:1])
    scale = LOGIT_SCALE / col[0:64]
    score = eb[...] * scale - jnp.where(hit, LOGIT_SCALE, 0.0)
    mine = block(y, zh)
    sa[mine, :] = score.astype(BF16)

    go("sz", 0, sa.at[mine], sa.at[mine], dev(zh=1 - zh))
    for d in (2, 1, 3):
        go("sy", d - 1, sa.at[mine], sa.at[mine], dev(y=ring(y, d)))
    losses = jnp.log(totals) - jnp.concatenate([totals[:, 64:], totals[:, :64]], axis=1)
    lossb[j] = losses
    for d, e in others:
        go("pl", d * 2 + e - 1, lossb.at[j], lossb.at[j], dev(y=ring(y, d), zh=(zh + e) % 2))
    pair = block(y, 1 - zh)
    got("sz", 0, sa.at[pair])
    for d in (2, 1, 3):
        go("sy", 3 + d - 1, sa.at[pair], sa.at[pair], dev(y=ring(y, d)))
    for k in (0, 1):
        e = zh if k == 0 else 1 - zh
        for d in (1, 3, 2):
            got("sy", k * 3 + d - 1, sa.at[block(ring(y, -d), e)])

    def answers_part(t):
        zz = ring(zl, t)
        gap[t] = tn(sa[:, rows(zz * 256, 256)], qx[...])
        away = rows((1 - core) * 128, 128)
        go("gc", t, gap.at[t, away], gcr.at[t], dev(core=1 - core))

    def answers_sum(t):
        got("gc", t, gcr.at[t])
        gzs[t] = gap[t, rows(core * 128, 128), :] + gcr[t]
        if t:
            go("gz", t - 1, gzs.at[t], gzr.at[t - 1], dev(zl=ring(zl, t)))

    def queries_part(d):
        gqs[d] = nn(sa[rows(ring(x, d) * 128, 128), :], aa[...])
        if d:
            go("gq", d - 1, gqs.at[d], gqr.at[d - 1], dev(x=ring(x, d)))

    answers_part(2)
    answers_part(1)
    answers_sum(2)
    answers_part(3)
    answers_sum(1)
    queries_part(2)
    answers_sum(3)
    queries_part(1)
    queries_part(3)
    answers_part(0)
    queries_part(0)
    answers_sum(0)

    def radial(h, g):
        at = pl.ds(h * 128, 128)
        ge[at, :] = g
        rb[h, 0] = to_row(jnp.sum(g * sc[at, :], axis=1, keepdims=True))
        for d, e in others:
            k = d * 2 + e
            go("rq" if h == 0 else "ra", k - 1, rb.at[h, 0], rb.at[h, k],
               dev(y=ring(y, d), zh=(zh + e) % 2))

    def spread(h):
        at = pl.ds(h * 128, 128)
        tot = rb[h, 0]
        for d, e in others[::-1]:
            k = d * 2 + e
            got("rq" if h == 0 else "ra", k - 1, rb.at[h, k])
        for k in range(1, 8):
            tot = tot + rb[h, k]
        rad = to_col(tot[0:1])
        iv = inv_s[at, 0:1]
        out = gain_ref[...] * (iv * ge[at, :] - (iv * iv * iv * rad) * sc[at, :])
        rg_ref[at, :] = out
        gg[j, at, :] = out.astype(BF16)
        go("gh", h, gg.at[j, at], gg.at[j, at], dev(zh=1 - zh))
        for d in (2, 1, 3):
            go("gy", h * 6 + d - 1, gg.at[j, at], gg.at[j, at], dev(y=ring(y, d)))

    def forward(h):
        at = pl.ds(h * 128, 128)
        jj = y * 2 + 1 - zh
        got("gh", h, gg.at[jj, at])
        for d in (2, 1, 3):
            go("gy", h * 6 + 3 + d - 1, gg.at[jj, at], gg.at[jj, at], dev(y=ring(y, d)))

    def columns(h, t):
        at = pl.ds(h * 128, 128)
        yy = ring(y, -t)
        if t:
            for k in (0, 1):
                e = zh if k == 0 else 1 - zh
                got("gy", h * 6 + k * 3 + t - 1, gg.at[yy * 2 + e, at])
        to = rows(x * 256 + h * 128, 128)
        for d in (2, 1, 3):
            xx = ring(x, d)
            src = gg.at[yy * 2 + xx // 2, at, rows((xx % 2) * 256, 256)]
            go("gx", (t * 2 + h) * 3 + d - 1, src, gx.at[t, to], dev(x=xx))
        gx[t, to, :] = gg[yy * 2 + x // 2, at, rows((x % 2) * 256, 256)]

    for d in (1, 3, 2):
        got("gq", d - 1, gqr.at[d - 1])
    radial(0, gqs[0] + gqr[0] + gqr[1] + gqr[2])
    spread(0)
    for d in (1, 3, 2):
        got("gz", d - 1, gzr.at[d - 1])
    radial(1, gzs[0] + gzr[0] + gzr[1] + gzr[2])
    forward(0)
    spread(1)
    columns(0, 0)
    columns(0, 1)
    forward(1)
    columns(1, 0)
    columns(0, 3)
    columns(0, 2)

    for d in (1, 3, 2):
        got("ax", d - 1, ax.at[rows(ring(x, -d) * 256, 256)])

    def weight_part(t):
        for h in (0, 1):
            for d in (1, 3, 2):
                got("gx", (t * 2 + h) * 3 + d - 1,
                    gx.at[t, rows(ring(x, -d) * 256 + h * 128, 128)])
        part = tn(ax[...], gx[t])
        tb[t, 0] = part[:, 0:128]
        tb[t, 1] = part[:, 128:256]
        go("wc", t, tb.at[t, 1 - core], tcr.at[t], dev(core=1 - core))

    def weight_sum(t):
        got("wc", t, tcr.at[t])
        zz = ring(y, -t)
        d = (zz - zl + 4) % 4
        wzs[d] = tb[t, core] + tcr[t]

        @pl.when(d > 0)
        def _():
            copy("wz", d - 1, wzs.at[d], wzr.at[d - 1], dev(zl=zz)).start()

    weight_part(0)
    columns(1, 1)
    weight_sum(0)
    weight_part(1)
    columns(1, 3)
    weight_sum(1)
    weight_part(3)
    columns(1, 2)
    weight_sum(3)
    weight_part(2)
    weight_sum(2)

    def attn_part(jj, acc):
        return acc + nt(gg[jj], w_ref[:, rows(jj * 512, 512)])

    ag_ref[...] = lax.fori_loop(0, 8, attn_part, jnp.zeros((256, 512), F32))

    for d, e in others:
        jj = ring(y, -d) * 2 + (zh + e) % 2
        got("pl", d * 2 + e - 1, lossb.at[jj])
    loss_ref[...] = jnp.concatenate(
        [lossb[x * 2][0:1, 0:64], lossb[x * 2 + 1][0:1, 0:64]], axis=1
    )
    for d in (1, 3, 2):
        got("wz", d - 1, wzr.at[d - 1])
    wg_ref[...] = wzs[0] + wzr[0] + wzr[1] + wzr[2]
    for c in pending:
        c.wait_send()
    for d in (1, 2, 3):
        copy("wz", d - 1, wzs.at[d], wzr.at[d - 1], dev(core=1 - core)).wait_send()


def body(attn_out, residual, o_weight, norm_gain, positive):
    vmem = pl.BlockSpec(memory_space=pltpu.VMEM)
    shape = jax.ShapeDtypeStruct
    scratch = [
        ((6, 256, 512), WIRE), ((6, 256, 512), WIRE), ((2, 256, 512), F32),
        ((256, 512), WIRE), ((256, 512), WIRE), ((256, 512), F32), ((256, 128), F32),
        ((8, 8, 256), F32),
        ((512, 512), BF16), ((1024, 512), BF16), ((4, 8, 128), jnp.int32), ((128, 128), F32),
        ((512, 1024), F32), ((6, 64, 1024), F32), ((64, 1024), F32), ((64, 1024), F32),
        ((64, 1024), F32), ((4, 8, 128), F32), ((8, 8, 128), F32),
        ((512, 1024), BF16), ((4, 256, 512), F32), ((4, 128, 512), F32), ((4, 128, 512), F32),
        ((3, 128, 512), F32), ((4, 128, 512), F32), ((3, 128, 512), F32), ((256, 512), F32),
        ((2, 8, 8, 128), F32),
        ((8, 256, 512), BF16), ((4, 1024, 256), BF16), ((1024, 512), BF16),
        ((4, 2, 512, 128), F32), ((4, 512, 128), F32), ((4, 512, 128), F32),
        ((3, 512, 128), F32),
    ]
    loss, rg, ag, wg = pl.pallas_call(
        kernel,
        name="step",
        out_shape=(
            shape((1, 128), F32), shape((256, 512), F32), shape((256, 512), F32),
            shape((512, 128), F32),
        ),
        in_specs=[vmem] * 5,
        out_specs=[vmem] * 4,
        scratch_shapes=[pltpu.VMEM(s, t) for s, t in scratch]
        + [pltpu.SemaphoreType.DMA((COUNT,)), pltpu.SemaphoreType.DMA((COUNT,))],
        compiler_params=pltpu.CompilerParams(
            collective_id=0, has_side_effects=True, vmem_limit_bytes=56 * 1024 * 1024
        ),
    )(
        attn_out.reshape(256, 512), residual.reshape(256, 512), o_weight,
        norm_gain.reshape(1, 512), positive.reshape(1, 128),
    )
    return (
        loss.reshape(128), rg.reshape(2, 128, 512), ag.reshape(2, 128, 512), wg,
    )


def solution(mesh):
    placed = (P(None, "dp", "mp"), P(None, "dp", "mp"), P("mp", None), P("mp"), P("dp"))
    return jax.shard_map(
        body,
        mesh=mesh,
        in_specs=placed,
        out_specs=(P("dp"), P(None, "dp", "mp"), P(None, "dp", "mp"), P("mp", "dp")),
        check_vma=False,
    )
```

```python
import jax
import jax.numpy as jnp
from jax import lax
from jax.sharding import PartitionSpec as P
from jax.experimental import pallas as pl
from jax.experimental.pallas import tpu as pltpu

LOGIT_SCALE = 50.0
EPS = 1e-06
F32 = jnp.float32
BF16 = jnp.bfloat16
MESH = pl.DeviceIdType.MESH
WIRE = BF16
GZ_WIRE = F32
WZ_WIRE = F32

STAGES = dict(
    y1=12, z1=2, ss=14, qx=3, ps=3, ax=3, az=3, ac=4, ly=24, lz=4, tx=3, td=7,
    ez=4, ey=24, gc=4, gz=3, gq=3, rr=14, gh=4, gy=24, gx=24, wc=4, wz=3,
)
BASE = {}
COUNT = 0
for _name, _n in STAGES.items():
    BASE[_name] = COUNT
    COUNT += _n


def nt(a, b):
    return lax.dot_general(a, b, (((1,), (1,)), ((), ())), preferred_element_type=F32)


def tn(a, b):
    return lax.dot_general(a, b, (((0,), (0,)), ((), ())), preferred_element_type=F32)


def nn(a, b):
    return lax.dot_general(a, b, (((1,), (0,)), ((), ())), preferred_element_type=F32)


def to_row(col):
    n = col.shape[0]
    return jnp.broadcast_to(col, (n, 128)).T[0:8]


def to_col(row):
    n = row.shape[1]
    return jnp.broadcast_to(row, (128, n)).T[:, 0:1]


def rows(start, size, unit=None):
    return pl.ds(pl.multiple_of(start, unit or size), size)


def kernel(
    a_ref, r_ref, w_ref, gain_ref, pos_ref,
    loss_ref, rg_ref, ag_ref, wg_ref,
    ys, yr, own, zs, zr, sc, inv_s, ssb,
    qx, aa, px, pc, lg, lr, lzs, lzr, pos_s, sums_s, txb, td,
    ea, sa, gap, gcr, gzs, gzr, gqs, gqr, ge, rb,
    gg, gx, ax, tb, tcr, wzs, wzr,
    send, recv,
):
    dp = lax.axis_index("dp")
    mp = lax.axis_index("mp")
    core, x, zl = dp % 2, (dp // 2) % 4, dp // 8
    y, zh = mp // 2, mp % 2
    j = mp
    pending = []

    def dev(core=core, x=x, zl=zl, y=y, zh=zh):
        return ((zl * 4 + x) * 2 + core, y * 2 + zh)

    def copy(stage, k, src, dst, to):
        return pltpu.make_async_remote_copy(
            src_ref=src, dst_ref=dst,
            send_sem=send.at[BASE[stage] + k], recv_sem=recv.at[BASE[stage] + k],
            device_id=to, device_id_type=MESH,
        )

    def go(*args):
        c = copy(*args)
        c.start()
        pending.append(c)

    def got(stage, k, dst):
        copy(stage, k, dst, dst, dev(core=1 - core)).wait_recv()

    def ring(v, d):
        return (v + d) % 4

    others = [(d, e) for d in (2, 1, 3, 0) for e in (1, 0) if (d, e) != (0, 0)]

    barrier = pltpu.get_barrier_semaphore()
    peers = [dev(y=ring(y, d), zh=(zh + e) % 2) for d, e in others]
    peers += [dev(x=ring(x, d)) for d in (1, 2, 3)]
    peers += [dev(zl=ring(zl, d)) for d in (1, 2, 3)]
    peers += [dev(core=1 - core)]
    for p in peers:
        pl.semaphore_signal(barrier, inc=1, device_id=p, device_id_type=MESH)

    def half(h):
        return pl.ds(h * 128, 128)

    def product(h, yy, er):
        e = (1 - zh) if er == 0 else zh
        return nn(a_ref[half(h), :], w_ref[:, rows(yy * 1024 + e * 512, 512)])

    def y_products(h):
        for er in (0, 1):
            for d in (2, 1, 3):
                ys[h * 2 + er, d - 1] = product(h, ring(y, d), er).astype(WIRE)

    def y_send(h):
        for er in (0, 1):
            c = h * 2 + er
            for d in (2, 1, 3):
                go("y1", c * 3 + d - 1, ys.at[c, d - 1], yr.at[c, d - 1], dev(y=ring(y, d)))

    def y_sum(c):
        for d in (1, 3, 2):
            got("y1", c * 3 + d - 1, yr.at[c, d - 1])
        return own[c] + yr[c, 0].astype(F32) + yr[c, 1].astype(F32) + yr[c, 2].astype(F32)

    def z_send(h):
        zs[h] = y_sum(h * 2).astype(WIRE)
        go("z1", h, zs.at[h], zr.at[h], dev(zh=1 - zh))

    def squares(h):
        got("z1", h, zr.at[h])
        proj = own[h * 2 + 1] + zr[h].astype(F32)
        scaled = (r_ref[half(h), :].astype(F32) + proj) * gain_ref[...]
        sc[half(h), :] = scaled
        ssb[h, 0] = to_row(jnp.sum(scaled * scaled, axis=1, keepdims=True))
        for d, e in others:
            k = d * 2 + e
            go("ss", h * 7 + k - 1, ssb.at[h, 0], ssb.at[h, k], dev(y=ring(y, d), zh=(zh + e) % 2))

    def embed(h):
        for d, e in others[::-1]:
            k = d * 2 + e
            got("ss", h * 7 + k - 1, ssb.at[h, k])
        total = ssb[h, 0]
        for k in range(1, 8):
            total = total + ssb[h, k]
        inv = to_col(lax.rsqrt(total[0:1] + EPS))
        inv_s[half(h), :] = jnp.broadcast_to(inv, (128, 128))
        return (sc[half(h), :] * inv).astype(BF16)

    y_products(0)
    px[x] = jnp.broadcast_to(pos_ref[...], (8, 128))
    pl.semaphore_wait(barrier, len(peers))
    y_send(0)
    y_products(1)
    y_send(1)
    for d in (2, 1, 3):
        go("ps", d - 1, px.at[x], px.at[x], dev(x=ring(x, d)))
        go("ax", d - 1, a_ref, ax.at[rows(x * 256, 256)], dev(x=ring(x, d)))
    for h in (0, 1):
        for er in (0, 1):
            own[h * 2 + er] = product(h, y, er)
    ax[rows(x * 256, 256), :] = a_ref[...]

    z_send(0)
    own[1] = y_sum(1)
    z_send(1)
    squares(0)
    emb = embed(0)
    q_at = rows(x * 128, 128)
    qx[q_at, :] = emb
    for d in (2, 1, 3):
        go("qx", d - 1, qx.at[q_at], qx.at[q_at], dev(x=ring(x, d)))
    own[3] = y_sum(3)
    squares(1)
    for d in (1, 3, 2):
        got("ps", d - 1, px.at[ring(x, -d)])
    for xx in range(4):
        pc[pl.ds(xx * 128, 128), :] = jnp.broadcast_to(
            to_col(px[xx].astype(F32)[0:1]), (128, 128)
        )
    for d in (1, 3, 2):
        got("qx", d - 1, qx.at[rows(ring(x, -d) * 128, 128)])
    emb = embed(1)

    a_at = rows((zl * 2 + core) * 128, 128)
    aa[a_at, :] = emb
    go("ac", 0, aa.at[a_at], aa.at[a_at], dev(core=1 - core))
    for d in (2, 1, 3):
        go("az", d - 1, aa.at[a_at], aa.at[a_at], dev(zl=ring(zl, d)))

    def block(yy, e):
        return rows((yy * 2 + e) * 64, 64)

    mine, pair = block(y, zh), block(y, 1 - zh)

    def logit_send(t):
        zz = ring(zl, -t)
        if t:
            at = rows((zz * 2 + core) * 128, 128)
            got("az", t - 1, aa.at[at])
            go("ac", t, aa.at[at], aa.at[at], dev(core=1 - core))
        got("ac", t, aa.at[rows((zz * 2 + 1 - core) * 128, 128)])
        lg[t] = nt(qx[...], aa[rows(zz * 256, 256), :])
        for er in (0, 1):
            e = (1 - zh) if er == 0 else zh
            for d in (2, 1, 3):
                k = er * 3 + d - 1
                go("ly", t * 6 + k, lg.at[t, block(ring(y, d), e)], lr.at[t, k], dev(y=ring(y, d)))

    def logit_pass(t):
        for d in (1, 3, 2):
            got("ly", t * 6 + d - 1, lr.at[t, d - 1])
        lzs[t] = lg[t, pair, :] + lr[t, 0] + lr[t, 1] + lr[t, 2]
        go("lz", t, lzs.at[t], lzr.at[t], dev(zh=1 - zh))

    def hits(t, positive):
        n = positive.shape[0]
        cols = lax.broadcasted_iota(jnp.int32, (n, 256), 1).astype(F32)
        first = (ring(zl, -t) * 1024 + x * 256).astype(F32)
        return cols == positive - first

    def logit_done(t):
        for d in (1, 3, 2):
            got("ly", t * 6 + 3 + d - 1, lr.at[t, 3 + d - 1])
        got("lz", t, lzr.at[t])
        logits = LOGIT_SCALE * (lg[t, mine, :] + lr[t, 3] + lr[t, 4] + lr[t, 5] + lzr[t])
        ex = jnp.exp(logits)
        ea[t, mine, :] = ex.astype(BF16)
        go("ez", t, ea.at[t, mine], ea.at[t, mine], dev(zh=1 - zh))
        for d in (2, 1, 3):
            go("ey", t * 6 + d - 1, ea.at[t, mine], ea.at[t, mine], dev(y=ring(y, d)))
        hit = hits(t, pc[mine, 0:1])
        sums_s[t] = jnp.concatenate(
            [
                jnp.sum(ex, axis=1, keepdims=True),
                jnp.sum(jnp.where(hit, logits, 0.0), axis=1, keepdims=True),
            ],
            axis=0,
        )

    def exp_pass(t):
        got("ez", t, ea.at[t, pair])
        for d in (2, 1, 3):
            go("ey", t * 6 + 3 + d - 1, ea.at[t, pair], ea.at[t, pair], dev(y=ring(y, d)))

    logit_send(0)
    logit_send(1)
    logit_pass(0)
    logit_send(3)
    logit_send(2)
    logit_pass(1)
    logit_done(0)
    logit_pass(3)
    logit_done(1)
    exp_pass(0)
    logit_pass(2)
    logit_done(3)
    exp_pass(1)
    logit_done(2)

    txb[0] = to_row(sums_s[0] + sums_s[1] + sums_s[2] + sums_s[3])
    for d in (2, 1, 3):
        go("tx", d - 1, txb.at[0], txb.at[d], dev(x=ring(x, d)))
    exp_pass(3)
    for d in (1, 3, 2):
        got("tx", d - 1, txb.at[d])
    td[j] = txb[0] + txb[1] + txb[2] + txb[3]
    for d, e in others:
        go("td", d * 2 + e - 1, td.at[j], td.at[j], dev(y=ring(y, d), zh=(zh + e) % 2))
    exp_pass(2)

    for d, e in others[::-1]:
        got("td", d * 2 + e - 1, td.at[ring(y, -d) * 2 + (zh + e) % 2])
    for xx in range(4):
        first, second = td[xx * 2][0:1], td[xx * 2 + 1][0:1]
        total = jnp.concatenate([first[:, 0:64], second[:, 0:64]], axis=1)
        top = jnp.concatenate([first[:, 64:128], second[:, 64:128]], axis=1)
        scale = LOGIT_SCALE / total
        at = pl.ds(xx * 128, 128)
        pos_s[0, at, :] = jnp.broadcast_to(to_col(scale), (128, 128))
        pos_s[1, at, :] = jnp.broadcast_to(
            to_col(jnp.exp(top) * scale - LOGIT_SCALE), (128, 128)
        )

    def score(t):
        for k in (0, 1):
            e = zh if k == 0 else 1 - zh
            for d in (1, 3, 2):
                got("ey", t * 6 + k * 3 + d - 1, ea.at[t, block(ring(y, -d), e)])
        for xx in range(4):
            at = pl.ds(xx * 128, 128)
            rest = ea[t, at, :].astype(F32) * pos_s[0, at, 0:1]
            sa[t, at, :] = jnp.where(
                hits(t, pc[at, 0:1]), pos_s[1, at, 0:1], rest
            ).astype(BF16)

    def answers_part(t):
        gap[t] = tn(sa[t], qx[...])
        away = rows((1 - core) * 128, 128)
        go("gc", t, gap.at[t, away], gcr.at[t], dev(core=1 - core))

    def answers_sum(t):
        got("gc", t, gcr.at[t])
        both = gap[t, rows(core * 128, 128), :] + gcr[t]
        if t:
            gzs[t] = both.astype(GZ_WIRE)
            go("gz", t - 1, gzs.at[t], gzr.at[t - 1], dev(zl=ring(zl, -t)))
        else:
            ge[half(1), :] = both

    def queries_part(d):
        part = jnp.zeros((128, 512), F32)
        for t in range(4):
            left = sa[t, rows(ring(x, d) * 128, 128), :]
            part = part + nn(left, aa[rows(ring(zl, -t) * 256, 256), :])
        gqs[d] = part
        if d:
            go("gq", d - 1, gqs.at[d], gqr.at[d - 1], dev(x=ring(x, d)))

    score(2)
    answers_part(2)
    score(3)
    answers_part(3)
    answers_sum(2)
    score(1)
    answers_part(1)
    answers_sum(3)
    score(0)
    queries_part(2)
    answers_sum(1)
    queries_part(1)
    queries_part(3)
    answers_part(0)
    queries_part(0)
    answers_sum(0)

    def radial(h, g):
        at = half(h)
        ge[at, :] = g
        rb[h, 0] = to_row(jnp.sum(g * sc[at, :], axis=1, keepdims=True))
        for d, e in others:
            k = d * 2 + e
            go("rr", h * 7 + k - 1, rb.at[h, 0], rb.at[h, k], dev(y=ring(y, d), zh=(zh + e) % 2))

    def spread(h):
        at = half(h)
        tot = rb[h, 0]
        for d, e in others[::-1]:
            k = d * 2 + e
            got("rr", h * 7 + k - 1, rb.at[h, k])
        for k in range(1, 8):
            tot = tot + rb[h, k]
        rad = to_col(tot[0:1])
        iv = inv_s[at, 0:1]
        out = gain_ref[...] * (iv * ge[at, :] - (iv * iv * iv * rad) * sc[at, :])
        rg_ref[at, :] = out
        for c in (0, 1):
            gg[j, c, at, :] = out[:, c * 256:(c + 1) * 256].astype(BF16)
        for c in (0, 1):
            part = gg.at[j, c, at]
            go("gh", h * 2 + c, part, part, dev(zh=1 - zh))
        for c in (0, 1):
            part = gg.at[j, c, at]
            for d in (2, 1, 3):
                go("gy", h * 12 + c * 3 + d - 1, part, part, dev(y=ring(y, d)))

    def forward(h):
        for c in (0, 1):
            part = gg.at[y * 2 + 1 - zh, c, half(h)]
            got("gh", h * 2 + c, part)
            for d in (2, 1, 3):
                go("gy", h * 12 + 6 + c * 3 + d - 1, part, part, dev(y=ring(y, d)))

    def columns(h, t):
        at = half(h)
        yy = ring(y, -t)
        if t:
            for k in (0, 1):
                e = zh if k == 0 else 1 - zh
                for c in (0, 1):
                    got("gy", h * 12 + k * 6 + c * 3 + t - 1, gg.at[yy * 2 + e, c, at])
        to = rows(x * 256 + h * 128, 128)
        for d in (2, 1, 3):
            xx = ring(x, d)
            src = gg.at[yy * 2 + xx // 2, xx % 2, at]
            go("gx", (t * 2 + h) * 3 + d - 1, src, gx.at[t, to], dev(x=xx))
        gx[t, to, :] = gg[yy * 2 + x // 2, x % 2, at, :]

    for d in (1, 3, 2):
        got("gq", d - 1, gqr.at[d - 1])
    radial(0, gqs[0] + gqr[0] + gqr[1] + gqr[2])
    spread(0)
    for d in (1, 3, 2):
        got("gz", d - 1, gzr.at[d - 1])
    radial(1, ge[half(1), :] + gzr[0].astype(F32) + gzr[1].astype(F32) + gzr[2].astype(F32))
    forward(0)
    spread(1)
    columns(0, 0)
    columns(0, 1)
    forward(1)
    columns(1, 0)
    columns(0, 3)
    columns(0, 2)

    for d in (1, 3, 2):
        got("ax", d - 1, ax.at[rows(ring(x, -d) * 256, 256)])

    def weight_part(t):
        for h in (0, 1):
            for d in (1, 3, 2):
                got("gx", (t * 2 + h) * 3 + d - 1,
                    gx.at[t, rows(ring(x, -d) * 256 + h * 128, 128)])
        part = tn(ax[...], gx[t])
        tb[t, 0] = part[:, 0:128]
        tb[t, 1] = part[:, 128:256]
        go("wc", t, tb.at[t, 1 - core], tcr.at[t], dev(core=1 - core))

    def weight_sum(t):
        got("wc", t, tcr.at[t])
        zz = ring(y, -t)
        d = (zz - zl + 4) % 4
        both = tb[t, core] + tcr[t]

        @pl.when(d > 0)
        def _():
            wzs[d - 1] = both.astype(WZ_WIRE)
            copy("wz", d - 1, wzs.at[d - 1], wzr.at[d - 1], dev(zl=zz)).start()

        @pl.when(d == 0)
        def _():
            wg_ref[...] = both

    weight_part(0)
    columns(1, 1)
    weight_sum(0)
    weight_part(1)
    columns(1, 3)
    weight_sum(1)
    columns(1, 2)
    weight_part(3)
    weight_sum(3)

    ag_ref[...] = jnp.zeros((256, 512), F32)
    for jj in range(8):
        for c in (0, 1):
            ag_ref[...] += nt(gg[jj, c], w_ref[:, pl.ds(jj * 512 + c * 256, 256)])
    weight_part(2)
    weight_sum(2)
    losses = [
        jnp.log(v[:, 0:64]) - v[:, 64:128] for v in (td[x * 2][0:1], td[x * 2 + 1][0:1])
    ]
    loss_ref[...] = jnp.concatenate(losses, axis=1)
    for d in (1, 3, 2):
        got("wz", d - 1, wzr.at[d - 1])
    wg_ref[...] += wzr[0].astype(F32) + wzr[1].astype(F32) + wzr[2].astype(F32)
    for c in pending:
        c.wait_send()
    for d in (1, 2, 3):
        copy("wz", d - 1, wzs.at[d - 1], wzr.at[d - 1], dev(core=1 - core)).wait_send()


def hand_over(*refs):
    for k in range(4):
        refs[4 + k][...] = refs[k][...]


def body(attn_out, residual, o_weight, norm_gain, positive):
    vmem = pl.BlockSpec(memory_space=pltpu.VMEM)
    shape = jax.ShapeDtypeStruct
    scratch = [
        ((4, 3, 128, 512), WIRE), ((4, 3, 128, 512), WIRE), ((4, 128, 512), F32),
        ((2, 128, 512), WIRE), ((2, 128, 512), WIRE), ((256, 512), F32), ((256, 128), F32),
        ((2, 8, 8, 128), F32),
        ((512, 512), BF16), ((1024, 512), BF16), ((4, 8, 128), jnp.int32), ((512, 128), F32),
        ((4, 512, 256), F32), ((4, 6, 64, 256), F32), ((4, 64, 256), F32), ((4, 64, 256), F32),
        ((2, 512, 128), F32), ((4, 128, 1), F32), ((4, 8, 128), F32), ((8, 8, 128), F32),
        ((4, 512, 256), BF16), ((4, 512, 256), BF16),
        ((4, 256, 512), F32), ((4, 128, 512), F32), ((4, 128, 512), GZ_WIRE),
        ((3, 128, 512), GZ_WIRE), ((4, 128, 512), F32), ((3, 128, 512), F32), ((256, 512), F32),
        ((2, 8, 8, 128), F32),
        ((8, 2, 256, 256), BF16), ((4, 1024, 256), BF16), ((1024, 512), BF16),
        ((4, 2, 512, 128), F32), ((4, 512, 128), F32), ((3, 512, 128), WZ_WIRE),
        ((3, 512, 128), WZ_WIRE),
    ]
    outs = (
        shape((1, 128), F32), shape((256, 512), F32), shape((256, 512), F32),
        shape((512, 128), F32),
    )
    made = pl.pallas_call(
        kernel,
        name="step",
        out_shape=outs,
        in_specs=[vmem] * 5,
        out_specs=[vmem] * 4,
        scratch_shapes=[pltpu.VMEM(s, t) for s, t in scratch]
        + [pltpu.SemaphoreType.DMA((COUNT,)), pltpu.SemaphoreType.DMA((COUNT,))],
        compiler_params=pltpu.CompilerParams(
            collective_id=0, has_side_effects=True, vmem_limit_bytes=56 * 1024 * 1024
        ),
    )(
        attn_out.reshape(256, 512), residual.reshape(256, 512), o_weight,
        norm_gain.reshape(1, 512), positive.reshape(1, 128),
    )
    loss, rg, ag, wg = pl.pallas_call(
        hand_over,
        name="hand_over",
        out_shape=outs,
        in_specs=[vmem] * 4,
        out_specs=[vmem] * 4,
    )(*made)
    return (
        loss.reshape(128), rg.reshape(2, 128, 512), ag.reshape(2, 128, 512), wg,
    )


def solution(mesh):
    placed = (P(None, "dp", "mp"), P(None, "dp", "mp"), P("mp", None), P("mp"), P("dp"))
    return jax.shard_map(
        body,
        mesh=mesh,
        in_specs=placed,
        out_specs=(P("dp"), P(None, "dp", "mp"), P(None, "dp", "mp"), P("mp", "dp")),
        check_vma=False,
    )
```

```python
import jax
import jax.numpy as jnp
from jax import lax
from jax.sharding import PartitionSpec as P
from jax.experimental import pallas as pl
from jax.experimental.pallas import tpu as pltpu

LOGIT_SCALE = 50.0
EPS = 1e-06
F32 = jnp.float32
BF16 = jnp.bfloat16
MESH = pl.DeviceIdType.MESH
WIRE = BF16
GZ_WIRE = BF16
WZ_WIRE = BF16

STAGES = dict(
    y1=24, z1=2, ss=14, qx=3, ps=3, ax=3, az=3, ac=4, ly=48, lz=4, tx=3, td=7,
    ez=4, ey=24, gc=4, gz=3, gq=3, rr=14, gh=4, gy=24, gx=32, wc=4, wz=3,
)
BASE = {}
COUNT = 0
for _name, _n in STAGES.items():
    BASE[_name] = COUNT
    COUNT += _n


def nt(a, b):
    return lax.dot_general(a, b, (((1,), (1,)), ((), ())), preferred_element_type=F32)


def tn(a, b):
    return lax.dot_general(a, b, (((0,), (0,)), ((), ())), preferred_element_type=F32)


def nn(a, b):
    return lax.dot_general(a, b, (((1,), (0,)), ((), ())), preferred_element_type=F32)


def to_row(col):
    n = col.shape[0]
    return jnp.broadcast_to(col, (n, 128)).T[0:8]


def to_col(row):
    n = row.shape[1]
    return jnp.broadcast_to(row, (128, n)).T[:, 0:1]


def rows(start, size, unit=None):
    return pl.ds(pl.multiple_of(start, unit or size), size)


def kernel(
    a_ref, r_ref, w_ref, gain_ref, pos_ref,
    loss_ref, rg_ref, ag_ref, wg_ref,
    ys, yf, yt, yr, own, zs, zr, sc, inv_s, ssb,
    qx, aa, px, pc, lg, lt, lr, lzs, lzr, pos_s, sums_s, txb, td,
    ea, sa, gap, gcr, gzs, gzr, gqs, gqr, ge, rb,
    gg, gx, ax, tb, tcr, wzs, wzr,
    send, recv,
):
    dp = lax.axis_index("dp")
    mp = lax.axis_index("mp")
    core, x, zl = dp % 2, (dp // 2) % 4, dp // 8
    y, zh = mp // 2, mp % 2
    j = mp
    pending = []

    def dev(core=core, x=x, zl=zl, y=y, zh=zh):
        return ((zl * 4 + x) * 2 + core, y * 2 + zh)

    def copy(stage, k, src, dst, to, r=None):
        return pltpu.make_async_remote_copy(
            src_ref=src, dst_ref=dst,
            send_sem=send.at[BASE[stage] + k],
            recv_sem=recv.at[BASE[stage] + (k if r is None else r)],
            device_id=to, device_id_type=MESH,
        )

    def go(*args):
        c = copy(*args)
        c.start()
        pending.append(c)

    def got(stage, k, dst):
        copy(stage, k, dst, dst, dev(core=1 - core)).wait_recv()

    def ring(v, d):
        return (v + d) % 4

    others = [(d, e) for d in (2, 1, 3, 0) for e in (1, 0) if (d, e) != (0, 0)]

    barrier = pltpu.get_barrier_semaphore()
    peers = [dev(y=ring(y, d), zh=(zh + e) % 2) for d, e in others]
    peers += [dev(x=ring(x, d)) for d in (1, 2, 3)]
    peers += [dev(zl=ring(zl, d)) for d in (1, 2, 3)]
    peers += [dev(core=1 - core)]
    for p in peers:
        pl.semaphore_signal(barrier, inc=1, device_id=p, device_id_type=MESH)

    def half(h):
        return pl.ds(h * 128, 128)

    def product(h, yy, er):
        e = (1 - zh) if er == 0 else zh
        return nn(a_ref[half(h), :], w_ref[:, rows(yy * 1024 + e * 512, 512)])

    low, high = pl.ds(0, 64), pl.ds(64, 64)
    right, left = dev(y=ring(y, 1)), dev(y=ring(y, 3))

    def y_products(h):
        for er in (0, 1):
            c = h * 2 + er
            ys[c, 0] = product(h, ring(y, 2), er).astype(WIRE)
            near = product(h, ring(y, 1), er)
            yf[c, 0] = near[0:64]
            ys[c, 1, high, :] = near[64:128].astype(WIRE)
            near = product(h, ring(y, 3), er)
            yf[c, 1] = near[64:128]
            ys[c, 1, low, :] = near[0:64].astype(WIRE)

    def y_send(c):
        go("y1", c * 6 + 0, ys.at[c, 0, low], yt.at[c, 0], right)
        go("y1", c * 6 + 1, ys.at[c, 0, high], yt.at[c, 1], left)
        go("y1", c * 6 + 2, ys.at[c, 1, high], yr.at[c, 0, high], right)
        go("y1", c * 6 + 3, ys.at[c, 1, low], yr.at[c, 1, low], left)

    def y_hop(c):
        got("y1", c * 6 + 0, yt.at[c, 0])
        ys[c, 2, low, :] = (yf[c, 0] + yt[c, 0].astype(F32)).astype(WIRE)
        go("y1", c * 6 + 4, ys.at[c, 2, low], yr.at[c, 0, low], right)
        got("y1", c * 6 + 1, yt.at[c, 1])
        ys[c, 2, high, :] = (yf[c, 1] + yt[c, 1].astype(F32)).astype(WIRE)
        go("y1", c * 6 + 5, ys.at[c, 2, high], yr.at[c, 1, high], left)

    def y_sum(c):
        got("y1", c * 6 + 2, yr.at[c, 0, high])
        got("y1", c * 6 + 3, yr.at[c, 1, low])
        got("y1", c * 6 + 4, yr.at[c, 0, low])
        got("y1", c * 6 + 5, yr.at[c, 1, high])
        return own[c] + yr[c, 0].astype(F32) + yr[c, 1].astype(F32)

    def z_send(h):
        zs[h] = y_sum(h * 2).astype(WIRE)
        go("z1", h, zs.at[h], zr.at[h], dev(zh=1 - zh))

    def squares(h):
        got("z1", h, zr.at[h])
        proj = own[h * 2 + 1] + zr[h].astype(F32)
        scaled = (r_ref[half(h), :].astype(F32) + proj) * gain_ref[...]
        sc[half(h), :] = scaled
        ssb[h, 0] = to_row(jnp.sum(scaled * scaled, axis=1, keepdims=True))
        for d, e in others:
            k = d * 2 + e
            go("ss", h * 7 + k - 1, ssb.at[h, 0], ssb.at[h, k], dev(y=ring(y, d), zh=(zh + e) % 2))

    def embed(h):
        for d, e in others[::-1]:
            k = d * 2 + e
            got("ss", h * 7 + k - 1, ssb.at[h, k])
        total = ssb[h, 0]
        for k in range(1, 8):
            total = total + ssb[h, k]
        inv = to_col(lax.rsqrt(total[0:1] + EPS))
        inv_s[half(h), :] = jnp.broadcast_to(inv, (128, 128))
        return (sc[half(h), :] * inv).astype(BF16)

    y_products(0)
    y_products(1)
    px[x] = jnp.broadcast_to(pos_ref[...], (8, 128))
    pl.semaphore_wait(barrier, len(peers))
    y_send(0)
    y_send(2)
    for d in (2, 1, 3):
        go("ps", d - 1, px.at[x], px.at[x], dev(x=ring(x, d)))
        go("ax", d - 1, a_ref, ax.at[rows(x * 256, 256)], dev(x=ring(x, d)))
    for h in (0, 1):
        for er in (0, 1):
            own[h * 2 + er] = product(h, y, er)
    y_hop(0)
    y_send(1)
    y_hop(2)
    y_send(3)
    ax[rows(x * 256, 256), :] = a_ref[...]

    z_send(0)
    y_hop(1)
    z_send(1)
    y_hop(3)
    own[1] = y_sum(1)
    squares(0)
    own[3] = y_sum(3)
    squares(1)
    emb = embed(0)
    q_at = rows(x * 128, 128)
    qx[q_at, :] = emb
    for d in (2, 1, 3):
        go("qx", d - 1, qx.at[q_at], qx.at[q_at], dev(x=ring(x, d)))
    emb = embed(1)
    a_at = rows((zl * 2 + core) * 128, 128)
    aa[a_at, :] = emb
    go("ac", 0, aa.at[a_at], aa.at[a_at], dev(core=1 - core))
    for d in (2, 1, 3):
        go("az", d - 1, aa.at[a_at], aa.at[a_at], dev(zl=ring(zl, d)))
    for d in (1, 3, 2):
        got("ps", d - 1, px.at[ring(x, -d)])
    for xx in range(4):
        pc[pl.ds(xx * 128, 128), :] = jnp.broadcast_to(
            to_col(px[xx].astype(F32)[0:1]), (128, 128)
        )
    for d in (1, 3, 2):
        got("qx", d - 1, qx.at[rows(ring(x, -d) * 128, 128)])

    def block(yy, e):
        return rows((yy * 2 + e) * 64, 64)

    mine, pair = block(y, zh), block(y, 1 - zh)

    def logit_send(t):
        zz = ring(zl, -t)
        if t:
            at = rows((zz * 2 + core) * 128, 128)
            got("az", t - 1, aa.at[at])
            go("ac", t, aa.at[at], aa.at[at], dev(core=1 - core))
        got("ac", t, aa.at[rows((zz * 2 + 1 - core) * 128, 128)])
        lg[t] = nt(qx[...], aa[rows(zz * 256, 256), :])
        for er in (0, 1):
            k = t * 12 + er * 6
            far, after, before = (logit_piece(t, er, d) for d in (2, 1, 3))
            go("ly", k + 0, far.at[top], lt.at[t, er, 0], right)
            go("ly", k + 1, far.at[end], lt.at[t, er, 1], left)
            go("ly", k + 2, after.at[end], lr.at[t, er, 0, end], right)
            go("ly", k + 3, before.at[top], lr.at[t, er, 1, top], left)

    top, end = pl.ds(0, 32), pl.ds(32, 32)

    def logit_piece(t, er, d):
        return lg.at[t, block(ring(y, d), (1 - zh) if er == 0 else zh)]

    def logit_hop(t):
        for er in (0, 1):
            k = t * 12 + er * 6
            after, before = (logit_piece(t, er, d) for d in (1, 3))
            got("ly", k + 0, lt.at[t, er, 0])
            after[top, :] = after[top, :] + lt[t, er, 0]
            go("ly", k + 4, after.at[top], lr.at[t, er, 0, top], right)
            got("ly", k + 1, lt.at[t, er, 1])
            before[end, :] = before[end, :] + lt[t, er, 1]
            go("ly", k + 5, before.at[end], lr.at[t, er, 1, end], left)

    def logit_sum(t, er):
        k = t * 12 + er * 6
        got("ly", k + 2, lr.at[t, er, 0, end])
        got("ly", k + 3, lr.at[t, er, 1, top])
        got("ly", k + 4, lr.at[t, er, 0, top])
        got("ly", k + 5, lr.at[t, er, 1, end])
        return lg[t, pair if er == 0 else mine, :] + lr[t, er, 0] + lr[t, er, 1]

    def logit_pass(t):
        lzs[t] = logit_sum(t, 0)
        go("lz", t, lzs.at[t], lzr.at[t], dev(zh=1 - zh))

    lanes = lax.broadcasted_iota(jnp.int32, (128, 128), 1).astype(F32)

    def hits(t, at, c):
        first = (ring(zl, -t) * 1024 + x * 256 + c * 128).astype(F32)
        mark = pc[at, :] - first
        return lanes[0:mark.shape[0]] == mark

    def logit_done(t):
        part = logit_sum(t, 1)
        got("lz", t, lzr.at[t])
        logits = LOGIT_SCALE * (part + lzr[t])
        ex = jnp.exp(logits)
        ea[t, mine, :] = ex.astype(BF16)
        go("ez", t, ea.at[t, mine], ea.at[t, mine], dev(zh=1 - zh))
        exp_send(t, zh)
        hit = jnp.concatenate([hits(t, mine, 0), hits(t, mine, 1)], axis=1)
        sums_s[t] = jnp.concatenate(
            [
                jnp.sum(ex, axis=1, keepdims=True),
                jnp.sum(jnp.where(hit, logits, 0.0), axis=1, keepdims=True),
            ],
            axis=0,
        )

    def exp_send(t, e):
        part = ea.at[t, block(y, e)]
        go("ey", t * 6 + e, part, part, right)
        go("ey", t * 6 + 2 + e, part, part, left)
        go("ey", t * 6 + 4 + e, part, part, dev(y=ring(y, 2)))

    def exp_pass(t):
        got("ez", t, ea.at[t, pair])
        exp_send(t, 1 - zh)

    logit_send(0)
    logit_send(1)
    logit_hop(0)
    logit_send(3)
    logit_hop(1)
    logit_send(2)
    logit_pass(0)
    logit_hop(3)
    logit_pass(1)
    logit_hop(2)
    logit_done(0)
    logit_pass(3)
    logit_done(1)
    exp_pass(0)
    logit_pass(2)
    logit_done(3)
    exp_pass(1)
    logit_done(2)

    txb[0] = to_row(sums_s[0] + sums_s[1] + sums_s[2] + sums_s[3])
    for d in (2, 1, 3):
        go("tx", d - 1, txb.at[0], txb.at[d], dev(x=ring(x, d)))
    exp_pass(3)
    for d in (1, 3, 2):
        got("tx", d - 1, txb.at[d])
    td[j] = txb[0] + txb[1] + txb[2] + txb[3]
    for d, e in others:
        go("td", d * 2 + e - 1, td.at[j], td.at[j], dev(y=ring(y, d), zh=(zh + e) % 2))
    exp_pass(2)

    for d, e in others[::-1]:
        got("td", d * 2 + e - 1, td.at[ring(y, -d) * 2 + (zh + e) % 2])
    for xx in range(4):
        first, second = td[xx * 2][0:1], td[xx * 2 + 1][0:1]
        total = jnp.concatenate([first[:, 0:64], second[:, 0:64]], axis=1)
        top = jnp.concatenate([first[:, 64:128], second[:, 64:128]], axis=1)
        scale = LOGIT_SCALE / total
        at = pl.ds(xx * 128, 128)
        pos_s[0, at, :] = jnp.broadcast_to(to_col(scale), (128, 128))
        pos_s[1, at, :] = jnp.broadcast_to(
            to_col(jnp.exp(top) * scale - LOGIT_SCALE), (128, 128)
        )

    def score(t):
        for e in (0, 1):
            got("ey", t * 6 + e, ea.at[t, block(ring(y, 3), e)])
            got("ey", t * 6 + 2 + e, ea.at[t, block(ring(y, 1), e)])
            got("ey", t * 6 + 4 + e, ea.at[t, block(ring(y, 2), e)])
        for xx in range(4):
            at = pl.ds(xx * 128, 128)
            for c in (0, 1):
                part = pl.ds(c * 128, 128)
                rest = ea[t, at, part].astype(F32) * pos_s[0, at, :]
                sa[t, at, part] = jnp.where(
                    hits(t, at, c), pos_s[1, at, :], rest
                ).astype(BF16)

    def answers_part(t):
        gap[t] = tn(sa[t], qx[...])
        away = rows((1 - core) * 128, 128)
        go("gc", t, gap.at[t, away], gcr.at[t], dev(core=1 - core))

    def answers_sum(t):
        got("gc", t, gcr.at[t])
        both = gap[t, rows(core * 128, 128), :] + gcr[t]
        if t:
            gzs[t] = both.astype(GZ_WIRE)
            go("gz", t - 1, gzs.at[t], gzr.at[t - 1], dev(zl=ring(zl, -t)))
        else:
            ge[half(1), :] = both

    def queries_part(d):
        part = jnp.zeros((128, 512), F32)
        for t in range(4):
            left = sa[t, rows(ring(x, d) * 128, 128), :]
            part = part + nn(left, aa[rows(ring(zl, -t) * 256, 256), :])
        gqs[d] = part
        if d:
            go("gq", d - 1, gqs.at[d], gqr.at[d - 1], dev(x=ring(x, d)))

    score(2)
    answers_part(2)
    score(3)
    answers_part(3)
    answers_sum(2)
    score(1)
    answers_part(1)
    answers_sum(3)
    score(0)
    queries_part(2)
    answers_sum(1)
    queries_part(1)
    queries_part(3)
    answers_part(0)
    queries_part(0)
    answers_sum(0)

    def radial(h, g):
        at = half(h)
        ge[at, :] = g
        rb[h, 0] = to_row(jnp.sum(g * sc[at, :], axis=1, keepdims=True))
        for d, e in others:
            k = d * 2 + e
            go("rr", h * 7 + k - 1, rb.at[h, 0], rb.at[h, k], dev(y=ring(y, d), zh=(zh + e) % 2))

    def spread(h):
        at = half(h)
        tot = rb[h, 0]
        for d, e in others[::-1]:
            k = d * 2 + e
            got("rr", h * 7 + k - 1, rb.at[h, k])
        for k in range(1, 8):
            tot = tot + rb[h, k]
        rad = to_col(tot[0:1])
        iv = inv_s[at, 0:1]
        out = gain_ref[...] * (iv * ge[at, :] - (iv * iv * iv * rad) * sc[at, :])
        rg_ref[at, :] = out
        for c in (0, 1):
            gg[j, c, at, :] = out[:, c * 256:(c + 1) * 256].astype(BF16)
        for c in (0, 1):
            part = gg.at[j, c, at]
            go("gh", h * 2 + c, part, part, dev(zh=1 - zh))
        near(h, 0)

    def near(h, k):
        e = zh if k == 0 else 1 - zh
        for c in (0, 1):
            part = gg.at[y * 2 + e, c, half(h)]
            if k:
                got("gh", h * 2 + c, part)
            go("gy", h * 12 + k * 6 + c, part, part, right)
            go("gy", h * 12 + k * 6 + 2 + c, part, part, left)

    def hop(h, k):
        e = zh if k == 0 else 1 - zh
        part = gg.at[ring(y, 3) * 2 + e, 0, half(h)]
        got("gy", h * 12 + k * 6, part)
        go("gy", h * 12 + k * 6 + 4, part, part, right)
        part = gg.at[ring(y, 1) * 2 + e, 1, half(h)]
        got("gy", h * 12 + k * 6 + 3, part)
        go("gy", h * 12 + k * 6 + 5, part, part, left)

    def column_copy(h, t, k, c):
        e = zh if k == 0 else 1 - zh
        xx = e * 2 + c
        d = (xx - x + 4) % 4
        src = gg.at[ring(y, -t) * 2 + e, c, half(h)]
        dst = gx.at[t, rows(x * 256 + h * 128, 128)]
        n = t * 2 + h
        return d, src, dst, copy("gx", (n * 2 + k) * 2 + c, src, dst, dev(x=xx), n * 3 + d - 1)

    def columns(h, t, k):
        for n, c in {0: (), 1: ((1, 1),), 3: ((2, 0),), 2: ((4, 0), (5, 1))}[t]:
            e = zh if k == 0 else 1 - zh
            got("gy", h * 12 + k * 6 + n, gg.at[ring(y, -t) * 2 + e, c, half(h)])
        for c in (0, 1):
            d, src, dst, remote = column_copy(h, t, k, c)

            @pl.when(d > 0)
            def _():
                remote.start()

            @pl.when(d == 0)
            def _():
                dst[...] = src[...]

    for d in (1, 3, 2):
        got("gq", d - 1, gqr.at[d - 1])
    radial(0, gqs[0] + gqr[0] + gqr[1] + gqr[2])
    for d in (1, 3, 2):
        got("gz", d - 1, gzr.at[d - 1])
    radial(1, ge[half(1), :] + gzr[0].astype(F32) + gzr[1].astype(F32) + gzr[2].astype(F32))
    spread(0)
    columns(0, 0, 0)
    spread(1)
    columns(1, 0, 0)
    hop(0, 0)
    columns(0, 1, 0)
    columns(0, 3, 0)
    hop(1, 0)
    columns(1, 1, 0)
    columns(1, 3, 0)
    near(0, 1)
    columns(0, 0, 1)
    columns(0, 2, 0)
    hop(0, 1)
    columns(0, 1, 1)
    columns(0, 3, 1)
    columns(1, 2, 0)
    near(1, 1)
    columns(1, 0, 1)
    columns(0, 2, 1)
    hop(1, 1)

    for d in (1, 3, 2):
        got("ax", d - 1, ax.at[rows(ring(x, -d) * 256, 256)])

    def weight_part(t):
        for h in (0, 1):
            for d in (1, 3, 2):
                got("gx", (t * 2 + h) * 3 + d - 1,
                    gx.at[t, rows(ring(x, -d) * 256 + h * 128, 128)])
        part = tn(ax[...], gx[t])
        tb[t, 0] = part[:, 0:128]
        tb[t, 1] = part[:, 128:256]
        go("wc", t, tb.at[t, 1 - core], tcr.at[t], dev(core=1 - core))

    def weight_sum(t):
        got("wc", t, tcr.at[t])
        zz = ring(y, -t)
        d = (zz - zl + 4) % 4
        both = tb[t, core] + tcr[t]

        @pl.when(d > 0)
        def _():
            wzs[d - 1] = both.astype(WZ_WIRE)
            copy("wz", d - 1, wzs.at[d - 1], wzr.at[d - 1], dev(zl=zz)).start()

        @pl.when(d == 0)
        def _():
            wg_ref[...] = both

    columns(1, 1, 1)
    columns(1, 3, 1)
    weight_part(0)
    columns(1, 2, 1)
    weight_sum(0)
    weight_part(1)
    weight_part(3)
    weight_sum(1)
    weight_sum(3)

    ag_ref[...] = jnp.zeros((256, 512), F32)
    for jj in range(8):
        for c in (0, 1):
            ag_ref[...] += nt(gg[jj, c], w_ref[:, pl.ds(jj * 512 + c * 256, 256)])
    weight_part(2)
    weight_sum(2)
    losses = [
        jnp.log(v[:, 0:64]) - v[:, 64:128] for v in (td[x * 2][0:1], td[x * 2 + 1][0:1])
    ]
    loss_ref[...] = jnp.concatenate(losses, axis=1)
    for d in (1, 3, 2):
        got("wz", d - 1, wzr.at[d - 1])
    wg_ref[...] += wzr[0].astype(F32) + wzr[1].astype(F32) + wzr[2].astype(F32)
    for c in pending:
        c.wait_send()
    for d in (1, 2, 3):
        copy("wz", d - 1, wzs.at[d - 1], wzr.at[d - 1], dev(core=1 - core)).wait_send()
    for n in range(32):
        d, _, _, remote = column_copy(n // 16, n // 4 % 4, n // 2 % 2, n % 2)

        @pl.when(d > 0)
        def _():
            remote.wait_send()


def hand_over(*refs):
    for k in range(4):
        refs[4 + k][...] = refs[k][...]


def body(attn_out, residual, o_weight, norm_gain, positive):
    vmem = pl.BlockSpec(memory_space=pltpu.VMEM)
    shape = jax.ShapeDtypeStruct
    scratch = [
        ((4, 3, 128, 512), WIRE), ((4, 2, 64, 512), F32), ((4, 2, 64, 512), WIRE),
        ((4, 2, 128, 512), WIRE), ((4, 128, 512), F32),
        ((2, 128, 512), WIRE), ((2, 128, 512), WIRE), ((256, 512), F32), ((256, 128), F32),
        ((2, 8, 8, 128), F32),
        ((512, 512), BF16), ((1024, 512), BF16), ((4, 8, 128), jnp.int32), ((512, 128), F32),
        ((4, 512, 256), F32), ((4, 2, 2, 32, 256), F32), ((4, 2, 2, 64, 256), F32), ((4, 64, 256), F32), ((4, 64, 256), F32),
        ((2, 512, 128), F32), ((4, 128, 1), F32), ((4, 8, 128), F32), ((8, 8, 128), F32),
        ((4, 512, 256), BF16), ((4, 512, 256), BF16),
        ((4, 256, 512), F32), ((4, 128, 512), F32), ((4, 128, 512), GZ_WIRE),
        ((3, 128, 512), GZ_WIRE), ((4, 128, 512), F32), ((3, 128, 512), F32), ((256, 512), F32),
        ((2, 8, 8, 128), F32),
        ((8, 2, 256, 256), BF16), ((4, 1024, 256), BF16), ((1024, 512), BF16),
        ((4, 2, 512, 128), F32), ((4, 512, 128), F32), ((3, 512, 128), WZ_WIRE),
        ((3, 512, 128), WZ_WIRE),
    ]
    outs = (
        shape((1, 128), F32), shape((256, 512), F32), shape((256, 512), F32),
        shape((512, 128), F32),
    )
    made = pl.pallas_call(
        kernel,
        name="step",
        out_shape=outs,
        in_specs=[vmem] * 5,
        out_specs=[vmem] * 4,
        scratch_shapes=[pltpu.VMEM(s, t) for s, t in scratch]
        + [pltpu.SemaphoreType.DMA((COUNT,)), pltpu.SemaphoreType.DMA((COUNT,))],
        compiler_params=pltpu.CompilerParams(
            collective_id=0, has_side_effects=True, vmem_limit_bytes=40 * 1024 * 1024
        ),
    )(
        attn_out.reshape(256, 512), residual.reshape(256, 512), o_weight,
        norm_gain.reshape(1, 512), positive.reshape(1, 128),
    )
    loss, rg, ag, wg = pl.pallas_call(
        hand_over,
        name="hand_over",
        out_shape=outs,
        in_specs=[vmem] * 4,
        out_specs=[vmem] * 4,
    )(*made)
    return (
        loss.reshape(128), rg.reshape(2, 128, 512), ag.reshape(2, 128, 512), wg,
    )


def solution(mesh):
    placed = (P(None, "dp", "mp"), P(None, "dp", "mp"), P("mp", None), P("mp"), P("dp"))
    return jax.shard_map(
        body,
        mesh=mesh,
        in_specs=placed,
        out_specs=(P("dp"), P(None, "dp", "mp"), P(None, "dp", "mp"), P("mp", "dp")),
        check_vma=False,
    )
```

```python
import jax
import jax.numpy as jnp
from jax import lax
from jax.sharding import PartitionSpec as P
from jax.experimental import pallas as pl
from jax.experimental.pallas import tpu as pltpu

LOGIT_SCALE = 50.0
EPS = 1e-06
F32 = jnp.float32
BF16 = jnp.bfloat16
MESH = pl.DeviceIdType.MESH
WIRE = BF16
GZ_WIRE = BF16
WZ_WIRE = BF16

STAGES = dict(
    y1=24, z1=2, ss=14, qx=3, ps=3, ax=3, az=3, ac=4, ly=48, lz=4, tx=3, td=7,
    ez=4, ey=24, gc=4, gz=3, gq=3, rr=14, gh=4, gy=24, gx=32, wc=4, wz=3,
)
BASE = {}
COUNT = 0
for _name, _n in STAGES.items():
    BASE[_name] = COUNT
    COUNT += _n


def nt(a, b):
    return lax.dot_general(a, b, (((1,), (1,)), ((), ())), preferred_element_type=F32)


def tn(a, b):
    return lax.dot_general(a, b, (((0,), (0,)), ((), ())), preferred_element_type=F32)


def nn(a, b):
    return lax.dot_general(a, b, (((1,), (0,)), ((), ())), preferred_element_type=F32)


def to_row(col):
    n = col.shape[0]
    return jnp.broadcast_to(col, (n, 128)).T[0:8]


def to_col(row):
    n = row.shape[1]
    return jnp.broadcast_to(row, (128, n)).T[:, 0:1]


def rows(start, size, unit=None):
    return pl.ds(pl.multiple_of(start, unit or size), size)


def kernel(
    a_in, r_in, w_in, gain_in, pos_in,
    loss_ref, rg_ref, ag_ref, wg_ref,
    a_ref, r_ref, w_ref, gain_ref, pos_ref,
    ys, yf, yt, yr, own, zs, zr, sc, inv_s, ssb,
    qx, aa, px, pc, lg, lt, lr, lzs, lzr, pos_s, sums_s, txb, td,
    ea, sa, gap, gcr, gzs, gzr, gqs, gqr, ge, rb,
    gg, gx, ax, tb, tcr, wzs, wzr,
    send, recv, load,
):
    dp = lax.axis_index("dp")
    mp = lax.axis_index("mp")
    core, x, zl = dp % 2, (dp // 2) % 4, dp // 8
    y, zh = mp // 2, mp % 2
    j = mp
    pending = []

    def dev(core=core, x=x, zl=zl, y=y, zh=zh):
        return ((zl * 4 + x) * 2 + core, y * 2 + zh)

    def copy(stage, k, src, dst, to, r=None):
        return pltpu.make_async_remote_copy(
            src_ref=src, dst_ref=dst,
            send_sem=send.at[BASE[stage] + k],
            recv_sem=recv.at[BASE[stage] + (k if r is None else r)],
            device_id=to, device_id_type=MESH,
        )

    def go(*args):
        c = copy(*args)
        c.start()
        pending.append(c)

    def settle(upto):
        while len(settled) < min(upto, len(pending)):
            c = pending[len(settled)]
            c.wait_send()
            settled.append(c)

    settled = []

    def got(stage, k, dst):
        copy(stage, k, dst, dst, dev(core=1 - core)).wait_recv()

    def ring(v, d):
        return (v + d) % 4

    others = [(d, e) for d in (2, 1, 3, 0) for e in (1, 0) if (d, e) != (0, 0)]

    barrier = pltpu.get_barrier_semaphore()
    peers = [dev(y=ring(y, d), zh=(zh + e) % 2) for d, e in others]
    peers += [dev(x=ring(x, d)) for d in (1, 2, 3)]
    peers += [dev(zl=ring(zl, d)) for d in (1, 2, 3)]
    peers += [dev(core=1 - core)]
    for p in peers:
        pl.semaphore_signal(barrier, inc=1, device_id=p, device_id_type=MESH)

    loads = [pltpu.make_async_copy(a_in, a_ref, load.at[0])]
    for k in range(4):
        part = pl.ds(k * 128, 128)
        loads.append(pltpu.make_async_copy(w_in.at[part], w_ref.at[part], load.at[1 + k]))
    loads.append(pltpu.make_async_copy(pos_in, pos_ref, load.at[5]))
    loads.append(pltpu.make_async_copy(gain_in, gain_ref, load.at[6]))
    loads.append(pltpu.make_async_copy(r_in, r_ref, load.at[7]))
    for c in loads:
        c.start()
    for c in loads[:6]:
        c.wait()

    def half(h):
        return pl.ds(h * 128, 128)

    def product(h, yy, er):
        e = (1 - zh) if er == 0 else zh
        return nn(a_ref[half(h), :], w_ref[:, rows(yy * 1024 + e * 512, 512)])

    low, high = pl.ds(0, 64), pl.ds(64, 64)
    right, left = dev(y=ring(y, 1)), dev(y=ring(y, 3))

    def y_products(h):
        for er in (0, 1):
            c = h * 2 + er
            ys[c, 0] = product(h, ring(y, 2), er).astype(WIRE)
            near = product(h, ring(y, 1), er)
            yf[c, 0] = near[0:64]
            ys[c, 1, high, :] = near[64:128].astype(WIRE)
            near = product(h, ring(y, 3), er)
            yf[c, 1] = near[64:128]
            ys[c, 1, low, :] = near[0:64].astype(WIRE)

    def y_send(c):
        go("y1", c * 6 + 0, ys.at[c, 0, low], yt.at[c, 0], right)
        go("y1", c * 6 + 1, ys.at[c, 0, high], yt.at[c, 1], left)
        go("y1", c * 6 + 2, ys.at[c, 1, high], yr.at[c, 0, high], right)
        go("y1", c * 6 + 3, ys.at[c, 1, low], yr.at[c, 1, low], left)

    def y_hop(c):
        got("y1", c * 6 + 0, yt.at[c, 0])
        ys[c, 2, low, :] = (yf[c, 0] + yt[c, 0].astype(F32)).astype(WIRE)
        go("y1", c * 6 + 4, ys.at[c, 2, low], yr.at[c, 0, low], right)
        got("y1", c * 6 + 1, yt.at[c, 1])
        ys[c, 2, high, :] = (yf[c, 1] + yt[c, 1].astype(F32)).astype(WIRE)
        go("y1", c * 6 + 5, ys.at[c, 2, high], yr.at[c, 1, high], left)

    def y_sum(c):
        got("y1", c * 6 + 2, yr.at[c, 0, high])
        got("y1", c * 6 + 3, yr.at[c, 1, low])
        got("y1", c * 6 + 4, yr.at[c, 0, low])
        got("y1", c * 6 + 5, yr.at[c, 1, high])
        return own[c] + yr[c, 0].astype(F32) + yr[c, 1].astype(F32)

    def z_send(h):
        zs[h] = y_sum(h * 2).astype(WIRE)
        go("z1", h, zs.at[h], zr.at[h], dev(zh=1 - zh))

    def squares(h):
        got("z1", h, zr.at[h])
        proj = own[h * 2 + 1] + zr[h].astype(F32)
        scaled = (r_ref[half(h), :].astype(F32) + proj) * gain_ref[...]
        sc[half(h), :] = scaled
        ssb[h, 0] = to_row(jnp.sum(scaled * scaled, axis=1, keepdims=True))
        for d, e in others:
            k = d * 2 + e
            go("ss", h * 7 + k - 1, ssb.at[h, 0], ssb.at[h, k], dev(y=ring(y, d), zh=(zh + e) % 2))

    def embed(h):
        for d, e in others[::-1]:
            k = d * 2 + e
            got("ss", h * 7 + k - 1, ssb.at[h, k])
        total = ssb[h, 0]
        for k in range(1, 8):
            total = total + ssb[h, k]
        inv = to_col(lax.rsqrt(total[0:1] + EPS))
        inv_s[half(h), :] = jnp.broadcast_to(inv, (128, 128))
        return (sc[half(h), :] * inv).astype(BF16)

    y_products(0)
    y_products(1)
    px[x] = jnp.broadcast_to(pos_ref[...], (8, 128))
    pl.semaphore_wait(barrier, len(peers))
    y_send(0)
    y_send(2)
    for d in (2, 1, 3):
        go("ps", d - 1, px.at[x], px.at[x], dev(x=ring(x, d)))
        go("ax", d - 1, a_ref, ax.at[rows(x * 256, 256)], dev(x=ring(x, d)))
    for h in (0, 1):
        for er in (0, 1):
            own[h * 2 + er] = product(h, y, er)
    y_hop(0)
    y_send(1)
    y_hop(2)
    y_send(3)
    ax[rows(x * 256, 256), :] = a_ref[...]

    for c in loads[6:]:
        c.wait()
    z_send(0)
    y_hop(1)
    z_send(1)
    y_hop(3)
    own[1] = y_sum(1)
    squares(0)
    own[3] = y_sum(3)
    squares(1)
    early = len(pending)
    settle(early - 14)
    emb = embed(0)
    q_at = rows(x * 128, 128)
    qx[q_at, :] = emb
    for d in (2, 1, 3):
        go("qx", d - 1, qx.at[q_at], qx.at[q_at], dev(x=ring(x, d)))
    emb = embed(1)
    a_at = rows((zl * 2 + core) * 128, 128)
    aa[a_at, :] = emb
    go("ac", 0, aa.at[a_at], aa.at[a_at], dev(core=1 - core))
    for d in (2, 1, 3):
        go("az", d - 1, aa.at[a_at], aa.at[a_at], dev(zl=ring(zl, d)))
    for d in (1, 3, 2):
        got("ps", d - 1, px.at[ring(x, -d)])
    for xx in range(4):
        pc[pl.ds(xx * 128, 128), :] = jnp.broadcast_to(
            to_col(px[xx].astype(F32)[0:1]), (128, 128)
        )
    for d in (1, 3, 2):
        got("qx", d - 1, qx.at[rows(ring(x, -d) * 128, 128)])

    def block(yy, e):
        return rows((yy * 2 + e) * 64, 64)

    mine, pair = block(y, zh), block(y, 1 - zh)

    def logit_send(t):
        zz = ring(zl, -t)
        if t:
            at = rows((zz * 2 + core) * 128, 128)
            got("az", t - 1, aa.at[at])
            go("ac", t, aa.at[at], aa.at[at], dev(core=1 - core))
        got("ac", t, aa.at[rows((zz * 2 + 1 - core) * 128, 128)])
        lg[t] = nt(qx[...], aa[rows(zz * 256, 256), :])
        for er in (0, 1):
            k = t * 12 + er * 6
            far, after, before = (logit_piece(t, er, d) for d in (2, 1, 3))
            go("ly", k + 0, far.at[top], lt.at[t, er, 0], right)
            go("ly", k + 1, far.at[end], lt.at[t, er, 1], left)
            go("ly", k + 2, after.at[end], lr.at[t, er, 0, end], right)
            go("ly", k + 3, before.at[top], lr.at[t, er, 1, top], left)

    top, end = pl.ds(0, 32), pl.ds(32, 32)

    def logit_piece(t, er, d):
        return lg.at[t, block(ring(y, d), (1 - zh) if er == 0 else zh)]

    def logit_hop(t):
        for er in (0, 1):
            k = t * 12 + er * 6
            after, before = (logit_piece(t, er, d) for d in (1, 3))
            got("ly", k + 0, lt.at[t, er, 0])
            after[top, :] = after[top, :] + lt[t, er, 0]
            go("ly", k + 4, after.at[top], lr.at[t, er, 0, top], right)
            got("ly", k + 1, lt.at[t, er, 1])
            before[end, :] = before[end, :] + lt[t, er, 1]
            go("ly", k + 5, before.at[end], lr.at[t, er, 1, end], left)

    def logit_sum(t, er):
        k = t * 12 + er * 6
        got("ly", k + 2, lr.at[t, er, 0, end])
        got("ly", k + 3, lr.at[t, er, 1, top])
        got("ly", k + 4, lr.at[t, er, 0, top])
        got("ly", k + 5, lr.at[t, er, 1, end])
        return lg[t, pair if er == 0 else mine, :] + lr[t, er, 0] + lr[t, er, 1]

    def logit_pass(t):
        lzs[t] = logit_sum(t, 0)
        go("lz", t, lzs.at[t], lzr.at[t], dev(zh=1 - zh))

    lanes = lax.broadcasted_iota(jnp.int32, (128, 128), 1).astype(F32)

    def hits(t, at, c):
        first = (ring(zl, -t) * 1024 + x * 256 + c * 128).astype(F32)
        mark = pc[at, :] - first
        return lanes[0:mark.shape[0]] == mark

    def logit_done(t):
        part = logit_sum(t, 1)
        got("lz", t, lzr.at[t])
        logits = LOGIT_SCALE * (part + lzr[t])
        ex = jnp.exp(logits)
        ea[t, mine, :] = ex.astype(BF16)
        go("ez", t, ea.at[t, mine], ea.at[t, mine], dev(zh=1 - zh))
        exp_send(t, zh)
        hit = jnp.concatenate([hits(t, mine, 0), hits(t, mine, 1)], axis=1)
        sums_s[t] = jnp.concatenate(
            [
                jnp.sum(ex, axis=1, keepdims=True),
                jnp.sum(jnp.where(hit, logits, 0.0), axis=1, keepdims=True),
            ],
            axis=0,
        )

    def exp_send(t, e):
        part = ea.at[t, block(y, e)]
        go("ey", t * 6 + e, part, part, right)
        go("ey", t * 6 + 2 + e, part, part, left)
        go("ey", t * 6 + 4 + e, part, part, dev(y=ring(y, 2)))

    def exp_pass(t):
        got("ez", t, ea.at[t, pair])
        exp_send(t, 1 - zh)

    logit_send(0)
    logit_send(1)
    logit_hop(0)
    logit_send(3)
    logit_hop(1)
    logit_send(2)
    logit_pass(0)
    logit_hop(3)
    logit_pass(1)
    logit_hop(2)
    settle(early)
    logit_done(0)
    logit_pass(3)
    logit_done(1)
    exp_pass(0)
    logit_pass(2)
    logit_done(3)
    exp_pass(1)
    early = len(pending) - 24
    settle(early)
    logit_done(2)

    txb[0] = to_row(sums_s[0] + sums_s[1] + sums_s[2] + sums_s[3])
    for d in (2, 1, 3):
        go("tx", d - 1, txb.at[0], txb.at[d], dev(x=ring(x, d)))
    exp_pass(3)
    for d in (1, 3, 2):
        got("tx", d - 1, txb.at[d])
    td[j] = txb[0] + txb[1] + txb[2] + txb[3]
    for d, e in others:
        go("td", d * 2 + e - 1, td.at[j], td.at[j], dev(y=ring(y, d), zh=(zh + e) % 2))
    exp_pass(2)

    settle(early + 12)

    for d, e in others[::-1]:
        got("td", d * 2 + e - 1, td.at[ring(y, -d) * 2 + (zh + e) % 2])
    for xx in range(4):
        first, second = td[xx * 2][0:1], td[xx * 2 + 1][0:1]
        total = jnp.concatenate([first[:, 0:64], second[:, 0:64]], axis=1)
        top = jnp.concatenate([first[:, 64:128], second[:, 64:128]], axis=1)
        scale = LOGIT_SCALE / total
        at = pl.ds(xx * 128, 128)
        pos_s[0, at, :] = jnp.broadcast_to(to_col(scale), (128, 128))
        pos_s[1, at, :] = jnp.broadcast_to(
            to_col(jnp.exp(top) * scale - LOGIT_SCALE), (128, 128)
        )

    def score(t):
        for e in (0, 1):
            got("ey", t * 6 + e, ea.at[t, block(ring(y, 3), e)])
            got("ey", t * 6 + 2 + e, ea.at[t, block(ring(y, 1), e)])
            got("ey", t * 6 + 4 + e, ea.at[t, block(ring(y, 2), e)])
        for xx in range(4):
            at = pl.ds(xx * 128, 128)
            for c in (0, 1):
                part = pl.ds(c * 128, 128)
                rest = ea[t, at, part].astype(F32) * pos_s[0, at, :]
                sa[t, at, part] = jnp.where(
                    hits(t, at, c), pos_s[1, at, :], rest
                ).astype(BF16)

    def answers_part(t):
        gap[t] = tn(sa[t], qx[...])
        away = rows((1 - core) * 128, 128)
        go("gc", t, gap.at[t, away], gcr.at[t], dev(core=1 - core))

    def answers_sum(t):
        got("gc", t, gcr.at[t])
        both = gap[t, rows(core * 128, 128), :] + gcr[t]
        if t:
            gzs[t] = both.astype(GZ_WIRE)
            go("gz", t - 1, gzs.at[t], gzr.at[t - 1], dev(zl=ring(zl, -t)))
        else:
            ge[half(1), :] = both

    def queries_part(d):
        part = jnp.zeros((128, 512), F32)
        for t in range(4):
            left = sa[t, rows(ring(x, d) * 128, 128), :]
            part = part + nn(left, aa[rows(ring(zl, -t) * 256, 256), :])
        gqs[d] = part
        if d:
            go("gq", d - 1, gqs.at[d], gqr.at[d - 1], dev(x=ring(x, d)))

    score(2)
    answers_part(2)
    score(3)
    answers_part(3)
    answers_sum(2)
    score(1)
    answers_part(1)
    answers_sum(3)
    score(0)
    queries_part(2)
    answers_sum(1)
    queries_part(1)
    queries_part(3)
    answers_part(0)
    queries_part(0)
    answers_sum(0)

    def radial(h, g):
        at = half(h)
        ge[at, :] = g
        rb[h, 0] = to_row(jnp.sum(g * sc[at, :], axis=1, keepdims=True))
        for d, e in others:
            k = d * 2 + e
            go("rr", h * 7 + k - 1, rb.at[h, 0], rb.at[h, k], dev(y=ring(y, d), zh=(zh + e) % 2))

    def spread(h):
        at = half(h)
        tot = rb[h, 0]
        for d, e in others[::-1]:
            k = d * 2 + e
            got("rr", h * 7 + k - 1, rb.at[h, k])
        for k in range(1, 8):
            tot = tot + rb[h, k]
        rad = to_col(tot[0:1])
        iv = inv_s[at, 0:1]
        out = gain_ref[...] * (iv * ge[at, :] - (iv * iv * iv * rad) * sc[at, :])
        rg_ref[at, :] = out
        for c in (0, 1):
            gg[j, c, at, :] = out[:, c * 256:(c + 1) * 256].astype(BF16)
        for c in (0, 1):
            part = gg.at[j, c, at]
            go("gh", h * 2 + c, part, part, dev(zh=1 - zh))
        near(h, 0)

    def near(h, k):
        e = zh if k == 0 else 1 - zh
        for c in (0, 1):
            part = gg.at[y * 2 + e, c, half(h)]
            if k:
                got("gh", h * 2 + c, part)
            go("gy", h * 12 + k * 6 + c, part, part, right)
            go("gy", h * 12 + k * 6 + 2 + c, part, part, left)

    def hop(h, k):
        e = zh if k == 0 else 1 - zh
        part = gg.at[ring(y, 3) * 2 + e, 0, half(h)]
        got("gy", h * 12 + k * 6, part)
        go("gy", h * 12 + k * 6 + 4, part, part, right)
        part = gg.at[ring(y, 1) * 2 + e, 1, half(h)]
        got("gy", h * 12 + k * 6 + 3, part)
        go("gy", h * 12 + k * 6 + 5, part, part, left)

    def column_copy(h, t, k, c):
        e = zh if k == 0 else 1 - zh
        xx = e * 2 + c
        d = (xx - x + 4) % 4
        src = gg.at[ring(y, -t) * 2 + e, c, half(h)]
        dst = gx.at[t, rows(x * 256 + h * 128, 128)]
        n = t * 2 + h
        return d, src, dst, copy("gx", (n * 2 + k) * 2 + c, src, dst, dev(x=xx), n * 3 + d - 1)

    def columns(h, t, k):
        for n, c in {0: (), 1: ((1, 1),), 3: ((2, 0),), 2: ((4, 0), (5, 1))}[t]:
            e = zh if k == 0 else 1 - zh
            got("gy", h * 12 + k * 6 + n, gg.at[ring(y, -t) * 2 + e, c, half(h)])
        for c in (0, 1):
            d, src, dst, remote = column_copy(h, t, k, c)

            @pl.when(d > 0)
            def _():
                remote.start()

            @pl.when(d == 0)
            def _():
                dst[...] = src[...]

    early = len(pending)
    settle(early - 10)
    for d in (1, 3, 2):
        got("gq", d - 1, gqr.at[d - 1])
    radial(0, gqs[0] + gqr[0] + gqr[1] + gqr[2])
    for d in (1, 3, 2):
        got("gz", d - 1, gzr.at[d - 1])
    radial(1, ge[half(1), :] + gzr[0].astype(F32) + gzr[1].astype(F32) + gzr[2].astype(F32))
    spread(0)
    columns(0, 0, 0)
    spread(1)
    columns(1, 0, 0)
    hop(0, 0)
    columns(0, 1, 0)
    columns(0, 3, 0)
    hop(1, 0)
    columns(1, 1, 0)
    columns(1, 3, 0)
    settle(early)
    near(0, 1)
    columns(0, 0, 1)
    columns(0, 2, 0)
    hop(0, 1)
    columns(0, 1, 1)
    columns(0, 3, 1)
    columns(1, 2, 0)
    near(1, 1)
    columns(1, 0, 1)
    columns(0, 2, 1)
    hop(1, 1)

    for d in (1, 3, 2):
        got("ax", d - 1, ax.at[rows(ring(x, -d) * 256, 256)])

    def weight_part(t):
        for h in (0, 1):
            for d in (1, 3, 2):
                got("gx", (t * 2 + h) * 3 + d - 1,
                    gx.at[t, rows(ring(x, -d) * 256 + h * 128, 128)])
        part = tn(ax[...], gx[t])
        tb[t, 0] = part[:, 0:128]
        tb[t, 1] = part[:, 128:256]
        go("wc", t, tb.at[t, 1 - core], tcr.at[t], dev(core=1 - core))

    def weight_sum(t):
        got("wc", t, tcr.at[t])
        zz = ring(y, -t)
        d = (zz - zl + 4) % 4
        both = tb[t, core] + tcr[t]

        @pl.when(d > 0)
        def _():
            wzs[d - 1] = both.astype(WZ_WIRE)
            copy("wz", d - 1, wzs.at[d - 1], wzr.at[d - 1], dev(zl=zz)).start()

        @pl.when(d == 0)
        def _():
            wg_ref[...] = both

    columns(1, 1, 1)
    columns(1, 3, 1)
    weight_part(0)
    columns(1, 2, 1)
    weight_sum(0)
    weight_part(1)
    weight_part(3)
    weight_sum(1)
    weight_sum(3)

    ag_ref[...] = jnp.zeros((256, 512), F32)
    for jj in range(8):
        for c in (0, 1):
            ag_ref[...] += nt(gg[jj, c], w_ref[:, pl.ds(jj * 512 + c * 256, 256)])
    weight_part(2)
    weight_sum(2)
    losses = [
        jnp.log(v[:, 0:64]) - v[:, 64:128] for v in (td[x * 2][0:1], td[x * 2 + 1][0:1])
    ]
    loss_ref[...] = jnp.concatenate(losses, axis=1)
    settle(len(pending))
    for n in range(32):
        d, _, _, remote = column_copy(n // 16, n // 4 % 4, n // 2 % 2, n % 2)

        @pl.when(d > 0)
        def _():
            remote.wait_send()

    for d in (1, 3, 2):
        got("wz", d - 1, wzr.at[d - 1])
    wg_ref[...] += wzr[0].astype(F32) + wzr[1].astype(F32) + wzr[2].astype(F32)
    for d in (1, 2, 3):
        copy("wz", d - 1, wzs.at[d - 1], wzr.at[d - 1], dev(core=1 - core)).wait_send()


def hand_over(*refs):
    copies = [pltpu.make_async_copy(refs[k], refs[4 + k], refs[8].at[k]) for k in range(4)]
    for c in copies:
        c.start()
    for c in copies:
        c.wait()


def body(attn_out, residual, o_weight, norm_gain, positive):
    vmem = pl.BlockSpec(memory_space=pltpu.VMEM)
    shape = jax.ShapeDtypeStruct
    scratch = [
        ((256, 512), BF16), ((256, 512), BF16), ((512, 4096), BF16), ((1, 512), F32),
        ((1, 128), jnp.int32),
        ((4, 3, 128, 512), WIRE), ((4, 2, 64, 512), F32), ((4, 2, 64, 512), WIRE),
        ((4, 2, 128, 512), WIRE), ((4, 128, 512), F32),
        ((2, 128, 512), WIRE), ((2, 128, 512), WIRE), ((256, 512), F32), ((256, 128), F32),
        ((2, 8, 8, 128), F32),
        ((512, 512), BF16), ((1024, 512), BF16), ((4, 8, 128), jnp.int32), ((512, 128), F32),
        ((4, 512, 256), F32), ((4, 2, 2, 32, 256), F32), ((4, 2, 2, 64, 256), F32), ((4, 64, 256), F32), ((4, 64, 256), F32),
        ((2, 512, 128), F32), ((4, 128, 1), F32), ((4, 8, 128), F32), ((8, 8, 128), F32),
        ((4, 512, 256), BF16), ((4, 512, 256), BF16),
        ((4, 256, 512), F32), ((4, 128, 512), F32), ((4, 128, 512), GZ_WIRE),
        ((3, 128, 512), GZ_WIRE), ((4, 128, 512), F32), ((3, 128, 512), F32), ((256, 512), F32),
        ((2, 8, 8, 128), F32),
        ((8, 2, 256, 256), BF16), ((4, 1024, 256), BF16), ((1024, 512), BF16),
        ((4, 2, 512, 128), F32), ((4, 512, 128), F32), ((3, 512, 128), WZ_WIRE),
        ((3, 512, 128), WZ_WIRE),
    ]
    outs = (
        shape((1, 128), F32), shape((256, 512), F32), shape((256, 512), F32),
        shape((512, 128), F32),
    )
    made = pl.pallas_call(
        kernel,
        name="step",
        out_shape=tuple(pltpu.VMEM(v.shape, v.dtype) for v in outs),
        in_specs=[pl.BlockSpec(memory_space=pl.ANY)] * 5,
        out_specs=[vmem] * 4,
        scratch_shapes=[pltpu.VMEM(s, t) for s, t in scratch]
        + [pltpu.SemaphoreType.DMA((n,)) for n in (COUNT, COUNT, 8)],
        compiler_params=pltpu.CompilerParams(
            collective_id=0, has_side_effects=True, vmem_limit_bytes=56 * 1024 * 1024
        ),
    )(
        attn_out.reshape(256, 512), residual.reshape(256, 512), o_weight,
        norm_gain.reshape(1, 512), positive.reshape(1, 128),
    )
    loss, rg, ag, wg = pl.pallas_call(
        hand_over,
        name="hand_over",
        out_shape=outs,
        in_specs=[vmem] * 4,
        out_specs=[pl.BlockSpec(memory_space=pl.ANY)] * 4,
        scratch_shapes=[pltpu.SemaphoreType.DMA((4,))],
    )(*made)
    return (
        loss.reshape(128), rg.reshape(2, 128, 512), ag.reshape(2, 128, 512), wg,
    )


def solution(mesh):
    placed = (P(None, "dp", "mp"), P(None, "dp", "mp"), P("mp", None), P("mp"), P("dp"))
    return jax.shard_map(
        body,
        mesh=mesh,
        in_specs=placed,
        out_specs=(P("dp"), P(None, "dp", "mp"), P(None, "dp", "mp"), P("mp", "dp")),
        check_vma=False,
    )
```

```python
import jax
import jax.numpy as jnp
from jax import lax
from jax.sharding import PartitionSpec as P
from jax.experimental import pallas as pl
from jax.experimental.pallas import tpu as pltpu

LOGIT_SCALE = 50.0
EPS = 1e-06
F32 = jnp.float32
BF16 = jnp.bfloat16
MESH = pl.DeviceIdType.MESH
WIRE = BF16
GZ_WIRE = BF16
WZ_WIRE = BF16

STAGES = dict(
    y1=24, z1=2, ss=14, qx=3, ps=3, ax=3, az=3, ac=4, ly=48, lz=4, tx=3, td=7,
    ez=4, ey=24, gc=4, gz=3, gq=3, rr=14, gh=4, gy=24, gx=32, wc=4, wz=3,
)
BASE = {}
COUNT = 0
for _name, _n in STAGES.items():
    BASE[_name] = COUNT
    COUNT += _n


def nt(a, b):
    return lax.dot_general(a, b, (((1,), (1,)), ((), ())), preferred_element_type=F32)


def tn(a, b):
    return lax.dot_general(a, b, (((0,), (0,)), ((), ())), preferred_element_type=F32)


def nn(a, b):
    return lax.dot_general(a, b, (((1,), (0,)), ((), ())), preferred_element_type=F32)


def to_row(col):
    n = col.shape[0]
    return jnp.broadcast_to(col, (n, 128)).T[0:8]


def to_col(row):
    n = row.shape[1]
    return jnp.broadcast_to(row, (128, n)).T[:, 0:1]


def rows(start, size, unit=None):
    return pl.ds(pl.multiple_of(start, unit or size), size)


def kernel(
    a_in, r_in, w_in, gain_in, pos_in,
    loss_ref, rg_ref, ag_ref, wg_ref,
    a_ref, r_ref, w_ref, gain_ref, pos_ref,
    ys, yf, yt, yr, own, zs, zr, sc, inv_s, ssb,
    qx, aa, px, pc, lg, lt, lr, lzs, lzr, pos_s, sums_s, txb, td,
    ea, sa, gap, gcr, gzs, gzr, gqs, gqr, ge, rb,
    gg, gx, ax, tb, tcr, wzs, wzr,
    send, recv, load,
):
    dp = lax.axis_index("dp")
    mp = lax.axis_index("mp")
    core, x, zl = dp % 2, (dp // 2) % 4, dp // 8
    y, zh = mp // 2, mp % 2
    j = mp
    pending = []

    def dev(core=core, x=x, zl=zl, y=y, zh=zh):
        return ((zl * 4 + x) * 2 + core, y * 2 + zh)

    def copy(stage, k, src, dst, to, r=None):
        return pltpu.make_async_remote_copy(
            src_ref=src, dst_ref=dst,
            send_sem=send.at[BASE[stage] + k],
            recv_sem=recv.at[BASE[stage] + (k if r is None else r)],
            device_id=to, device_id_type=MESH,
        )

    def go(*args):
        c = copy(*args)
        c.start()
        pending.append(c)

    def settle(upto):
        while len(settled) < min(upto, len(pending)):
            c = pending[len(settled)]
            c.wait_send()
            settled.append(c)

    settled = []

    def got(stage, k, dst):
        copy(stage, k, dst, dst, dev(core=1 - core)).wait_recv()

    def ring(v, d):
        return (v + d) % 4

    others = [(d, e) for d in (2, 1, 3, 0) for e in (1, 0) if (d, e) != (0, 0)]

    barrier = pltpu.get_barrier_semaphore()
    peers = [dev(y=ring(y, d), zh=(zh + e) % 2) for d, e in others]
    peers += [dev(x=ring(x, d)) for d in (1, 2, 3)]
    peers += [dev(zl=ring(zl, d)) for d in (1, 2, 3)]
    peers += [dev(core=1 - core)]
    for p in peers:
        pl.semaphore_signal(barrier, inc=1, device_id=p, device_id_type=MESH)

    loads = [pltpu.make_async_copy(a_in, a_ref, load.at[0])]
    for k in range(4):
        part = pl.ds(k * 128, 128)
        loads.append(pltpu.make_async_copy(w_in.at[part], w_ref.at[part], load.at[1 + k]))
    loads.append(pltpu.make_async_copy(pos_in, pos_ref, load.at[5]))
    loads.append(pltpu.make_async_copy(gain_in, gain_ref, load.at[6]))
    loads.append(pltpu.make_async_copy(r_in, r_ref, load.at[7]))
    for c in loads:
        c.start()
    for c in loads[:6]:
        c.wait()

    def half(h):
        return pl.ds(h * 128, 128)

    def product(h, yy, er):
        e = (1 - zh) if er == 0 else zh
        return nn(a_ref[half(h), :], w_ref[:, rows(yy * 1024 + e * 512, 512)])

    low, high = pl.ds(0, 64), pl.ds(64, 64)
    right, left = dev(y=ring(y, 1)), dev(y=ring(y, 3))

    def y_products(h):
        for er in (0, 1):
            c = h * 2 + er
            ys[c, 0] = product(h, ring(y, 2), er).astype(WIRE)
            near = product(h, ring(y, 1), er)
            yf[c, 0] = near[0:64]
            ys[c, 1, high, :] = near[64:128].astype(WIRE)
            near = product(h, ring(y, 3), er)
            yf[c, 1] = near[64:128]
            ys[c, 1, low, :] = near[0:64].astype(WIRE)

    def y_send(c):
        go("y1", c * 6 + 0, ys.at[c, 0, low], yt.at[c, 0], right)
        go("y1", c * 6 + 1, ys.at[c, 0, high], yt.at[c, 1], left)
        go("y1", c * 6 + 2, ys.at[c, 1, high], yr.at[c, 0, high], right)
        go("y1", c * 6 + 3, ys.at[c, 1, low], yr.at[c, 1, low], left)

    def y_hop(c):
        got("y1", c * 6 + 0, yt.at[c, 0])
        ys[c, 2, low, :] = (yf[c, 0] + yt[c, 0].astype(F32)).astype(WIRE)
        go("y1", c * 6 + 4, ys.at[c, 2, low], yr.at[c, 0, low], right)
        got("y1", c * 6 + 1, yt.at[c, 1])
        ys[c, 2, high, :] = (yf[c, 1] + yt[c, 1].astype(F32)).astype(WIRE)
        go("y1", c * 6 + 5, ys.at[c, 2, high], yr.at[c, 1, high], left)

    def y_sum(c):
        got("y1", c * 6 + 2, yr.at[c, 0, high])
        got("y1", c * 6 + 3, yr.at[c, 1, low])
        got("y1", c * 6 + 4, yr.at[c, 0, low])
        got("y1", c * 6 + 5, yr.at[c, 1, high])
        return own[c] + yr[c, 0].astype(F32) + yr[c, 1].astype(F32)

    def z_send(h):
        zs[h] = y_sum(h * 2).astype(WIRE)
        go("z1", h, zs.at[h], zr.at[h], dev(zh=1 - zh))

    def squares(h):
        got("z1", h, zr.at[h])
        proj = own[h * 2 + 1] + zr[h].astype(F32)
        scaled = (r_ref[half(h), :].astype(F32) + proj) * gain_ref[...]
        sc[half(h), :] = scaled
        ssb[h, 0] = to_row(jnp.sum(scaled * scaled, axis=1, keepdims=True))
        for d, e in others:
            k = d * 2 + e
            go("ss", h * 7 + k - 1, ssb.at[h, 0], ssb.at[h, k], dev(y=ring(y, d), zh=(zh + e) % 2))

    def embed(h):
        for d, e in others[::-1]:
            k = d * 2 + e
            got("ss", h * 7 + k - 1, ssb.at[h, k])
        total = ssb[h, 0]
        for k in range(1, 8):
            total = total + ssb[h, k]
        inv = to_col(lax.rsqrt(total[0:1] + EPS))
        inv_s[half(h), :] = jnp.broadcast_to(inv, (128, 128))
        return (sc[half(h), :] * inv).astype(BF16)

    y_products(0)
    y_products(1)
    px[x] = jnp.broadcast_to(pos_ref[...], (8, 128))
    pl.semaphore_wait(barrier, len(peers))
    y_send(0)
    y_send(2)
    for d in (2, 1, 3):
        go("ps", d - 1, px.at[x], px.at[x], dev(x=ring(x, d)))
        go("ax", d - 1, a_ref, ax.at[rows(x * 256, 256)], dev(x=ring(x, d)))
    for h in (0, 1):
        for er in (0, 1):
            own[h * 2 + er] = product(h, y, er)
    y_hop(0)
    y_send(1)
    y_hop(2)
    y_send(3)
    ax[rows(x * 256, 256), :] = a_ref[...]

    for c in loads[6:]:
        c.wait()
    z_send(0)
    y_hop(1)
    z_send(1)
    y_hop(3)
    own[1] = y_sum(1)
    squares(0)
    own[3] = y_sum(3)
    squares(1)
    early = len(pending)
    settle(early - 14)
    emb = embed(0)
    q_at = rows(x * 128, 128)
    qx[q_at, :] = emb
    for d in (2, 1, 3):
        go("qx", d - 1, qx.at[q_at], qx.at[q_at], dev(x=ring(x, d)))
    emb = embed(1)
    a_at = rows((zl * 2 + core) * 128, 128)
    aa[a_at, :] = emb
    go("ac", 0, aa.at[a_at], aa.at[a_at], dev(core=1 - core))
    for d in (2, 1, 3):
        go("az", d - 1, aa.at[a_at], aa.at[a_at], dev(zl=ring(zl, d)))
    for d in (1, 3, 2):
        got("ps", d - 1, px.at[ring(x, -d)])
    for xx in range(4):
        pc[pl.ds(xx * 128, 128), :] = jnp.broadcast_to(
            to_col(px[xx].astype(F32)[0:1]), (128, 128)
        )
    for d in (1, 3, 2):
        got("qx", d - 1, qx.at[rows(ring(x, -d) * 128, 128)])

    def block(yy, e):
        return rows((yy * 2 + e) * 64, 64)

    mine, pair = block(y, zh), block(y, 1 - zh)

    def logit_send(t):
        zz = ring(zl, -t)
        if t:
            at = rows((zz * 2 + core) * 128, 128)
            got("az", t - 1, aa.at[at])
            go("ac", t, aa.at[at], aa.at[at], dev(core=1 - core))
        got("ac", t, aa.at[rows((zz * 2 + 1 - core) * 128, 128)])
        lg[t] = nt(qx[...], aa[rows(zz * 256, 256), :])
        for er in (0, 1):
            k = t * 12 + er * 6
            far, after, before = (logit_piece(t, er, d) for d in (2, 1, 3))
            go("ly", k + 0, far.at[top], lt.at[t, er, 0], right)
            go("ly", k + 1, far.at[end], lt.at[t, er, 1], left)
            go("ly", k + 2, after.at[end], lr.at[t, er, 0, end], right)
            go("ly", k + 3, before.at[top], lr.at[t, er, 1, top], left)

    top, end = pl.ds(0, 32), pl.ds(32, 32)

    def logit_piece(t, er, d):
        return lg.at[t, block(ring(y, d), (1 - zh) if er == 0 else zh)]

    def logit_hop(t):
        for er in (0, 1):
            k = t * 12 + er * 6
            after, before = (logit_piece(t, er, d) for d in (1, 3))
            got("ly", k + 0, lt.at[t, er, 0])
            after[top, :] = after[top, :] + lt[t, er, 0]
            go("ly", k + 4, after.at[top], lr.at[t, er, 0, top], right)
            got("ly", k + 1, lt.at[t, er, 1])
            before[end, :] = before[end, :] + lt[t, er, 1]
            go("ly", k + 5, before.at[end], lr.at[t, er, 1, end], left)

    def logit_sum(t, er):
        k = t * 12 + er * 6
        got("ly", k + 2, lr.at[t, er, 0, end])
        got("ly", k + 3, lr.at[t, er, 1, top])
        got("ly", k + 4, lr.at[t, er, 0, top])
        got("ly", k + 5, lr.at[t, er, 1, end])
        return lg[t, pair if er == 0 else mine, :] + lr[t, er, 0] + lr[t, er, 1]

    def logit_pass(t):
        lzs[t] = logit_sum(t, 0)
        go("lz", t, lzs.at[t], lzr.at[t], dev(zh=1 - zh))

    lanes = lax.broadcasted_iota(jnp.int32, (128, 128), 1).astype(F32)

    def hits(t, at, c):
        first = (ring(zl, -t) * 1024 + x * 256 + c * 128).astype(F32)
        mark = pc[at, :] - first
        return lanes[0:mark.shape[0]] == mark

    def logit_done(t):
        part = logit_sum(t, 1)
        got("lz", t, lzr.at[t])
        logits = LOGIT_SCALE * (part + lzr[t])
        ex = jnp.exp(logits)
        ea[t, mine, :] = ex.astype(BF16)
        go("ez", t, ea.at[t, mine], ea.at[t, mine], dev(zh=1 - zh))
        exp_send(t, zh)
        hit = jnp.concatenate([hits(t, mine, 0), hits(t, mine, 1)], axis=1)
        sums_s[t] = jnp.concatenate(
            [
                jnp.sum(ex, axis=1, keepdims=True),
                jnp.sum(jnp.where(hit, logits, 0.0), axis=1, keepdims=True),
            ],
            axis=0,
        )

    def exp_send(t, e):
        part = ea.at[t, block(y, e)]
        go("ey", t * 6 + e, part, part, right)
        go("ey", t * 6 + 2 + e, part, part, left)
        go("ey", t * 6 + 4 + e, part, part, dev(y=ring(y, 2)))

    def exp_pass(t):
        got("ez", t, ea.at[t, pair])
        exp_send(t, 1 - zh)

    logit_send(0)
    logit_send(1)
    logit_hop(0)
    logit_send(3)
    logit_hop(1)
    logit_send(2)
    logit_pass(0)
    logit_hop(3)
    logit_pass(1)
    logit_hop(2)
    settle(early)
    logit_done(0)
    logit_pass(3)
    logit_done(1)
    exp_pass(0)
    logit_pass(2)
    logit_done(3)
    exp_pass(1)
    early = len(pending) - 24
    settle(early)
    logit_done(2)

    txb[0] = to_row(sums_s[0] + sums_s[1] + sums_s[2] + sums_s[3])
    for d in (2, 1, 3):
        go("tx", d - 1, txb.at[0], txb.at[d], dev(x=ring(x, d)))
    exp_pass(3)
    for d in (1, 3, 2):
        got("tx", d - 1, txb.at[d])
    td[j] = txb[0] + txb[1] + txb[2] + txb[3]
    for d, e in others:
        go("td", d * 2 + e - 1, td.at[j], td.at[j], dev(y=ring(y, d), zh=(zh + e) % 2))
    exp_pass(2)

    settle(early + 12)

    for d, e in others[::-1]:
        got("td", d * 2 + e - 1, td.at[ring(y, -d) * 2 + (zh + e) % 2])
    for xx in range(4):
        first, second = td[xx * 2][0:1], td[xx * 2 + 1][0:1]
        total = jnp.concatenate([first[:, 0:64], second[:, 0:64]], axis=1)
        top = jnp.concatenate([first[:, 64:128], second[:, 64:128]], axis=1)
        scale = LOGIT_SCALE / total
        at = pl.ds(xx * 128, 128)
        pos_s[0, at, :] = jnp.broadcast_to(to_col(scale), (128, 128))
        pos_s[1, at, :] = jnp.broadcast_to(
            to_col(jnp.exp(top) * scale - LOGIT_SCALE), (128, 128)
        )

    def score(t):
        for e in (0, 1):
            got("ey", t * 6 + e, ea.at[t, block(ring(y, 3), e)])
            got("ey", t * 6 + 2 + e, ea.at[t, block(ring(y, 1), e)])
            got("ey", t * 6 + 4 + e, ea.at[t, block(ring(y, 2), e)])
        for xx in range(4):
            at = pl.ds(xx * 128, 128)
            for c in (0, 1):
                part = pl.ds(c * 128, 128)
                rest = ea[t, at, part].astype(F32) * pos_s[0, at, :]
                sa[t, at, part] = jnp.where(
                    hits(t, at, c), pos_s[1, at, :], rest
                ).astype(BF16)

    def answers_part(t):
        gap[t] = tn(sa[t], qx[...])
        away = rows((1 - core) * 128, 128)
        go("gc", t, gap.at[t, away], gcr.at[t], dev(core=1 - core))

    def answers_sum(t):
        got("gc", t, gcr.at[t])
        both = gap[t, rows(core * 128, 128), :] + gcr[t]
        if t:
            gzs[t] = both.astype(GZ_WIRE)
            go("gz", t - 1, gzs.at[t], gzr.at[t - 1], dev(zl=ring(zl, -t)))
        else:
            ge[half(1), :] = both

    def queries_part(d):
        part = jnp.zeros((128, 512), F32)
        for t in range(4):
            left = sa[t, rows(ring(x, d) * 128, 128), :]
            part = part + nn(left, aa[rows(ring(zl, -t) * 256, 256), :])
        gqs[d] = part
        if d:
            go("gq", d - 1, gqs.at[d], gqr.at[d - 1], dev(x=ring(x, d)))

    score(2)
    answers_part(2)
    score(3)
    answers_part(3)
    answers_sum(2)
    score(1)
    answers_part(1)
    answers_sum(3)
    score(0)
    queries_part(2)
    answers_sum(1)
    queries_part(1)
    queries_part(3)
    answers_part(0)
    queries_part(0)
    answers_sum(0)

    def radial(h, g):
        at = half(h)
        ge[at, :] = g
        rb[h, 0] = to_row(jnp.sum(g * sc[at, :], axis=1, keepdims=True))
        for d, e in others:
            k = d * 2 + e
            go("rr", h * 7 + k - 1, rb.at[h, 0], rb.at[h, k], dev(y=ring(y, d), zh=(zh + e) % 2))

    def spread(h):
        at = half(h)
        tot = rb[h, 0]
        for d, e in others[::-1]:
            k = d * 2 + e
            got("rr", h * 7 + k - 1, rb.at[h, k])
        for k in range(1, 8):
            tot = tot + rb[h, k]
        rad = to_col(tot[0:1])
        iv = inv_s[at, 0:1]
        out = gain_ref[...] * (iv * ge[at, :] - (iv * iv * iv * rad) * sc[at, :])
        rg_ref[at, :] = out
        for c in (0, 1):
            gg[j, c, at, :] = out[:, c * 256:(c + 1) * 256].astype(BF16)
        for c in (0, 1):
            part = gg.at[j, c, at]
            go("gh", h * 2 + c, part, part, dev(zh=1 - zh))
        near(h, 0)

    def near(h, k):
        e = zh if k == 0 else 1 - zh
        for c in (0, 1):
            part = gg.at[y * 2 + e, c, half(h)]
            if k:
                got("gh", h * 2 + c, part)
            go("gy", h * 12 + k * 6 + c, part, part, right)
            go("gy", h * 12 + k * 6 + 2 + c, part, part, left)

    def hop(h, k):
        e = zh if k == 0 else 1 - zh
        part = gg.at[ring(y, 3) * 2 + e, 0, half(h)]
        got("gy", h * 12 + k * 6, part)
        go("gy", h * 12 + k * 6 + 4, part, part, right)
        part = gg.at[ring(y, 1) * 2 + e, 1, half(h)]
        got("gy", h * 12 + k * 6 + 3, part)
        go("gy", h * 12 + k * 6 + 5, part, part, left)

    def column_copy(h, t, k, c):
        e = zh if k == 0 else 1 - zh
        xx = e * 2 + c
        d = (xx - x + 4) % 4
        src = gg.at[ring(y, -t) * 2 + e, c, half(h)]
        dst = gx.at[t, rows(x * 256 + h * 128, 128)]
        n = t * 2 + h
        return d, src, dst, copy("gx", (n * 2 + k) * 2 + c, src, dst, dev(x=xx), n * 3 + d - 1)

    def columns(h, t, k):
        for n, c in {0: (), 1: ((1, 1),), 3: ((2, 0),), 2: ((4, 0), (5, 1))}[t]:
            e = zh if k == 0 else 1 - zh
            got("gy", h * 12 + k * 6 + n, gg.at[ring(y, -t) * 2 + e, c, half(h)])
        for c in (0, 1):
            d, src, dst, remote = column_copy(h, t, k, c)

            @pl.when(d > 0)
            def _():
                remote.start()

            @pl.when(d == 0)
            def _():
                dst[...] = src[...]

    early = len(pending)
    settle(early - 10)
    for d in (1, 3, 2):
        got("gq", d - 1, gqr.at[d - 1])
    radial(0, gqs[0] + gqr[0] + gqr[1] + gqr[2])
    for d in (1, 3, 2):
        got("gz", d - 1, gzr.at[d - 1])
    radial(1, ge[half(1), :] + gzr[0].astype(F32) + gzr[1].astype(F32) + gzr[2].astype(F32))
    spread(0)
    columns(0, 0, 0)
    spread(1)
    columns(1, 0, 0)
    hop(0, 0)
    columns(0, 1, 0)
    columns(0, 3, 0)
    hop(1, 0)
    columns(1, 1, 0)
    columns(1, 3, 0)
    settle(early)
    near(0, 1)
    columns(0, 0, 1)
    columns(0, 2, 0)
    hop(0, 1)
    columns(0, 1, 1)
    columns(0, 3, 1)
    columns(1, 2, 0)
    near(1, 1)
    columns(1, 0, 1)
    columns(0, 2, 1)
    hop(1, 1)

    for d in (1, 3, 2):
        got("ax", d - 1, ax.at[rows(ring(x, -d) * 256, 256)])

    def weight_part(t):
        for h in (0, 1):
            for d in (1, 3, 2):
                got("gx", (t * 2 + h) * 3 + d - 1,
                    gx.at[t, rows(ring(x, -d) * 256 + h * 128, 128)])
        part = tn(ax[...], gx[t])
        tb[t, 0] = part[:, 0:128]
        tb[t, 1] = part[:, 128:256]
        go("wc", t, tb.at[t, 1 - core], tcr.at[t], dev(core=1 - core))

    def weight_sum(t):
        got("wc", t, tcr.at[t])
        zz = ring(y, -t)
        d = (zz - zl + 4) % 4
        both = tb[t, core] + tcr[t]

        @pl.when(d > 0)
        def _():
            wzs[d - 1] = both.astype(WZ_WIRE)
            copy("wz", d - 1, wzs.at[d - 1], wzr.at[d - 1], dev(zl=zz)).start()

        @pl.when(d == 0)
        def _():
            wg_ref[...] = both

    columns(1, 1, 1)
    columns(1, 3, 1)
    weight_part(0)
    columns(1, 2, 1)
    weight_sum(0)
    weight_part(1)
    weight_part(3)
    weight_sum(1)
    weight_sum(3)

    ag_ref[...] = jnp.zeros((256, 512), F32)
    for jj in range(8):
        for c in (0, 1):
            ag_ref[...] += nt(gg[jj, c], w_ref[:, pl.ds(jj * 512 + c * 256, 256)])
    weight_part(2)
    weight_sum(2)
    losses = [
        jnp.log(v[:, 0:64]) - v[:, 64:128] for v in (td[x * 2][0:1], td[x * 2 + 1][0:1])
    ]
    loss_ref[...] = jnp.concatenate(losses, axis=1)
    settle(len(pending))
    for n in range(32):
        d, _, _, remote = column_copy(n // 16, n // 4 % 4, n // 2 % 2, n % 2)

        @pl.when(d > 0)
        def _():
            remote.wait_send()

    for d in (1, 3, 2):
        got("wz", d - 1, wzr.at[d - 1])
    wg_ref[...] += wzr[0].astype(F32) + wzr[1].astype(F32) + wzr[2].astype(F32)
    for d in (1, 2, 3):
        copy("wz", d - 1, wzs.at[d - 1], wzr.at[d - 1], dev(core=1 - core)).wait_send()


def hand_over(*refs):
    copies = [pltpu.make_async_copy(refs[k], refs[4 + k], refs[8].at[k]) for k in range(4)]
    for c in copies:
        c.start()
    for c in copies:
        c.wait()


def body(attn_out, residual, o_weight, norm_gain, positive):
    vmem = pl.BlockSpec(memory_space=pltpu.VMEM)
    shape = jax.ShapeDtypeStruct
    scratch = [
        ((256, 512), BF16), ((256, 512), BF16), ((512, 4096), BF16), ((1, 512), F32),
        ((1, 128), jnp.int32),
        ((4, 3, 128, 512), WIRE), ((4, 2, 64, 512), F32), ((4, 2, 64, 512), WIRE),
        ((4, 2, 128, 512), WIRE), ((4, 128, 512), F32),
        ((2, 128, 512), WIRE), ((2, 128, 512), WIRE), ((256, 512), F32), ((256, 128), F32),
        ((2, 8, 8, 128), F32),
        ((512, 512), BF16), ((1024, 512), BF16), ((4, 8, 128), jnp.int32), ((512, 128), F32),
        ((4, 512, 256), F32), ((4, 2, 2, 32, 256), F32), ((4, 2, 2, 64, 256), F32), ((4, 64, 256), F32), ((4, 64, 256), F32),
        ((2, 512, 128), F32), ((4, 128, 1), F32), ((4, 8, 128), F32), ((8, 8, 128), F32),
        ((4, 512, 256), BF16), ((4, 512, 256), BF16),
        ((4, 256, 512), F32), ((4, 128, 512), F32), ((4, 128, 512), GZ_WIRE),
        ((3, 128, 512), GZ_WIRE), ((4, 128, 512), F32), ((3, 128, 512), F32), ((256, 512), F32),
        ((2, 8, 8, 128), F32),
        ((8, 2, 256, 256), BF16), ((4, 1024, 256), BF16), ((1024, 512), BF16),
        ((4, 2, 512, 128), F32), ((4, 512, 128), F32), ((3, 512, 128), WZ_WIRE),
        ((3, 512, 128), WZ_WIRE),
    ]
    outs = (
        shape((1, 128), F32), shape((256, 512), F32), shape((256, 512), F32),
        shape((512, 128), F32),
    )
    made = pl.pallas_call(
        kernel,
        name="step",
        out_shape=tuple(pltpu.VMEM(v.shape, v.dtype) for v in outs),
        in_specs=[pl.BlockSpec(memory_space=pl.ANY)] * 5,
        out_specs=[vmem] * 4,
        scratch_shapes=[pltpu.VMEM(s, t) for s, t in scratch]
        + [pltpu.SemaphoreType.DMA((n,)) for n in (COUNT, COUNT, 8)],
        compiler_params=pltpu.CompilerParams(
            collective_id=0, has_side_effects=True, vmem_limit_bytes=56 * 1024 * 1024
        ),
    )(
        attn_out.reshape(256, 512), residual.reshape(256, 512), o_weight,
        norm_gain.reshape(1, 512), positive.reshape(1, 128),
    )
    loss, rg, ag, wg = pl.pallas_call(
        hand_over,
        name="hand_over",
        out_shape=outs,
        in_specs=[vmem] * 4,
        out_specs=[pl.BlockSpec(memory_space=pl.ANY)] * 4,
        scratch_shapes=[pltpu.SemaphoreType.DMA((4,))],
        compiler_params=pltpu.CompilerParams(vmem_limit_bytes=4 * 1024 * 1024),
    )(*made)
    return (
        loss.reshape(128), rg.reshape(2, 128, 512), ag.reshape(2, 128, 512), wg,
    )


def solution(mesh):
    placed = (P(None, "dp", "mp"), P(None, "dp", "mp"), P("mp", None), P("mp"), P("dp"))
    return jax.shard_map(
        body,
        mesh=mesh,
        in_specs=placed,
        out_specs=(P("dp"), P(None, "dp", "mp"), P(None, "dp", "mp"), P("mp", "dp")),
        check_vma=False,
    )
```

```python
import jax
import jax.numpy as jnp
from jax import lax
from jax.sharding import PartitionSpec as P
from jax.experimental import pallas as pl
from jax.experimental.pallas import tpu as pltpu

LOGIT_SCALE = 50.0
EPS = 1e-06
F32 = jnp.float32
BF16 = jnp.bfloat16
MESH = pl.DeviceIdType.MESH
WIRE = BF16
GZ_WIRE = BF16
WZ_WIRE = BF16

STAGES = dict(
    y1=24, z1=2, ss=14, qx=3, ps=3, ax=3, az=3, ac=4, ly=48, lz=4, tx=3, td=7,
    ez=4, ey=24, gc=4, gz=3, gq=3, rr=14, gh=4, gy=24, gx=32, wc=4, wz=3,
)
BASE = {}
COUNT = 0
for _name, _n in STAGES.items():
    BASE[_name] = COUNT
    COUNT += _n


def nt(a, b):
    return lax.dot_general(a, b, (((1,), (1,)), ((), ())), preferred_element_type=F32)


def tn(a, b):
    return lax.dot_general(a, b, (((0,), (0,)), ((), ())), preferred_element_type=F32)


def nn(a, b):
    return lax.dot_general(a, b, (((1,), (0,)), ((), ())), preferred_element_type=F32)


def to_row(col):
    n = col.shape[0]
    return jnp.broadcast_to(col, (n, 128)).T[0:8]


def to_col(row):
    n = row.shape[1]
    return jnp.broadcast_to(row, (128, n)).T[:, 0:1]


def rows(start, size, unit=None):
    return pl.ds(pl.multiple_of(start, unit or size), size)


def kernel(
    a_in, r_in, w_in, gain_in, pos_in,
    loss_ref, rg_ref, ag_ref, wg_ref,
    a_ref, r_ref, w_ref, gain_ref, pos_ref,
    ys, yf, yt, yr, own, zs, zr, sc, inv_s, ssb,
    qx, aa, px, pc, lg, lt, lr, lzs, lzr, pos_s, sums_s, txb, td,
    ea, sa, gap, gcr, gzs, gzr, gqs, gqr, ge, rb,
    gg, gx, ax, tb, tcr, wzs, wzr,
    send, recv, load,
):
    dp = lax.axis_index("dp")
    mp = lax.axis_index("mp")
    core, x, zl = dp % 2, (dp // 2) % 4, dp // 8
    y, zh = mp // 2, mp % 2
    j = mp
    pending = []

    def dev(core=core, x=x, zl=zl, y=y, zh=zh):
        return ((zl * 4 + x) * 2 + core, y * 2 + zh)

    def copy(stage, k, src, dst, to, r=None):
        return pltpu.make_async_remote_copy(
            src_ref=src, dst_ref=dst,
            send_sem=send.at[BASE[stage] + k],
            recv_sem=recv.at[BASE[stage] + (k if r is None else r)],
            device_id=to, device_id_type=MESH,
        )

    def go(*args):
        c = copy(*args)
        c.start()
        pending.append(c)

    def settle(upto):
        while len(settled) < min(upto, len(pending)):
            c = pending[len(settled)]
            c.wait_send()
            settled.append(c)

    settled = []

    def got(stage, k, dst):
        copy(stage, k, dst, dst, dev(core=1 - core)).wait_recv()

    def ring(v, d):
        return (v + d) % 4

    others = [(d, e) for d in (2, 1, 3, 0) for e in (1, 0) if (d, e) != (0, 0)]

    barrier = pltpu.get_barrier_semaphore()
    peers = [dev(y=ring(y, d), zh=(zh + e) % 2) for d, e in others]
    peers += [dev(x=ring(x, d)) for d in (1, 2, 3)]
    peers += [dev(zl=ring(zl, d)) for d in (1, 2, 3)]
    peers += [dev(core=1 - core)]
    for p in peers:
        pl.semaphore_signal(barrier, inc=1, device_id=p, device_id_type=MESH)

    loads = [pltpu.make_async_copy(a_in, a_ref, load.at[0])]
    for k in range(4):
        part = pl.ds(k * 128, 128)
        loads.append(pltpu.make_async_copy(w_in.at[part], w_ref.at[part], load.at[1 + k]))
    loads.append(pltpu.make_async_copy(pos_in, pos_ref, load.at[5]))
    loads.append(pltpu.make_async_copy(gain_in, gain_ref, load.at[6]))
    loads.append(pltpu.make_async_copy(r_in, r_ref, load.at[7]))
    for c in loads:
        c.start()
    for c in loads[:6]:
        c.wait()

    def half(h):
        return pl.ds(h * 128, 128)

    def product(h, yy, er):
        e = (1 - zh) if er == 0 else zh
        return nn(a_ref[half(h), :], w_ref[:, rows(yy * 1024 + e * 512, 512)])

    low, high = pl.ds(0, 64), pl.ds(64, 64)
    right, left = dev(y=ring(y, 1)), dev(y=ring(y, 3))

    def y_products(h):
        for er in (0, 1):
            c = h * 2 + er
            ys[c, 0] = product(h, ring(y, 2), er).astype(WIRE)
            near = product(h, ring(y, 1), er)
            yf[c, 0] = near[0:64]
            ys[c, 1, high, :] = near[64:128].astype(WIRE)
            near = product(h, ring(y, 3), er)
            yf[c, 1] = near[64:128]
            ys[c, 1, low, :] = near[0:64].astype(WIRE)

    def y_send(c):
        go("y1", c * 6 + 0, ys.at[c, 0, low], yt.at[c, 0], right)
        go("y1", c * 6 + 1, ys.at[c, 0, high], yt.at[c, 1], left)
        go("y1", c * 6 + 2, ys.at[c, 1, high], yr.at[c, 0, high], right)
        go("y1", c * 6 + 3, ys.at[c, 1, low], yr.at[c, 1, low], left)

    def y_hop(c):
        got("y1", c * 6 + 0, yt.at[c, 0])
        ys[c, 2, low, :] = (yf[c, 0] + yt[c, 0].astype(F32)).astype(WIRE)
        go("y1", c * 6 + 4, ys.at[c, 2, low], yr.at[c, 0, low], right)
        got("y1", c * 6 + 1, yt.at[c, 1])
        ys[c, 2, high, :] = (yf[c, 1] + yt[c, 1].astype(F32)).astype(WIRE)
        go("y1", c * 6 + 5, ys.at[c, 2, high], yr.at[c, 1, high], left)

    def y_sum(c):
        got("y1", c * 6 + 2, yr.at[c, 0, high])
        got("y1", c * 6 + 3, yr.at[c, 1, low])
        got("y1", c * 6 + 4, yr.at[c, 0, low])
        got("y1", c * 6 + 5, yr.at[c, 1, high])
        return own[c] + yr[c, 0].astype(F32) + yr[c, 1].astype(F32)

    def z_send(h):
        zs[h] = y_sum(h * 2).astype(WIRE)
        go("z1", h, zs.at[h], zr.at[h], dev(zh=1 - zh))

    def squares(h):
        got("z1", h, zr.at[h])
        proj = own[h * 2 + 1] + zr[h].astype(F32)
        scaled = (r_ref[half(h), :].astype(F32) + proj) * gain_ref[...]
        sc[half(h), :] = scaled
        ssb[h, 0] = to_row(jnp.sum(scaled * scaled, axis=1, keepdims=True))
        for d, e in others:
            k = d * 2 + e
            go("ss", h * 7 + k - 1, ssb.at[h, 0], ssb.at[h, k], dev(y=ring(y, d), zh=(zh + e) % 2))

    def embed(h):
        for d, e in others[::-1]:
            k = d * 2 + e
            got("ss", h * 7 + k - 1, ssb.at[h, k])
        total = ssb[h, 0]
        for k in range(1, 8):
            total = total + ssb[h, k]
        inv = to_col(lax.rsqrt(total[0:1] + EPS))
        inv_s[half(h), :] = jnp.broadcast_to(inv, (128, 128))
        return (sc[half(h), :] * inv).astype(BF16)

    y_products(0)
    px[x] = jnp.broadcast_to(pos_ref[...], (8, 128))
    pl.semaphore_wait(barrier, len(peers))
    y_send(0)
    y_products(1)
    y_send(2)
    for d in (2, 1, 3):
        go("ps", d - 1, px.at[x], px.at[x], dev(x=ring(x, d)))
        go("ax", d - 1, a_ref, ax.at[rows(x * 256, 256)], dev(x=ring(x, d)))
    for h in (0, 1):
        for er in (0, 1):
            own[h * 2 + er] = product(h, y, er)
    y_hop(0)
    y_send(1)
    y_hop(2)
    y_send(3)
    ax[rows(x * 256, 256), :] = a_ref[...]

    for c in loads[6:]:
        c.wait()
    z_send(0)
    y_hop(1)
    z_send(1)
    y_hop(3)
    own[1] = y_sum(1)
    squares(0)
    own[3] = y_sum(3)
    squares(1)
    early = len(pending)
    settle(early - 14)
    emb = embed(0)
    q_at = rows(x * 128, 128)
    qx[q_at, :] = emb
    for d in (2, 1, 3):
        go("qx", d - 1, qx.at[q_at], qx.at[q_at], dev(x=ring(x, d)))
    emb = embed(1)
    a_at = rows((zl * 2 + core) * 128, 128)
    aa[a_at, :] = emb
    go("ac", 0, aa.at[a_at], aa.at[a_at], dev(core=1 - core))
    for d in (2, 1, 3):
        go("az", d - 1, aa.at[a_at], aa.at[a_at], dev(zl=ring(zl, d)))
    for d in (1, 3, 2):
        got("ps", d - 1, px.at[ring(x, -d)])
    for xx in range(4):
        pc[pl.ds(xx * 128, 128), :] = jnp.broadcast_to(
            to_col(px[xx].astype(F32)[0:1]), (128, 128)
        )
    for d in (1, 3, 2):
        got("qx", d - 1, qx.at[rows(ring(x, -d) * 128, 128)])

    def block(yy, e):
        return rows((yy * 2 + e) * 64, 64)

    mine, pair = block(y, zh), block(y, 1 - zh)

    def logit_send(t):
        zz = ring(zl, -t)
        if t:
            at = rows((zz * 2 + core) * 128, 128)
            got("az", t - 1, aa.at[at])
            go("ac", t, aa.at[at], aa.at[at], dev(core=1 - core))
        got("ac", t, aa.at[rows((zz * 2 + 1 - core) * 128, 128)])
        lg[t] = nt(qx[...], aa[rows(zz * 256, 256), :])
        for er in (0, 1):
            k = t * 12 + er * 6
            far, after, before = (logit_piece(t, er, d) for d in (2, 1, 3))
            go("ly", k + 0, far.at[top], lt.at[t, er, 0], right)
            go("ly", k + 1, far.at[end], lt.at[t, er, 1], left)
            go("ly", k + 2, after.at[end], lr.at[t, er, 0, end], right)
            go("ly", k + 3, before.at[top], lr.at[t, er, 1, top], left)

    top, end = pl.ds(0, 32), pl.ds(32, 32)

    def logit_piece(t, er, d):
        return lg.at[t, block(ring(y, d), (1 - zh) if er == 0 else zh)]

    def logit_hop(t):
        for er in (0, 1):
            k = t * 12 + er * 6
            after, before = (logit_piece(t, er, d) for d in (1, 3))
            got("ly", k + 0, lt.at[t, er, 0])
            after[top, :] = after[top, :] + lt[t, er, 0]
            go("ly", k + 4, after.at[top], lr.at[t, er, 0, top], right)
            got("ly", k + 1, lt.at[t, er, 1])
            before[end, :] = before[end, :] + lt[t, er, 1]
            go("ly", k + 5, before.at[end], lr.at[t, er, 1, end], left)

    def logit_sum(t, er):
        k = t * 12 + er * 6
        got("ly", k + 2, lr.at[t, er, 0, end])
        got("ly", k + 3, lr.at[t, er, 1, top])
        got("ly", k + 4, lr.at[t, er, 0, top])
        got("ly", k + 5, lr.at[t, er, 1, end])
        return lg[t, pair if er == 0 else mine, :] + lr[t, er, 0] + lr[t, er, 1]

    def logit_pass(t):
        lzs[t] = logit_sum(t, 0)
        go("lz", t, lzs.at[t], lzr.at[t], dev(zh=1 - zh))

    lanes = lax.broadcasted_iota(jnp.int32, (128, 128), 1).astype(F32)

    def hits(t, at, c):
        first = (ring(zl, -t) * 1024 + x * 256 + c * 128).astype(F32)
        mark = pc[at, :] - first
        return lanes[0:mark.shape[0]] == mark

    def logit_done(t):
        part = logit_sum(t, 1)
        got("lz", t, lzr.at[t])
        logits = LOGIT_SCALE * (part + lzr[t])
        ex = jnp.exp(logits)
        ea[t, mine, :] = ex.astype(BF16)
        go("ez", t, ea.at[t, mine], ea.at[t, mine], dev(zh=1 - zh))
        exp_send(t, zh)
        hit = jnp.concatenate([hits(t, mine, 0), hits(t, mine, 1)], axis=1)
        sums_s[t] = jnp.concatenate(
            [
                jnp.sum(ex, axis=1, keepdims=True),
                jnp.sum(jnp.where(hit, logits, 0.0), axis=1, keepdims=True),
            ],
            axis=0,
        )

    def exp_send(t, e):
        part = ea.at[t, block(y, e)]
        go("ey", t * 6 + e, part, part, right)
        go("ey", t * 6 + 2 + e, part, part, left)
        go("ey", t * 6 + 4 + e, part, part, dev(y=ring(y, 2)))

    def exp_pass(t):
        got("ez", t, ea.at[t, pair])
        exp_send(t, 1 - zh)

    logit_send(0)
    logit_send(1)
    logit_hop(0)
    logit_send(3)
    logit_hop(1)
    logit_send(2)
    logit_pass(0)
    logit_hop(3)
    logit_pass(1)
    logit_hop(2)
    settle(early)
    logit_done(0)
    logit_pass(3)
    logit_done(1)
    exp_pass(0)
    logit_pass(2)
    logit_done(3)
    exp_pass(1)
    early = len(pending) - 24
    settle(early)
    logit_done(2)

    txb[0] = to_row(sums_s[0] + sums_s[1] + sums_s[2] + sums_s[3])
    for d in (2, 1, 3):
        go("tx", d - 1, txb.at[0], txb.at[d], dev(x=ring(x, d)))
    exp_pass(3)
    for d in (1, 3, 2):
        got("tx", d - 1, txb.at[d])
    td[j] = txb[0] + txb[1] + txb[2] + txb[3]
    for d, e in others:
        go("td", d * 2 + e - 1, td.at[j], td.at[j], dev(y=ring(y, d), zh=(zh + e) % 2))
    exp_pass(2)

    settle(early + 12)

    for d, e in others[::-1]:
        got("td", d * 2 + e - 1, td.at[ring(y, -d) * 2 + (zh + e) % 2])
    for xx in range(4):
        first, second = td[xx * 2][0:1], td[xx * 2 + 1][0:1]
        total = jnp.concatenate([first[:, 0:64], second[:, 0:64]], axis=1)
        top = jnp.concatenate([first[:, 64:128], second[:, 64:128]], axis=1)
        scale = LOGIT_SCALE / total
        at = pl.ds(xx * 128, 128)
        pos_s[0, at, :] = jnp.broadcast_to(to_col(scale), (128, 128))
        pos_s[1, at, :] = jnp.broadcast_to(
            to_col(-LOGIT_SCALE * ((total - jnp.exp(top)) / total)), (128, 128)
        )

    def score(t):
        for e in (0, 1):
            got("ey", t * 6 + e, ea.at[t, block(ring(y, 3), e)])
            got("ey", t * 6 + 2 + e, ea.at[t, block(ring(y, 1), e)])
            got("ey", t * 6 + 4 + e, ea.at[t, block(ring(y, 2), e)])
        for xx in range(4):
            at = pl.ds(xx * 128, 128)
            for c in (0, 1):
                part = pl.ds(c * 128, 128)
                rest = ea[t, at, part].astype(F32) * pos_s[0, at, :]
                sa[t, at, part] = jnp.where(
                    hits(t, at, c), pos_s[1, at, :], rest
                ).astype(BF16)

    def answers_part(t):
        gap[t] = tn(sa[t], qx[...])
        away = rows((1 - core) * 128, 128)
        go("gc", t, gap.at[t, away], gcr.at[t], dev(core=1 - core))

    def answers_sum(t):
        got("gc", t, gcr.at[t])
        both = gap[t, rows(core * 128, 128), :] + gcr[t]
        if t:
            gzs[t] = both.astype(GZ_WIRE)
            go("gz", t - 1, gzs.at[t], gzr.at[t - 1], dev(zl=ring(zl, -t)))
        else:
            ge[half(1), :] = both

    def queries_part(d):
        part = jnp.zeros((128, 512), F32)
        for t in range(4):
            left = sa[t, rows(ring(x, d) * 128, 128), :]
            part = part + nn(left, aa[rows(ring(zl, -t) * 256, 256), :])
        gqs[d] = part
        if d:
            go("gq", d - 1, gqs.at[d], gqr.at[d - 1], dev(x=ring(x, d)))

    score(2)
    answers_part(2)
    score(3)
    answers_part(3)
    answers_sum(2)
    score(1)
    answers_part(1)
    answers_sum(3)
    score(0)
    queries_part(2)
    answers_sum(1)
    queries_part(1)
    queries_part(3)
    answers_part(0)
    queries_part(0)
    answers_sum(0)

    def radial(h, g):
        at = half(h)
        ge[at, :] = g
        rb[h, 0] = to_row(jnp.sum(g * sc[at, :], axis=1, keepdims=True))
        for d, e in others:
            k = d * 2 + e
            go("rr", h * 7 + k - 1, rb.at[h, 0], rb.at[h, k], dev(y=ring(y, d), zh=(zh + e) % 2))

    def spread(h):
        at = half(h)
        tot = rb[h, 0]
        for d, e in others[::-1]:
            k = d * 2 + e
            got("rr", h * 7 + k - 1, rb.at[h, k])
        for k in range(1, 8):
            tot = tot + rb[h, k]
        rad = to_col(tot[0:1])
        iv = inv_s[at, 0:1]
        out = gain_ref[...] * (iv * ge[at, :] - (iv * iv * iv * rad) * sc[at, :])
        rg_ref[at, :] = out
        for c in (0, 1):
            gg[j, c, at, :] = out[:, c * 256:(c + 1) * 256].astype(BF16)
        for c in (0, 1):
            part = gg.at[j, c, at]
            go("gh", h * 2 + c, part, part, dev(zh=1 - zh))
        near(h, 0)

    def near(h, k):
        e = zh if k == 0 else 1 - zh
        for c in (0, 1):
            part = gg.at[y * 2 + e, c, half(h)]
            if k:
                got("gh", h * 2 + c, part)
            go("gy", h * 12 + k * 6 + c, part, part, right)
            go("gy", h * 12 + k * 6 + 2 + c, part, part, left)
            if straight(h, k):
                go("gy", h * 12 + k * 6 + 4 + c, part, part, dev(y=ring(y, 2)))

    def straight(h, k):
        return h == 1 and k == 1

    def hop(h, k):
        e = zh if k == 0 else 1 - zh
        part = gg.at[ring(y, 3) * 2 + e, 0, half(h)]
        got("gy", h * 12 + k * 6, part)
        go("gy", h * 12 + k * 6 + 4, part, part, right)
        part = gg.at[ring(y, 1) * 2 + e, 1, half(h)]
        got("gy", h * 12 + k * 6 + 3, part)
        go("gy", h * 12 + k * 6 + 5, part, part, left)

    def column_copy(h, t, k, c):
        e = zh if k == 0 else 1 - zh
        xx = e * 2 + c
        d = (xx - x + 4) % 4
        src = gg.at[ring(y, -t) * 2 + e, c, half(h)]
        dst = gx.at[t, rows(x * 256 + h * 128, 128)]
        n = t * 2 + h
        return d, src, dst, copy("gx", (n * 2 + k) * 2 + c, src, dst, dev(x=xx), n * 3 + d - 1)

    def columns(h, t, k):
        arrivals = {0: (), 1: ((1, 1),), 3: ((2, 0),), 2: ((4, 0), (5, 1))}[t]
        if straight(h, k):
            arrivals += {0: (), 1: ((0, 0),), 3: ((3, 1),), 2: ()}[t]
        for n, c in arrivals:
            e = zh if k == 0 else 1 - zh
            got("gy", h * 12 + k * 6 + n, gg.at[ring(y, -t) * 2 + e, c, half(h)])
        for c in (0, 1):
            d, src, dst, remote = column_copy(h, t, k, c)

            @pl.when(d > 0)
            def _():
                remote.start()

            @pl.when(d == 0)
            def _():
                dst[...] = src[...]

    early = len(pending)
    settle(early - 10)
    for d in (1, 3, 2):
        got("gq", d - 1, gqr.at[d - 1])
    radial(0, gqs[0] + gqr[0] + gqr[1] + gqr[2])
    for d in (1, 3, 2):
        got("gz", d - 1, gzr.at[d - 1])
    radial(1, ge[half(1), :] + gzr[0].astype(F32) + gzr[1].astype(F32) + gzr[2].astype(F32))
    spread(0)
    columns(0, 0, 0)
    spread(1)
    columns(1, 0, 0)
    hop(0, 0)
    columns(0, 1, 0)
    columns(0, 3, 0)
    hop(1, 0)
    columns(1, 1, 0)
    columns(1, 3, 0)
    settle(early)
    near(0, 1)
    columns(0, 0, 1)
    columns(0, 2, 0)
    hop(0, 1)
    columns(0, 1, 1)
    columns(0, 3, 1)
    columns(1, 2, 0)
    near(1, 1)
    columns(1, 0, 1)
    columns(0, 2, 1)

    for d in (1, 3, 2):
        got("ax", d - 1, ax.at[rows(ring(x, -d) * 256, 256)])

    def weight_part(t):
        for h in (0, 1):
            for d in (1, 3, 2):
                got("gx", (t * 2 + h) * 3 + d - 1,
                    gx.at[t, rows(ring(x, -d) * 256 + h * 128, 128)])
        part = tn(ax[...], gx[t])
        tb[t, 0] = part[:, 0:128]
        tb[t, 1] = part[:, 128:256]
        go("wc", t, tb.at[t, 1 - core], tcr.at[t], dev(core=1 - core))

    def weight_sum(t):
        got("wc", t, tcr.at[t])
        zz = ring(y, -t)
        d = (zz - zl + 4) % 4
        both = tb[t, core] + tcr[t]

        @pl.when(d > 0)
        def _():
            wzs[d - 1] = both.astype(WZ_WIRE)
            copy("wz", d - 1, wzs.at[d - 1], wzr.at[d - 1], dev(zl=zz)).start()

        @pl.when(d == 0)
        def _():
            wg_ref[...] = both

    columns(1, 1, 1)
    columns(1, 3, 1)
    weight_part(0)
    columns(1, 2, 1)
    weight_sum(0)
    weight_part(1)
    weight_part(3)
    weight_sum(1)
    weight_sum(3)

    weight_part(2)
    weight_sum(2)
    ag_ref[...] = jnp.zeros((256, 512), F32)
    for jj in range(8):
        for c in (0, 1):
            ag_ref[...] += nt(gg[jj, c], w_ref[:, pl.ds(jj * 512 + c * 256, 256)])
    losses = []
    for v in (td[x * 2][0:1], td[x * 2 + 1][0:1]):
        total, top = v[:, 0:64], v[:, 64:128]
        peak = jnp.exp(top)
        losses.append(
            jnp.where(
                total < 4.0 * peak, jnp.log1p((total - peak) / peak), jnp.log(total) - top
            )
        )
    loss_ref[...] = jnp.concatenate(losses, axis=1)
    settle(len(pending))
    for n in range(32):
        d, _, _, remote = column_copy(n // 16, n // 4 % 4, n // 2 % 2, n % 2)

        @pl.when(d > 0)
        def _():
            remote.wait_send()

    for d in (1, 3, 2):
        got("wz", d - 1, wzr.at[d - 1])
    wg_ref[...] += wzr[0].astype(F32) + wzr[1].astype(F32) + wzr[2].astype(F32)
    for d in (1, 2, 3):
        copy("wz", d - 1, wzs.at[d - 1], wzr.at[d - 1], dev(core=1 - core)).wait_send()


def hand_over(*refs):
    copies = [pltpu.make_async_copy(refs[k], refs[4 + k], refs[8].at[k]) for k in range(4)]
    for c in copies:
        c.start()
    for c in copies:
        c.wait()


def body(attn_out, residual, o_weight, norm_gain, positive):
    vmem = pl.BlockSpec(memory_space=pltpu.VMEM)
    shape = jax.ShapeDtypeStruct
    scratch = [
        ((256, 512), BF16), ((256, 512), BF16), ((512, 4096), BF16), ((1, 512), F32),
        ((1, 128), jnp.int32),
        ((4, 3, 128, 512), WIRE), ((4, 2, 64, 512), F32), ((4, 2, 64, 512), WIRE),
        ((4, 2, 128, 512), WIRE), ((4, 128, 512), F32),
        ((2, 128, 512), WIRE), ((2, 128, 512), WIRE), ((256, 512), F32), ((256, 128), F32),
        ((2, 8, 8, 128), F32),
        ((512, 512), BF16), ((1024, 512), BF16), ((4, 8, 128), jnp.int32), ((512, 128), F32),
        ((4, 512, 256), F32), ((4, 2, 2, 32, 256), F32), ((4, 2, 2, 64, 256), F32), ((4, 64, 256), F32), ((4, 64, 256), F32),
        ((2, 512, 128), F32), ((4, 128, 1), F32), ((4, 8, 128), F32), ((8, 8, 128), F32),
        ((4, 512, 256), BF16), ((4, 512, 256), BF16),
        ((4, 256, 512), F32), ((4, 128, 512), F32), ((4, 128, 512), GZ_WIRE),
        ((3, 128, 512), GZ_WIRE), ((4, 128, 512), F32), ((3, 128, 512), F32), ((256, 512), F32),
        ((2, 8, 8, 128), F32),
        ((8, 2, 256, 256), BF16), ((4, 1024, 256), BF16), ((1024, 512), BF16),
        ((4, 2, 512, 128), F32), ((4, 512, 128), F32), ((3, 512, 128), WZ_WIRE),
        ((3, 512, 128), WZ_WIRE),
    ]
    outs = (
        shape((1, 128), F32), shape((256, 512), F32), shape((256, 512), F32),
        shape((512, 128), F32),
    )
    made = pl.pallas_call(
        kernel,
        name="step",
        out_shape=tuple(pltpu.VMEM(v.shape, v.dtype) for v in outs),
        in_specs=[pl.BlockSpec(memory_space=pl.ANY)] * 5,
        out_specs=[vmem] * 4,
        scratch_shapes=[pltpu.VMEM(s, t) for s, t in scratch]
        + [pltpu.SemaphoreType.DMA((n,)) for n in (COUNT, COUNT, 8)],
        compiler_params=pltpu.CompilerParams(
            collective_id=0, has_side_effects=True, vmem_limit_bytes=56 * 1024 * 1024
        ),
    )(
        attn_out.reshape(256, 512), residual.reshape(256, 512), o_weight,
        norm_gain.reshape(1, 512), positive.reshape(1, 128),
    )
    loss, rg, ag, wg = pl.pallas_call(
        hand_over,
        name="hand_over",
        out_shape=outs,
        in_specs=[vmem] * 4,
        out_specs=[pl.BlockSpec(memory_space=pl.ANY)] * 4,
        scratch_shapes=[pltpu.SemaphoreType.DMA((4,))],
        compiler_params=pltpu.CompilerParams(vmem_limit_bytes=4 * 1024 * 1024),
    )(*made)
    return (
        loss.reshape(128), rg.reshape(2, 128, 512), ag.reshape(2, 128, 512), wg,
    )


def solution(mesh):
    placed = (P(None, "dp", "mp"), P(None, "dp", "mp"), P("mp", None), P("mp"), P("dp"))
    return jax.shard_map(
        body,
        mesh=mesh,
        in_specs=placed,
        out_specs=(P("dp"), P(None, "dp", "mp"), P(None, "dp", "mp"), P("mp", "dp")),
        check_vma=False,
    )
```

```python
import jax
import jax.numpy as jnp
from jax import lax
from jax.sharding import PartitionSpec as P
from jax.experimental import pallas as pl
from jax.experimental.pallas import tpu as pltpu

LOGIT_SCALE = 50.0
EPS = 1e-06
F32 = jnp.float32
BF16 = jnp.bfloat16
MESH = pl.DeviceIdType.MESH
WIRE = F32
GZ_WIRE = BF16
WZ_WIRE = BF16

STAGES = dict(
    y1=24, z1=2, ss=14, qx=3, ps=3, ax=3, az=3, ac=4, ly=48, lz=4, tx=3, td=7,
    ez=4, ey=24, gc=4, gz=3, gq=3, rr=14, gh=4, gy=24, gx=32, wc=4, wz=3,
)
BASE = {}
COUNT = 0
for _name, _n in STAGES.items():
    BASE[_name] = COUNT
    COUNT += _n


def nt(a, b):
    return lax.dot_general(a, b, (((1,), (1,)), ((), ())), preferred_element_type=F32)


def tn(a, b):
    return lax.dot_general(a, b, (((0,), (0,)), ((), ())), preferred_element_type=F32)


def nn(a, b):
    return lax.dot_general(a, b, (((1,), (0,)), ((), ())), preferred_element_type=F32)


def to_row(col):
    n = col.shape[0]
    return jnp.broadcast_to(col, (n, 128)).T[0:8]


def to_col(row):
    n = row.shape[1]
    return jnp.broadcast_to(row, (128, n)).T[:, 0:1]


def rows(start, size, unit=None):
    return pl.ds(pl.multiple_of(start, unit or size), size)


def kernel(
    a_in, r_in, w_in, gain_in, pos_in,
    loss_ref, rg_ref, ag_ref, wg_ref,
    a_ref, r_ref, w_ref, gain_ref, pos_ref,
    ys, yf, yt, yr, own, zs, zr, sc, inv_s, ssb,
    qx, aa, px, pc, lg, lt, lr, lzs, lzr, pos_s, sums_s, txb, td,
    ea, sa, gap, gcr, gzs, gzr, gqs, gqr, ge, rb,
    gg, gx, ax, tb, tcr, wzs, wzr,
    send, recv, load,
):
    dp = lax.axis_index("dp")
    mp = lax.axis_index("mp")
    core, x, zl = dp % 2, (dp // 2) % 4, dp // 8
    y, zh = mp // 2, mp % 2
    j = mp
    pending = []

    def dev(core=core, x=x, zl=zl, y=y, zh=zh):
        return ((zl * 4 + x) * 2 + core, y * 2 + zh)

    def copy(stage, k, src, dst, to, r=None):
        return pltpu.make_async_remote_copy(
            src_ref=src, dst_ref=dst,
            send_sem=send.at[BASE[stage] + k],
            recv_sem=recv.at[BASE[stage] + (k if r is None else r)],
            device_id=to, device_id_type=MESH,
        )

    def go(*args):
        c = copy(*args)
        c.start()
        pending.append(c)

    def settle(upto):
        while len(settled) < min(upto, len(pending)):
            c = pending[len(settled)]
            c.wait_send()
            settled.append(c)

    settled = []

    def got(stage, k, dst):
        copy(stage, k, dst, dst, dev(core=1 - core)).wait_recv()

    def ring(v, d):
        return (v + d) % 4

    others = [(d, e) for d in (2, 1, 3, 0) for e in (1, 0) if (d, e) != (0, 0)]

    barrier = pltpu.get_barrier_semaphore()
    peers = [dev(y=ring(y, d), zh=(zh + e) % 2) for d, e in others]
    peers += [dev(x=ring(x, d)) for d in (1, 2, 3)]
    peers += [dev(zl=ring(zl, d)) for d in (1, 2, 3)]
    peers += [dev(core=1 - core)]
    for p in peers:
        pl.semaphore_signal(barrier, inc=1, device_id=p, device_id_type=MESH)

    loads = [pltpu.make_async_copy(a_in, a_ref, load.at[0])]
    for k in range(4):
        part = pl.ds(k * 128, 128)
        loads.append(pltpu.make_async_copy(w_in.at[part], w_ref.at[part], load.at[1 + k]))
    loads.append(pltpu.make_async_copy(pos_in, pos_ref, load.at[5]))
    loads.append(pltpu.make_async_copy(gain_in, gain_ref, load.at[6]))
    loads.append(pltpu.make_async_copy(r_in, r_ref, load.at[7]))
    for c in loads:
        c.start()
    for c in loads[:6]:
        c.wait()

    def half(h):
        return pl.ds(h * 128, 128)

    def product(h, yy, er):
        e = (1 - zh) if er == 0 else zh
        return nn(a_ref[half(h), :], w_ref[:, rows(yy * 1024 + e * 512, 512)])

    low, high = pl.ds(0, 64), pl.ds(64, 64)
    right, left = dev(y=ring(y, 1)), dev(y=ring(y, 3))

    def y_products(h):
        for er in (0, 1):
            c = h * 2 + er
            ys[c, 0] = product(h, ring(y, 2), er).astype(WIRE)
            near = product(h, ring(y, 1), er)
            yf[c, 0] = near[0:64]
            ys[c, 1, high, :] = near[64:128].astype(WIRE)
            near = product(h, ring(y, 3), er)
            yf[c, 1] = near[64:128]
            ys[c, 1, low, :] = near[0:64].astype(WIRE)

    def y_send(c):
        go("y1", c * 6 + 0, ys.at[c, 0, low], yt.at[c, 0], right)
        go("y1", c * 6 + 1, ys.at[c, 0, high], yt.at[c, 1], left)
        go("y1", c * 6 + 2, ys.at[c, 1, high], yr.at[c, 0, high], right)
        go("y1", c * 6 + 3, ys.at[c, 1, low], yr.at[c, 1, low], left)

    def y_hop(c):
        got("y1", c * 6 + 0, yt.at[c, 0])
        ys[c, 2, low, :] = (yf[c, 0] + yt[c, 0].astype(F32)).astype(WIRE)
        go("y1", c * 6 + 4, ys.at[c, 2, low], yr.at[c, 0, low], right)
        got("y1", c * 6 + 1, yt.at[c, 1])
        ys[c, 2, high, :] = (yf[c, 1] + yt[c, 1].astype(F32)).astype(WIRE)
        go("y1", c * 6 + 5, ys.at[c, 2, high], yr.at[c, 1, high], left)

    def y_sum(c):
        got("y1", c * 6 + 2, yr.at[c, 0, high])
        got("y1", c * 6 + 3, yr.at[c, 1, low])
        got("y1", c * 6 + 4, yr.at[c, 0, low])
        got("y1", c * 6 + 5, yr.at[c, 1, high])
        return own[c] + yr[c, 0].astype(F32) + yr[c, 1].astype(F32)

    def z_send(h):
        zs[h] = y_sum(h * 2).astype(WIRE)
        go("z1", h, zs.at[h], zr.at[h], dev(zh=1 - zh))

    def squares(h):
        got("z1", h, zr.at[h])
        proj = own[h * 2 + 1] + zr[h].astype(F32)
        scaled = (r_ref[half(h), :].astype(F32) + proj) * gain_ref[...]
        sc[half(h), :] = scaled
        ssb[h, 0] = to_row(jnp.sum(scaled * scaled, axis=1, keepdims=True))
        for d, e in others:
            k = d * 2 + e
            go("ss", h * 7 + k - 1, ssb.at[h, 0], ssb.at[h, k], dev(y=ring(y, d), zh=(zh + e) % 2))

    def embed(h):
        for d, e in others[::-1]:
            k = d * 2 + e
            got("ss", h * 7 + k - 1, ssb.at[h, k])
        total = ssb[h, 0]
        for k in range(1, 8):
            total = total + ssb[h, k]
        inv = to_col(lax.rsqrt(total[0:1] + EPS))
        inv_s[half(h), :] = jnp.broadcast_to(inv, (128, 128))
        return (sc[half(h), :] * inv).astype(BF16)

    y_products(0)
    px[x] = jnp.broadcast_to(pos_ref[...], (8, 128))
    pl.semaphore_wait(barrier, len(peers))
    y_send(0)
    y_products(1)
    y_send(2)
    for d in (2, 1, 3):
        go("ps", d - 1, px.at[x], px.at[x], dev(x=ring(x, d)))
        go("ax", d - 1, a_ref, ax.at[rows(x * 256, 256)], dev(x=ring(x, d)))
    for h in (0, 1):
        for er in (0, 1):
            own[h * 2 + er] = product(h, y, er)
    y_hop(0)
    y_send(1)
    y_hop(2)
    y_send(3)
    ax[rows(x * 256, 256), :] = a_ref[...]

    for c in loads[6:]:
        c.wait()
    z_send(0)
    y_hop(1)
    z_send(1)
    y_hop(3)
    own[1] = y_sum(1)
    squares(0)
    own[3] = y_sum(3)
    squares(1)
    early = len(pending)
    settle(early - 14)
    emb = embed(0)
    q_at = rows(x * 128, 128)
    qx[q_at, :] = emb
    for d in (2, 1, 3):
        go("qx", d - 1, qx.at[q_at], qx.at[q_at], dev(x=ring(x, d)))
    emb = embed(1)
    a_at = rows((zl * 2 + core) * 128, 128)
    aa[a_at, :] = emb
    go("ac", 0, aa.at[a_at], aa.at[a_at], dev(core=1 - core))
    for d in (2, 1, 3):
        go("az", d - 1, aa.at[a_at], aa.at[a_at], dev(zl=ring(zl, d)))
    for d in (1, 3, 2):
        got("ps", d - 1, px.at[ring(x, -d)])
    for xx in range(4):
        pc[pl.ds(xx * 128, 128), :] = jnp.broadcast_to(
            to_col(px[xx].astype(F32)[0:1]), (128, 128)
        )
    for d in (1, 3, 2):
        got("qx", d - 1, qx.at[rows(ring(x, -d) * 128, 128)])

    def block(yy, e):
        return rows((yy * 2 + e) * 64, 64)

    mine, pair = block(y, zh), block(y, 1 - zh)

    def logit_send(t):
        zz = ring(zl, -t)
        if t:
            at = rows((zz * 2 + core) * 128, 128)
            got("az", t - 1, aa.at[at])
            go("ac", t, aa.at[at], aa.at[at], dev(core=1 - core))
        got("ac", t, aa.at[rows((zz * 2 + 1 - core) * 128, 128)])
        lg[t] = nt(qx[...], aa[rows(zz * 256, 256), :])
        for er in (0, 1):
            k = t * 12 + er * 6
            far, after, before = (logit_piece(t, er, d) for d in (2, 1, 3))
            go("ly", k + 0, far.at[top], lt.at[t, er, 0], right)
            go("ly", k + 1, far.at[end], lt.at[t, er, 1], left)
            go("ly", k + 2, after.at[end], lr.at[t, er, 0, end], right)
            go("ly", k + 3, before.at[top], lr.at[t, er, 1, top], left)

    top, end = pl.ds(0, 32), pl.ds(32, 32)

    def logit_piece(t, er, d):
        return lg.at[t, block(ring(y, d), (1 - zh) if er == 0 else zh)]

    def logit_hop(t):
        for er in (0, 1):
            k = t * 12 + er * 6
            after, before = (logit_piece(t, er, d) for d in (1, 3))
            got("ly", k + 0, lt.at[t, er, 0])
            after[top, :] = after[top, :] + lt[t, er, 0]
            go("ly", k + 4, after.at[top], lr.at[t, er, 0, top], right)
            got("ly", k + 1, lt.at[t, er, 1])
            before[end, :] = before[end, :] + lt[t, er, 1]
            go("ly", k + 5, before.at[end], lr.at[t, er, 1, end], left)

    def logit_sum(t, er):
        k = t * 12 + er * 6
        got("ly", k + 2, lr.at[t, er, 0, end])
        got("ly", k + 3, lr.at[t, er, 1, top])
        got("ly", k + 4, lr.at[t, er, 0, top])
        got("ly", k + 5, lr.at[t, er, 1, end])
        return lg[t, pair if er == 0 else mine, :] + lr[t, er, 0] + lr[t, er, 1]

    def logit_pass(t):
        lzs[t] = logit_sum(t, 0)
        go("lz", t, lzs.at[t], lzr.at[t], dev(zh=1 - zh))

    lanes = lax.broadcasted_iota(jnp.int32, (128, 128), 1).astype(F32)

    def hits(t, at, c):
        first = (ring(zl, -t) * 1024 + x * 256 + c * 128).astype(F32)
        mark = pc[at, :] - first
        return lanes[0:mark.shape[0]] == mark

    def logit_done(t):
        part = logit_sum(t, 1)
        got("lz", t, lzr.at[t])
        logits = LOGIT_SCALE * (part + lzr[t])
        ex = jnp.exp(logits)
        ea[t, mine, :] = ex.astype(BF16)
        go("ez", t, ea.at[t, mine], ea.at[t, mine], dev(zh=1 - zh))
        exp_send(t, zh)
        hit = jnp.concatenate([hits(t, mine, 0), hits(t, mine, 1)], axis=1)
        sums_s[t] = jnp.concatenate(
            [
                jnp.sum(ex, axis=1, keepdims=True),
                jnp.sum(jnp.where(hit, logits, 0.0), axis=1, keepdims=True),
            ],
            axis=0,
        )

    def exp_send(t, e):
        part = ea.at[t, block(y, e)]
        go("ey", t * 6 + e, part, part, right)
        go("ey", t * 6 + 2 + e, part, part, left)
        go("ey", t * 6 + 4 + e, part, part, dev(y=ring(y, 2)))

    def exp_pass(t):
        got("ez", t, ea.at[t, pair])
        exp_send(t, 1 - zh)

    logit_send(0)
    logit_send(1)
    logit_hop(0)
    logit_send(3)
    logit_hop(1)
    logit_send(2)
    logit_pass(0)
    logit_hop(3)
    logit_pass(1)
    logit_hop(2)
    settle(early)
    logit_done(0)
    logit_pass(3)
    logit_done(1)
    exp_pass(0)
    logit_pass(2)
    logit_done(3)
    exp_pass(1)
    early = len(pending) - 24
    settle(early)
    logit_done(2)

    txb[0] = to_row(sums_s[0] + sums_s[1] + sums_s[2] + sums_s[3])
    for d in (2, 1, 3):
        go("tx", d - 1, txb.at[0], txb.at[d], dev(x=ring(x, d)))
    exp_pass(3)
    for d in (1, 3, 2):
        got("tx", d - 1, txb.at[d])
    td[j] = txb[0] + txb[1] + txb[2] + txb[3]
    for d, e in others:
        go("td", d * 2 + e - 1, td.at[j], td.at[j], dev(y=ring(y, d), zh=(zh + e) % 2))
    exp_pass(2)

    settle(early + 12)

    for d, e in others[::-1]:
        got("td", d * 2 + e - 1, td.at[ring(y, -d) * 2 + (zh + e) % 2])
    for xx in range(4):
        first, second = td[xx * 2][0:1], td[xx * 2 + 1][0:1]
        total = jnp.concatenate([first[:, 0:64], second[:, 0:64]], axis=1)
        top = jnp.concatenate([first[:, 64:128], second[:, 64:128]], axis=1)
        scale = LOGIT_SCALE / total
        at = pl.ds(xx * 128, 128)
        pos_s[0, at, :] = jnp.broadcast_to(to_col(scale), (128, 128))
        pos_s[1, at, :] = jnp.broadcast_to(
            to_col(-LOGIT_SCALE * ((total - jnp.exp(top)) / total)), (128, 128)
        )

    def score(t):
        for e in (0, 1):
            got("ey", t * 6 + e, ea.at[t, block(ring(y, 3), e)])
            got("ey", t * 6 + 2 + e, ea.at[t, block(ring(y, 1), e)])
            got("ey", t * 6 + 4 + e, ea.at[t, block(ring(y, 2), e)])
        for xx in range(4):
            at = pl.ds(xx * 128, 128)
            for c in (0, 1):
                part = pl.ds(c * 128, 128)
                rest = ea[t, at, part].astype(F32) * pos_s[0, at, :]
                sa[t, at, part] = jnp.where(
                    hits(t, at, c), pos_s[1, at, :], rest
                ).astype(BF16)

    def answers_part(t):
        gap[t] = tn(sa[t], qx[...])
        away = rows((1 - core) * 128, 128)
        go("gc", t, gap.at[t, away], gcr.at[t], dev(core=1 - core))

    def answers_sum(t):
        got("gc", t, gcr.at[t])
        both = gap[t, rows(core * 128, 128), :] + gcr[t]
        if t:
            gzs[t] = both.astype(GZ_WIRE)
            go("gz", t - 1, gzs.at[t], gzr.at[t - 1], dev(zl=ring(zl, -t)))
        else:
            ge[half(1), :] = both

    def queries_part(d):
        part = jnp.zeros((128, 512), F32)
        for t in range(4):
            left = sa[t, rows(ring(x, d) * 128, 128), :]
            part = part + nn(left, aa[rows(ring(zl, -t) * 256, 256), :])
        gqs[d] = part
        if d:
            go("gq", d - 1, gqs.at[d], gqr.at[d - 1], dev(x=ring(x, d)))

    score(2)
    answers_part(2)
    score(3)
    answers_part(3)
    answers_sum(2)
    score(1)
    answers_part(1)
    answers_sum(3)
    score(0)
    queries_part(2)
    answers_sum(1)
    queries_part(1)
    queries_part(3)
    answers_part(0)
    queries_part(0)
    answers_sum(0)

    def radial(h, g):
        at = half(h)
        ge[at, :] = g
        rb[h, 0] = to_row(jnp.sum(g * sc[at, :], axis=1, keepdims=True))
        for d, e in others:
            k = d * 2 + e
            go("rr", h * 7 + k - 1, rb.at[h, 0], rb.at[h, k], dev(y=ring(y, d), zh=(zh + e) % 2))

    def spread(h):
        at = half(h)
        tot = rb[h, 0]
        for d, e in others[::-1]:
            k = d * 2 + e
            got("rr", h * 7 + k - 1, rb.at[h, k])
        for k in range(1, 8):
            tot = tot + rb[h, k]
        rad = to_col(tot[0:1])
        iv = inv_s[at, 0:1]
        out = gain_ref[...] * (iv * ge[at, :] - (iv * iv * iv * rad) * sc[at, :])
        rg_ref[at, :] = out
        for c in (0, 1):
            gg[j, c, at, :] = out[:, c * 256:(c + 1) * 256].astype(BF16)
        for c in (0, 1):
            part = gg.at[j, c, at]
            go("gh", h * 2 + c, part, part, dev(zh=1 - zh))
        near(h, 0)

    def near(h, k):
        e = zh if k == 0 else 1 - zh
        for c in (0, 1):
            part = gg.at[y * 2 + e, c, half(h)]
            if k:
                got("gh", h * 2 + c, part)
            go("gy", h * 12 + k * 6 + c, part, part, right)
            go("gy", h * 12 + k * 6 + 2 + c, part, part, left)
            if straight(h, k):
                go("gy", h * 12 + k * 6 + 4 + c, part, part, dev(y=ring(y, 2)))

    def straight(h, k):
        return h == 1 and k == 1

    def hop(h, k):
        e = zh if k == 0 else 1 - zh
        part = gg.at[ring(y, 3) * 2 + e, 0, half(h)]
        got("gy", h * 12 + k * 6, part)
        go("gy", h * 12 + k * 6 + 4, part, part, right)
        part = gg.at[ring(y, 1) * 2 + e, 1, half(h)]
        got("gy", h * 12 + k * 6 + 3, part)
        go("gy", h * 12 + k * 6 + 5, part, part, left)

    def column_copy(h, t, k, c):
        e = zh if k == 0 else 1 - zh
        xx = e * 2 + c
        d = (xx - x + 4) % 4
        src = gg.at[ring(y, -t) * 2 + e, c, half(h)]
        dst = gx.at[t, rows(x * 256 + h * 128, 128)]
        n = t * 2 + h
        return d, src, dst, copy("gx", (n * 2 + k) * 2 + c, src, dst, dev(x=xx), n * 3 + d - 1)

    def columns(h, t, k):
        arrivals = {0: (), 1: ((1, 1),), 3: ((2, 0),), 2: ((4, 0), (5, 1))}[t]
        if straight(h, k):
            arrivals += {0: (), 1: ((0, 0),), 3: ((3, 1),), 2: ()}[t]
        for n, c in arrivals:
            e = zh if k == 0 else 1 - zh
            got("gy", h * 12 + k * 6 + n, gg.at[ring(y, -t) * 2 + e, c, half(h)])
        for c in (0, 1):
            d, src, dst, remote = column_copy(h, t, k, c)

            @pl.when(d > 0)
            def _():
                remote.start()

            @pl.when(d == 0)
            def _():
                dst[...] = src[...]

    early = len(pending)
    settle(early - 10)
    for d in (1, 3, 2):
        got("gq", d - 1, gqr.at[d - 1])
    radial(0, gqs[0] + gqr[0] + gqr[1] + gqr[2])
    for d in (1, 3, 2):
        got("gz", d - 1, gzr.at[d - 1])
    radial(1, ge[half(1), :] + gzr[0].astype(F32) + gzr[1].astype(F32) + gzr[2].astype(F32))
    spread(0)
    columns(0, 0, 0)
    spread(1)
    columns(1, 0, 0)
    hop(0, 0)
    columns(0, 1, 0)
    columns(0, 3, 0)
    hop(1, 0)
    columns(1, 1, 0)
    columns(1, 3, 0)
    settle(early)
    near(0, 1)
    columns(0, 0, 1)
    columns(0, 2, 0)
    hop(0, 1)
    columns(0, 1, 1)
    columns(0, 3, 1)
    columns(1, 2, 0)
    near(1, 1)
    columns(1, 0, 1)
    columns(0, 2, 1)

    for d in (1, 3, 2):
        got("ax", d - 1, ax.at[rows(ring(x, -d) * 256, 256)])

    def weight_part(t):
        for h in (0, 1):
            for d in (1, 3, 2):
                got("gx", (t * 2 + h) * 3 + d - 1,
                    gx.at[t, rows(ring(x, -d) * 256 + h * 128, 128)])
        part = tn(ax[...], gx[t])
        tb[t, 0] = part[:, 0:128]
        tb[t, 1] = part[:, 128:256]
        go("wc", t, tb.at[t, 1 - core], tcr.at[t], dev(core=1 - core))

    def weight_sum(t):
        got("wc", t, tcr.at[t])
        zz = ring(y, -t)
        d = (zz - zl + 4) % 4
        both = tb[t, core] + tcr[t]

        @pl.when(d > 0)
        def _():
            wzs[d - 1] = both.astype(WZ_WIRE)
            copy("wz", d - 1, wzs.at[d - 1], wzr.at[d - 1], dev(zl=zz)).start()

        @pl.when(d == 0)
        def _():
            wg_ref[...] = both

    columns(1, 1, 1)
    columns(1, 3, 1)
    weight_part(0)
    columns(1, 2, 1)
    weight_sum(0)
    weight_part(1)
    weight_part(3)
    weight_sum(1)
    weight_sum(3)

    weight_part(2)
    weight_sum(2)
    ag_ref[...] = jnp.zeros((256, 512), F32)
    for jj in range(8):
        for c in (0, 1):
            ag_ref[...] += nt(gg[jj, c], w_ref[:, pl.ds(jj * 512 + c * 256, 256)])
    losses = []
    for v in (td[x * 2][0:1], td[x * 2 + 1][0:1]):
        total, top = v[:, 0:64], v[:, 64:128]
        peak = jnp.exp(top)
        losses.append(
            jnp.where(
                total < 4.0 * peak, jnp.log1p((total - peak) / peak), jnp.log(total) - top
            )
        )
    loss_ref[...] = jnp.concatenate(losses, axis=1)
    settle(len(pending))
    for n in range(32):
        d, _, _, remote = column_copy(n // 16, n // 4 % 4, n // 2 % 2, n % 2)

        @pl.when(d > 0)
        def _():
            remote.wait_send()

    for d in (1, 3, 2):
        got("wz", d - 1, wzr.at[d - 1])
    wg_ref[...] += wzr[0].astype(F32) + wzr[1].astype(F32) + wzr[2].astype(F32)
    for d in (1, 2, 3):
        copy("wz", d - 1, wzs.at[d - 1], wzr.at[d - 1], dev(core=1 - core)).wait_send()


def hand_over(*refs):
    copies = [pltpu.make_async_copy(refs[k], refs[4 + k], refs[8].at[k]) for k in range(4)]
    for c in copies:
        c.start()
    for c in copies:
        c.wait()


def body(attn_out, residual, o_weight, norm_gain, positive):
    vmem = pl.BlockSpec(memory_space=pltpu.VMEM)
    shape = jax.ShapeDtypeStruct
    scratch = [
        ((256, 512), BF16), ((256, 512), BF16), ((512, 4096), BF16), ((1, 512), F32),
        ((1, 128), jnp.int32),
        ((4, 3, 128, 512), WIRE), ((4, 2, 64, 512), F32), ((4, 2, 64, 512), WIRE),
        ((4, 2, 128, 512), WIRE), ((4, 128, 512), F32),
        ((2, 128, 512), WIRE), ((2, 128, 512), WIRE), ((256, 512), F32), ((256, 128), F32),
        ((2, 8, 8, 128), F32),
        ((512, 512), BF16), ((1024, 512), BF16), ((4, 8, 128), jnp.int32), ((512, 128), F32),
        ((4, 512, 256), F32), ((4, 2, 2, 32, 256), F32), ((4, 2, 2, 64, 256), F32), ((4, 64, 256), F32), ((4, 64, 256), F32),
        ((2, 512, 128), F32), ((4, 128, 1), F32), ((4, 8, 128), F32), ((8, 8, 128), F32),
        ((4, 512, 256), BF16), ((4, 512, 256), BF16),
        ((4, 256, 512), F32), ((4, 128, 512), F32), ((4, 128, 512), GZ_WIRE),
        ((3, 128, 512), GZ_WIRE), ((4, 128, 512), F32), ((3, 128, 512), F32), ((256, 512), F32),
        ((2, 8, 8, 128), F32),
        ((8, 2, 256, 256), BF16), ((4, 1024, 256), BF16), ((1024, 512), BF16),
        ((4, 2, 512, 128), F32), ((4, 512, 128), F32), ((3, 512, 128), WZ_WIRE),
        ((3, 512, 128), WZ_WIRE),
    ]
    outs = (
        shape((1, 128), F32), shape((256, 512), F32), shape((256, 512), F32),
        shape((512, 128), F32),
    )
    made = pl.pallas_call(
        kernel,
        name="step",
        out_shape=tuple(pltpu.VMEM(v.shape, v.dtype) for v in outs),
        in_specs=[pl.BlockSpec(memory_space=pl.ANY)] * 5,
        out_specs=[vmem] * 4,
        scratch_shapes=[pltpu.VMEM(s, t) for s, t in scratch]
        + [pltpu.SemaphoreType.DMA((n,)) for n in (COUNT, COUNT, 8)],
        compiler_params=pltpu.CompilerParams(
            collective_id=0, has_side_effects=True, vmem_limit_bytes=56 * 1024 * 1024
        ),
    )(
        attn_out.reshape(256, 512), residual.reshape(256, 512), o_weight,
        norm_gain.reshape(1, 512), positive.reshape(1, 128),
    )
    loss, rg, ag, wg = pl.pallas_call(
        hand_over,
        name="hand_over",
        out_shape=outs,
        in_specs=[vmem] * 4,
        out_specs=[pl.BlockSpec(memory_space=pl.ANY)] * 4,
        scratch_shapes=[pltpu.SemaphoreType.DMA((4,))],
        compiler_params=pltpu.CompilerParams(vmem_limit_bytes=4 * 1024 * 1024),
    )(*made)
    return (
        loss.reshape(128), rg.reshape(2, 128, 512), ag.reshape(2, 128, 512), wg,
    )


def solution(mesh):
    placed = (P(None, "dp", "mp"), P(None, "dp", "mp"), P("mp", None), P("mp"), P("dp"))
    return jax.shard_map(
        body,
        mesh=mesh,
        in_specs=placed,
        out_specs=(P("dp"), P(None, "dp", "mp"), P(None, "dp", "mp"), P("mp", "dp")),
        check_vma=False,
    )
```

```python
import jax
import jax.numpy as jnp
from jax import lax
from jax.sharding import PartitionSpec as P
from jax.experimental import pallas as pl
from jax.experimental.pallas import tpu as pltpu

LOGIT_SCALE = 50.0
EPS = 1e-06
F32 = jnp.float32
BF16 = jnp.bfloat16
MESH = pl.DeviceIdType.MESH
WIRE = BF16
GZ_WIRE = BF16
WZ_WIRE = BF16

STAGES = dict(
    y1=24, z1=2, ss=14, qx=3, ps=3, ax=3, az=3, ac=4, ly=48, lz=4, tx=3, td=7,
    ez=4, ey=24, gc=4, gz=3, gq=3, rr=14, gh=4, gy=24, gx=32, wc=4, wz=3,
)
BASE = {}
COUNT = 0
for _name, _n in STAGES.items():
    BASE[_name] = COUNT
    COUNT += _n


def nt(a, b):
    return lax.dot_general(a, b, (((1,), (1,)), ((), ())), preferred_element_type=F32)


def tn(a, b):
    return lax.dot_general(a, b, (((0,), (0,)), ((), ())), preferred_element_type=F32)


def nn(a, b):
    return lax.dot_general(a, b, (((1,), (0,)), ((), ())), preferred_element_type=F32)


def to_row(col):
    n = col.shape[0]
    return jnp.broadcast_to(col, (n, 128)).T[0:8]


def to_col(row):
    n = row.shape[1]
    return jnp.broadcast_to(row, (128, n)).T[:, 0:1]


def rows(start, size, unit=None):
    return pl.ds(pl.multiple_of(start, unit or size), size)


def kernel(
    a_in, r_in, w_in, gain_in, pos_in,
    loss_ref, rg_ref, ag_ref, wg_ref,
    a_ref, r_ref, w_ref, gain_ref, pos_ref,
    ys, yf, yt, yr, own, zs, zr, sc, inv_s, ssb,
    qx, aa, px, pc, lg, lt, lr, lzs, lzr, pos_s, sums_s, txb, td,
    ea, sa, gap, gcr, gzs, gzr, gqs, gqr, ge, rb,
    gg, gx, ax, tb, tcr, wzs, wzr,
    send, recv, load,
):
    dp = lax.axis_index("dp")
    mp = lax.axis_index("mp")
    core, x, zl = dp % 2, (dp // 2) % 4, dp // 8
    y, zh = mp // 2, mp % 2
    j = mp
    pending = []

    def dev(core=core, x=x, zl=zl, y=y, zh=zh):
        return ((zl * 4 + x) * 2 + core, y * 2 + zh)

    def copy(stage, k, src, dst, to, r=None):
        return pltpu.make_async_remote_copy(
            src_ref=src, dst_ref=dst,
            send_sem=send.at[BASE[stage] + k],
            recv_sem=recv.at[BASE[stage] + (k if r is None else r)],
            device_id=to, device_id_type=MESH,
        )

    def go(*args):
        c = copy(*args)
        c.start()
        pending.append(c)

    def settle(upto):
        while len(settled) < min(upto, len(pending)):
            c = pending[len(settled)]
            c.wait_send()
            settled.append(c)

    settled = []

    def got(stage, k, dst):
        copy(stage, k, dst, dst, dev(core=1 - core)).wait_recv()

    def ring(v, d):
        return (v + d) % 4

    others = [(d, e) for d in (2, 1, 3, 0) for e in (1, 0) if (d, e) != (0, 0)]

    barrier = pltpu.get_barrier_semaphore()
    peers = [dev(y=ring(y, d), zh=(zh + e) % 2) for d, e in others]
    peers += [dev(x=ring(x, d)) for d in (1, 2, 3)]
    peers += [dev(zl=ring(zl, d)) for d in (1, 2, 3)]
    peers += [dev(core=1 - core)]
    for p in peers:
        pl.semaphore_signal(barrier, inc=1, device_id=p, device_id_type=MESH)

    loads = [pltpu.make_async_copy(a_in, a_ref, load.at[0])]
    for k in range(4):
        part = pl.ds(k * 128, 128)
        loads.append(pltpu.make_async_copy(w_in.at[part], w_ref.at[part], load.at[1 + k]))
    loads.append(pltpu.make_async_copy(pos_in, pos_ref, load.at[5]))
    loads.append(pltpu.make_async_copy(gain_in, gain_ref, load.at[6]))
    loads.append(pltpu.make_async_copy(r_in, r_ref, load.at[7]))
    for c in loads:
        c.start()
    for c in loads[:6]:
        c.wait()

    def half(h):
        return pl.ds(h * 128, 128)

    def product(h, yy, er):
        e = (1 - zh) if er == 0 else zh
        return nn(a_ref[half(h), :], w_ref[:, rows(yy * 1024 + e * 512, 512)])

    low, high = pl.ds(0, 64), pl.ds(64, 64)
    right, left, opposite = dev(y=ring(y, 1)), dev(y=ring(y, 3)), dev(y=ring(y, 2))

    def y_products(h):
        for er in (0, 1):
            c = h * 2 + er
            ys[c, 0] = product(h, ring(y, 2), er).astype(WIRE)
            near = product(h, ring(y, 1), er)
            yf[c, 0] = near[0:64]
            ys[c, 1, high, :] = near[64:128].astype(WIRE)
            near = product(h, ring(y, 3), er)
            yf[c, 1] = near[64:128]
            ys[c, 1, low, :] = near[0:64].astype(WIRE)

    def y_send(c):
        go("y1", c * 6 + 0, ys.at[c, 0, low], yt.at[c, 0], right)
        go("y1", c * 6 + 1, ys.at[c, 0, high], yt.at[c, 1], left)
        go("y1", c * 6 + 2, ys.at[c, 1, high], yr.at[c, 0, high], right)
        go("y1", c * 6 + 3, ys.at[c, 1, low], yr.at[c, 1, low], left)

    def y_hop(c):
        got("y1", c * 6 + 0, yt.at[c, 0])
        ys[c, 2, low, :] = (yf[c, 0] + yt[c, 0].astype(F32)).astype(WIRE)
        go("y1", c * 6 + 4, ys.at[c, 2, low], yr.at[c, 0, low], right)
        got("y1", c * 6 + 1, yt.at[c, 1])
        ys[c, 2, high, :] = (yf[c, 1] + yt[c, 1].astype(F32)).astype(WIRE)
        go("y1", c * 6 + 5, ys.at[c, 2, high], yr.at[c, 1, high], left)

    def y_sum(c):
        got("y1", c * 6 + 2, yr.at[c, 0, high])
        got("y1", c * 6 + 3, yr.at[c, 1, low])
        got("y1", c * 6 + 4, yr.at[c, 0, low])
        got("y1", c * 6 + 5, yr.at[c, 1, high])
        return own[c] + yr[c, 0].astype(F32) + yr[c, 1].astype(F32)

    def z_send(h):
        zs[h] = y_sum(h * 2).astype(WIRE)
        go("z1", h, zs.at[h], zr.at[h], dev(zh=1 - zh))

    def squares(h):
        got("z1", h, zr.at[h])
        proj = own[h * 2 + 1] + zr[h].astype(F32)
        scaled = (r_ref[half(h), :].astype(F32) + proj) * gain_ref[...]
        sc[half(h), :] = scaled
        ssb[h, 0] = to_row(jnp.sum(scaled * scaled, axis=1, keepdims=True))
        for d, e in others:
            k = d * 2 + e
            go("ss", h * 7 + k - 1, ssb.at[h, 0], ssb.at[h, k], dev(y=ring(y, d), zh=(zh + e) % 2))

    def embed(h):
        for d, e in others[::-1]:
            k = d * 2 + e
            got("ss", h * 7 + k - 1, ssb.at[h, k])
        total = ssb[h, 0]
        for k in range(1, 8):
            total = total + ssb[h, k]
        inv = to_col(lax.rsqrt(total[0:1] + EPS))
        inv_s[half(h), :] = jnp.broadcast_to(inv, (128, 128))
        return (sc[half(h), :] * inv).astype(BF16)

    y_products(0)
    px[x] = jnp.broadcast_to(pos_ref[...], (8, 128))
    pl.semaphore_wait(barrier, len(peers))
    y_send(0)
    y_products(1)
    y_send(2)
    for d in (2, 1, 3):
        go("ps", d - 1, px.at[x], px.at[x], dev(x=ring(x, d)))
        go("ax", d - 1, a_ref, ax.at[rows(x * 256, 256)], dev(x=ring(x, d)))
    for h in (0, 1):
        for er in (0, 1):
            own[h * 2 + er] = product(h, y, er)
    y_hop(0)
    y_send(1)
    y_hop(2)
    y_send(3)
    ax[rows(x * 256, 256), :] = a_ref[...]

    for c in loads[6:]:
        c.wait()
    z_send(0)
    y_hop(1)
    z_send(1)
    y_hop(3)
    own[1] = y_sum(1)
    squares(0)
    own[3] = y_sum(3)
    squares(1)
    early = len(pending)
    settle(early - 14)
    emb = embed(0)
    q_at = rows(x * 128, 128)
    qx[q_at, :] = emb
    for d in (2, 1, 3):
        go("qx", d - 1, qx.at[q_at], qx.at[q_at], dev(x=ring(x, d)))
    emb = embed(1)
    a_at = rows((zl * 2 + core) * 128, 128)
    aa[a_at, :] = emb
    go("ac", 0, aa.at[a_at], aa.at[a_at], dev(core=1 - core))
    for d in (2, 1, 3):
        go("az", d - 1, aa.at[a_at], aa.at[a_at], dev(zl=ring(zl, d)))
    for d in (1, 3, 2):
        got("ps", d - 1, px.at[ring(x, -d)])
    for xx in range(4):
        pc[pl.ds(xx * 128, 128), :] = jnp.broadcast_to(
            to_col(px[xx].astype(F32)[0:1]), (128, 128)
        )
    for d in (1, 3, 2):
        got("qx", d - 1, qx.at[rows(ring(x, -d) * 128, 128)])

    def block(yy, e):
        return rows((yy * 2 + e) * 64, 64)

    mine, pair = block(y, zh), block(y, 1 - zh)

    def logit_send(t):
        zz = ring(zl, -t)
        if t:
            at = rows((zz * 2 + core) * 128, 128)
            got("az", t - 1, aa.at[at])
            go("ac", t, aa.at[at], aa.at[at], dev(core=1 - core))
        got("ac", t, aa.at[rows((zz * 2 + 1 - core) * 128, 128)])
        lg[t] = nt(qx[...], aa[rows(zz * 256, 256), :])
        for er in (0, 1):
            k = t * 12 + er * 6
            far, after, before = (logit_piece(t, er, d) for d in (2, 1, 3))
            last = t == 2
            go("ly", k + 0, far.at[top], lt.at[t, er, 0], opposite if last else right)
            go("ly", k + 1, far.at[end], lt.at[t, er, 1], opposite if last else left)
            if last:
                go("ly", k + 4, after.at[top], lr.at[t, er, 0, top], right)
                go("ly", k + 5, before.at[end], lr.at[t, er, 1, end], left)
            go("ly", k + 2, after.at[end], lr.at[t, er, 0, end], right)
            go("ly", k + 3, before.at[top], lr.at[t, er, 1, top], left)

    top, end = pl.ds(0, 32), pl.ds(32, 32)

    def logit_piece(t, er, d):
        return lg.at[t, block(ring(y, d), (1 - zh) if er == 0 else zh)]

    def logit_hop(t):
        for er in (0, 1):
            k = t * 12 + er * 6
            after, before = (logit_piece(t, er, d) for d in (1, 3))
            got("ly", k + 0, lt.at[t, er, 0])
            after[top, :] = after[top, :] + lt[t, er, 0]
            go("ly", k + 4, after.at[top], lr.at[t, er, 0, top], right)
            got("ly", k + 1, lt.at[t, er, 1])
            before[end, :] = before[end, :] + lt[t, er, 1]
            go("ly", k + 5, before.at[end], lr.at[t, er, 1, end], left)

    def logit_sum(t, er):
        k = t * 12 + er * 6
        got("ly", k + 2, lr.at[t, er, 0, end])
        got("ly", k + 3, lr.at[t, er, 1, top])
        got("ly", k + 4, lr.at[t, er, 0, top])
        got("ly", k + 5, lr.at[t, er, 1, end])
        part = lg[t, pair if er == 0 else mine, :] + lr[t, er, 0] + lr[t, er, 1]
        if t == 2:
            got("ly", k + 0, lt.at[t, er, 0])
            got("ly", k + 1, lt.at[t, er, 1])
            part = part + jnp.concatenate([lt[t, er, 0], lt[t, er, 1]], axis=0)
        return part

    def logit_pass(t):
        lzs[t] = logit_sum(t, 0)
        go("lz", t, lzs.at[t], lzr.at[t], dev(zh=1 - zh))

    lanes = lax.broadcasted_iota(jnp.int32, (128, 128), 1).astype(F32)

    def hits(t, at, c):
        first = (ring(zl, -t) * 1024 + x * 256 + c * 128).astype(F32)
        mark = pc[at, :] - first
        return lanes[0:mark.shape[0]] == mark

    def logit_done(t):
        part = logit_sum(t, 1)
        got("lz", t, lzr.at[t])
        logits = LOGIT_SCALE * (part + lzr[t])
        ex = jnp.exp(logits)
        ea[t, mine, :] = ex.astype(BF16)
        go("ez", t, ea.at[t, mine], ea.at[t, mine], dev(zh=1 - zh))
        exp_send(t, zh)
        hit = jnp.concatenate([hits(t, mine, 0), hits(t, mine, 1)], axis=1)
        sums_s[t] = jnp.concatenate(
            [
                jnp.sum(ex, axis=1, keepdims=True),
                jnp.sum(jnp.where(hit, logits, 0.0), axis=1, keepdims=True),
            ],
            axis=0,
        )

    def exp_send(t, e):
        part = ea.at[t, block(y, e)]
        go("ey", t * 6 + e, part, part, right)
        go("ey", t * 6 + 2 + e, part, part, left)
        go("ey", t * 6 + 4 + e, part, part, dev(y=ring(y, 2)))

    def exp_pass(t):
        got("ez", t, ea.at[t, pair])
        exp_send(t, 1 - zh)

    logit_send(0)
    logit_send(1)
    logit_hop(0)
    logit_send(3)
    logit_hop(1)
    logit_send(2)
    logit_pass(0)
    logit_hop(3)
    logit_pass(1)
    settle(early)
    logit_done(0)
    logit_pass(3)
    logit_done(1)
    exp_pass(0)
    logit_pass(2)
    logit_done(3)
    exp_pass(1)
    early = len(pending) - 24
    settle(early)
    logit_done(2)

    txb[0] = to_row(sums_s[0] + sums_s[1] + sums_s[2] + sums_s[3])
    for d in (2, 1, 3):
        go("tx", d - 1, txb.at[0], txb.at[d], dev(x=ring(x, d)))
    exp_pass(3)
    for d in (1, 3, 2):
        got("tx", d - 1, txb.at[d])
    td[j] = txb[0] + txb[1] + txb[2] + txb[3]
    for d, e in others:
        go("td", d * 2 + e - 1, td.at[j], td.at[j], dev(y=ring(y, d), zh=(zh + e) % 2))
    exp_pass(2)

    settle(early + 12)

    for d, e in others[::-1]:
        got("td", d * 2 + e - 1, td.at[ring(y, -d) * 2 + (zh + e) % 2])
    for xx in range(4):
        first, second = td[xx * 2][0:1], td[xx * 2 + 1][0:1]
        total = jnp.concatenate([first[:, 0:64], second[:, 0:64]], axis=1)
        top = jnp.concatenate([first[:, 64:128], second[:, 64:128]], axis=1)
        scale = LOGIT_SCALE / total
        at = pl.ds(xx * 128, 128)
        pos_s[0, at, :] = jnp.broadcast_to(to_col(scale), (128, 128))
        pos_s[1, at, :] = jnp.broadcast_to(
            to_col(-LOGIT_SCALE * ((total - jnp.exp(top)) / total)), (128, 128)
        )

    def score(t):
        for e in (0, 1):
            got("ey", t * 6 + e, ea.at[t, block(ring(y, 3), e)])
            got("ey", t * 6 + 2 + e, ea.at[t, block(ring(y, 1), e)])
            got("ey", t * 6 + 4 + e, ea.at[t, block(ring(y, 2), e)])
        for xx in range(4):
            at = pl.ds(xx * 128, 128)
            for c in (0, 1):
                part = pl.ds(c * 128, 128)
                rest = ea[t, at, part].astype(F32) * pos_s[0, at, :]
                sa[t, at, part] = jnp.where(
                    hits(t, at, c), pos_s[1, at, :], rest
                ).astype(BF16)

    def answers_part(t):
        gap[t] = tn(sa[t], qx[...])
        away = rows((1 - core) * 128, 128)
        go("gc", t, gap.at[t, away], gcr.at[t], dev(core=1 - core))

    def answers_sum(t):
        got("gc", t, gcr.at[t])
        both = gap[t, rows(core * 128, 128), :] + gcr[t]
        if t:
            gzs[t] = both.astype(GZ_WIRE)
            go("gz", t - 1, gzs.at[t], gzr.at[t - 1], dev(zl=ring(zl, -t)))
        else:
            ge[half(1), :] = both

    def queries_part(d):
        part = jnp.zeros((128, 512), F32)
        for t in range(4):
            left = sa[t, rows(ring(x, d) * 128, 128), :]
            part = part + nn(left, aa[rows(ring(zl, -t) * 256, 256), :])
        gqs[d] = part
        if d:
            go("gq", d - 1, gqs.at[d], gqr.at[d - 1], dev(x=ring(x, d)))

    score(2)
    answers_part(2)
    score(3)
    answers_part(3)
    answers_sum(2)
    score(1)
    answers_part(1)
    answers_sum(3)
    score(0)
    queries_part(2)
    answers_sum(1)
    queries_part(1)
    queries_part(3)
    answers_part(0)
    queries_part(0)
    answers_sum(0)

    def radial(h, g):
        at = half(h)
        ge[at, :] = g
        rb[h, 0] = to_row(jnp.sum(g * sc[at, :], axis=1, keepdims=True))
        for d, e in others:
            k = d * 2 + e
            go("rr", h * 7 + k - 1, rb.at[h, 0], rb.at[h, k], dev(y=ring(y, d), zh=(zh + e) % 2))

    def spread(h):
        at = half(h)
        tot = rb[h, 0]
        for d, e in others[::-1]:
            k = d * 2 + e
            got("rr", h * 7 + k - 1, rb.at[h, k])
        for k in range(1, 8):
            tot = tot + rb[h, k]
        rad = to_col(tot[0:1])
        iv = inv_s[at, 0:1]
        out = gain_ref[...] * (iv * ge[at, :] - (iv * iv * iv * rad) * sc[at, :])
        rg_ref[at, :] = out
        for c in (0, 1):
            gg[j, c, at, :] = out[:, c * 256:(c + 1) * 256].astype(BF16)
        for c in (0, 1):
            part = gg.at[j, c, at]
            go("gh", h * 2 + c, part, part, dev(zh=1 - zh))
        near(h, 0)

    def near(h, k):
        e = zh if k == 0 else 1 - zh
        for c in (0, 1):
            part = gg.at[y * 2 + e, c, half(h)]
            if k:
                got("gh", h * 2 + c, part)
            go("gy", h * 12 + k * 6 + c, part, part, right)
            go("gy", h * 12 + k * 6 + 2 + c, part, part, left)
            if straight(h, k):
                go("gy", h * 12 + k * 6 + 4 + c, part, part, dev(y=ring(y, 2)))

    def straight(h, k):
        return h == 1 and k == 1

    def hop(h, k):
        e = zh if k == 0 else 1 - zh
        part = gg.at[ring(y, 3) * 2 + e, 0, half(h)]
        got("gy", h * 12 + k * 6, part)
        go("gy", h * 12 + k * 6 + 4, part, part, right)
        part = gg.at[ring(y, 1) * 2 + e, 1, half(h)]
        got("gy", h * 12 + k * 6 + 3, part)
        go("gy", h * 12 + k * 6 + 5, part, part, left)

    def column_copy(h, t, k, c):
        e = zh if k == 0 else 1 - zh
        xx = e * 2 + c
        d = (xx - x + 4) % 4
        src = gg.at[ring(y, -t) * 2 + e, c, half(h)]
        dst = gx.at[t, rows(x * 256 + h * 128, 128)]
        n = t * 2 + h
        return d, src, dst, copy("gx", (n * 2 + k) * 2 + c, src, dst, dev(x=xx), n * 3 + d - 1)

    def columns(h, t, k):
        arrivals = {0: (), 1: ((1, 1),), 3: ((2, 0),), 2: ((4, 0), (5, 1))}[t]
        if straight(h, k):
            arrivals += {0: (), 1: ((0, 0),), 3: ((3, 1),), 2: ()}[t]
        for n, c in arrivals:
            e = zh if k == 0 else 1 - zh
            got("gy", h * 12 + k * 6 + n, gg.at[ring(y, -t) * 2 + e, c, half(h)])
        for c in (0, 1):
            d, src, dst, remote = column_copy(h, t, k, c)

            @pl.when(d > 0)
            def _():
                remote.start()

            @pl.when(d == 0)
            def _():
                dst[...] = src[...]

    early = len(pending)
    settle(early - 10)
    for d in (1, 3, 2):
        got("gq", d - 1, gqr.at[d - 1])
    radial(0, gqs[0] + gqr[0] + gqr[1] + gqr[2])
    for d in (1, 3, 2):
        got("gz", d - 1, gzr.at[d - 1])
    radial(1, ge[half(1), :] + gzr[0].astype(F32) + gzr[1].astype(F32) + gzr[2].astype(F32))
    spread(0)
    columns(0, 0, 0)
    spread(1)
    columns(1, 0, 0)
    hop(0, 0)
    columns(0, 1, 0)
    columns(0, 3, 0)
    hop(1, 0)
    columns(1, 1, 0)
    columns(1, 3, 0)
    settle(early)
    near(0, 1)
    columns(0, 0, 1)
    columns(0, 2, 0)
    hop(0, 1)
    columns(0, 1, 1)
    columns(0, 3, 1)
    columns(1, 2, 0)
    near(1, 1)
    columns(1, 0, 1)
    columns(0, 2, 1)

    for d in (1, 3, 2):
        got("ax", d - 1, ax.at[rows(ring(x, -d) * 256, 256)])

    def weight_part(t):
        for h in (0, 1):
            for d in (1, 3, 2):
                got("gx", (t * 2 + h) * 3 + d - 1,
                    gx.at[t, rows(ring(x, -d) * 256 + h * 128, 128)])
        part = tn(ax[...], gx[t])
        tb[t, 0] = part[:, 0:128]
        tb[t, 1] = part[:, 128:256]
        go("wc", t, tb.at[t, 1 - core], tcr.at[t], dev(core=1 - core))

    def weight_sum(t):
        got("wc", t, tcr.at[t])
        zz = ring(y, -t)
        d = (zz - zl + 4) % 4
        both = tb[t, core] + tcr[t]

        @pl.when(d > 0)
        def _():
            wzs[d - 1] = both.astype(WZ_WIRE)
            copy("wz", d - 1, wzs.at[d - 1], wzr.at[d - 1], dev(zl=zz)).start()

        @pl.when(d == 0)
        def _():
            wg_ref[...] = both

    columns(1, 1, 1)
    columns(1, 3, 1)
    weight_part(0)
    columns(1, 2, 1)
    weight_sum(0)
    weight_part(1)
    weight_part(3)
    weight_sum(1)
    weight_sum(3)

    weight_part(2)
    weight_sum(2)
    ag_ref[...] = jnp.zeros((256, 512), F32)
    for jj in range(8):
        for c in (0, 1):
            ag_ref[...] += nt(gg[jj, c], w_ref[:, pl.ds(jj * 512 + c * 256, 256)])
    losses = []
    for v in (td[x * 2][0:1], td[x * 2 + 1][0:1]):
        total, top = v[:, 0:64], v[:, 64:128]
        peak = jnp.exp(top)
        losses.append(
            jnp.where(
                total < 4.0 * peak, jnp.log1p((total - peak) / peak), jnp.log(total) - top
            )
        )
    loss_ref[...] = jnp.concatenate(losses, axis=1)
    settle(len(pending))
    for n in range(32):
        d, _, _, remote = column_copy(n // 16, n // 4 % 4, n // 2 % 2, n % 2)

        @pl.when(d > 0)
        def _():
            remote.wait_send()

    for d in (1, 3, 2):
        got("wz", d - 1, wzr.at[d - 1])
    wg_ref[...] += wzr[0].astype(F32) + wzr[1].astype(F32) + wzr[2].astype(F32)
    for d in (1, 2, 3):
        copy("wz", d - 1, wzs.at[d - 1], wzr.at[d - 1], dev(core=1 - core)).wait_send()


def hand_over(*refs):
    copies = [pltpu.make_async_copy(refs[k], refs[4 + k], refs[8].at[k]) for k in range(4)]
    for c in copies:
        c.start()
    for c in copies:
        c.wait()


def body(attn_out, residual, o_weight, norm_gain, positive):
    vmem = pl.BlockSpec(memory_space=pltpu.VMEM)
    shape = jax.ShapeDtypeStruct
    scratch = [
        ((256, 512), BF16), ((256, 512), BF16), ((512, 4096), BF16), ((1, 512), F32),
        ((1, 128), jnp.int32),
        ((4, 3, 128, 512), WIRE), ((4, 2, 64, 512), F32), ((4, 2, 64, 512), WIRE),
        ((4, 2, 128, 512), WIRE), ((4, 128, 512), F32),
        ((2, 128, 512), WIRE), ((2, 128, 512), WIRE), ((256, 512), F32), ((256, 128), F32),
        ((2, 8, 8, 128), F32),
        ((512, 512), BF16), ((1024, 512), BF16), ((4, 8, 128), jnp.int32), ((512, 128), F32),
        ((4, 512, 256), F32), ((4, 2, 2, 32, 256), F32), ((4, 2, 2, 64, 256), F32), ((4, 64, 256), F32), ((4, 64, 256), F32),
        ((2, 512, 128), F32), ((4, 128, 1), F32), ((4, 8, 128), F32), ((8, 8, 128), F32),
        ((4, 512, 256), BF16), ((4, 512, 256), BF16),
        ((4, 256, 512), F32), ((4, 128, 512), F32), ((4, 128, 512), GZ_WIRE),
        ((3, 128, 512), GZ_WIRE), ((4, 128, 512), F32), ((3, 128, 512), F32), ((256, 512), F32),
        ((2, 8, 8, 128), F32),
        ((8, 2, 256, 256), BF16), ((4, 1024, 256), BF16), ((1024, 512), BF16),
        ((4, 2, 512, 128), F32), ((4, 512, 128), F32), ((3, 512, 128), WZ_WIRE),
        ((3, 512, 128), WZ_WIRE),
    ]
    outs = (
        shape((1, 128), F32), shape((256, 512), F32), shape((256, 512), F32),
        shape((512, 128), F32),
    )
    made = pl.pallas_call(
        kernel,
        name="step",
        out_shape=tuple(pltpu.VMEM(v.shape, v.dtype) for v in outs),
        in_specs=[pl.BlockSpec(memory_space=pl.ANY)] * 5,
        out_specs=[vmem] * 4,
        scratch_shapes=[pltpu.VMEM(s, t) for s, t in scratch]
        + [pltpu.SemaphoreType.DMA((n,)) for n in (COUNT, COUNT, 8)],
        compiler_params=pltpu.CompilerParams(
            collective_id=0, has_side_effects=True, vmem_limit_bytes=56 * 1024 * 1024
        ),
    )(
        attn_out.reshape(256, 512), residual.reshape(256, 512), o_weight,
        norm_gain.reshape(1, 512), positive.reshape(1, 128),
    )
    loss, rg, ag, wg = pl.pallas_call(
        hand_over,
        name="hand_over",
        out_shape=outs,
        in_specs=[vmem] * 4,
        out_specs=[pl.BlockSpec(memory_space=pl.ANY)] * 4,
        scratch_shapes=[pltpu.SemaphoreType.DMA((4,))],
        compiler_params=pltpu.CompilerParams(vmem_limit_bytes=4 * 1024 * 1024),
    )(*made)
    return (
        loss.reshape(128), rg.reshape(2, 128, 512), ag.reshape(2, 128, 512), wg,
    )


def solution(mesh):
    placed = (P(None, "dp", "mp"), P(None, "dp", "mp"), P("mp", None), P("mp"), P("dp"))
    return jax.shard_map(
        body,
        mesh=mesh,
        in_specs=placed,
        out_specs=(P("dp"), P(None, "dp", "mp"), P(None, "dp", "mp"), P("mp", "dp")),
        check_vma=False,
    )
```

```python
import jax
import jax.numpy as jnp
from jax import lax
from jax.sharding import PartitionSpec as P
from jax.experimental import pallas as pl
from jax.experimental.pallas import tpu as pltpu

LOGIT_SCALE = 50.0
EPS = 1e-06
F32 = jnp.float32
BF16 = jnp.bfloat16
MESH = pl.DeviceIdType.MESH
WIRE = BF16
GZ_WIRE = BF16
WZ_WIRE = BF16

STAGES = dict(
    y1=24, z1=2, ss=14, qx=3, ps=3, ax=3, az=3, ac=4, ly=48, lz=4, tx=3, td=7,
    ez=4, ey=24, gc=4, gz=3, gq=3, rr=14, gh=4, gy=24, gx=32, wc=4, wz=3,
)
BASE = {}
COUNT = 0
for _name, _n in STAGES.items():
    BASE[_name] = COUNT
    COUNT += _n


def nt(a, b):
    return lax.dot_general(a, b, (((1,), (1,)), ((), ())), preferred_element_type=F32)


def tn(a, b):
    return lax.dot_general(a, b, (((0,), (0,)), ((), ())), preferred_element_type=F32)


def nn(a, b):
    return lax.dot_general(a, b, (((1,), (0,)), ((), ())), preferred_element_type=F32)


def to_row(col):
    n = col.shape[0]
    return jnp.broadcast_to(col, (n, 128)).T[0:8]


def to_col(row):
    n = row.shape[1]
    return jnp.broadcast_to(row, (128, n)).T[:, 0:1]


def rows(start, size, unit=None):
    return pl.ds(pl.multiple_of(start, unit or size), size)


def kernel(
    a_in, r_in, w_in, gain_in, pos_in,
    loss_ref, rg_ref, ag_ref, wg_ref,
    a_ref, r_ref, w_ref, gain_ref, pos_ref,
    ys, yf, yt, yr, own, zs, zr, sc, inv_s, ssb,
    qx, aa, px, pc, lg, lt, lr, lzs, lzr, pos_s, sums_s, txb, td,
    ea, sa, gap, gcr, gzs, gzr, gqs, gqr, ge, rb,
    gg, gx, ax, tb, tcr, wzs, wzr,
    send, recv, load,
):
    dp = lax.axis_index("dp")
    mp = lax.axis_index("mp")
    core, x, zl = dp % 2, (dp // 2) % 4, dp // 8
    y, zh = mp // 2, mp % 2
    j = mp
    pending = []

    def dev(core=core, x=x, zl=zl, y=y, zh=zh):
        return ((zl * 4 + x) * 2 + core, y * 2 + zh)

    def copy(stage, k, src, dst, to, r=None):
        return pltpu.make_async_remote_copy(
            src_ref=src, dst_ref=dst,
            send_sem=send.at[BASE[stage] + k],
            recv_sem=recv.at[BASE[stage] + (k if r is None else r)],
            device_id=to, device_id_type=MESH,
        )

    def go(*args):
        c = copy(*args)
        c.start()
        pending.append(c)

    def settle(upto):
        while len(settled) < min(upto, len(pending)):
            c = pending[len(settled)]
            c.wait_send()
            settled.append(c)

    settled = []

    def got(stage, k, dst):
        copy(stage, k, dst, dst, dev(core=1 - core)).wait_recv()

    def ring(v, d):
        return (v + d) % 4

    others = [(d, e) for d in (2, 1, 3, 0) for e in (1, 0) if (d, e) != (0, 0)]

    barrier = pltpu.get_barrier_semaphore()
    peers = [dev(y=ring(y, d), zh=(zh + e) % 2) for d, e in others]
    peers += [dev(x=ring(x, d)) for d in (1, 2, 3)]
    peers += [dev(zl=ring(zl, d)) for d in (1, 2, 3)]
    peers += [dev(core=1 - core)]
    for p in peers:
        pl.semaphore_signal(barrier, inc=1, device_id=p, device_id_type=MESH)

    loads = [pltpu.make_async_copy(a_in, a_ref, load.at[0])]
    for k in range(4):
        part = pl.ds(k * 128, 128)
        loads.append(pltpu.make_async_copy(w_in.at[part], w_ref.at[part], load.at[1 + k]))
    loads.append(pltpu.make_async_copy(pos_in, pos_ref, load.at[5]))
    loads.append(pltpu.make_async_copy(gain_in, gain_ref, load.at[6]))
    loads.append(pltpu.make_async_copy(r_in, r_ref, load.at[7]))
    for c in loads:
        c.start()
    for c in loads[:6]:
        c.wait()

    def half(h):
        return pl.ds(h * 128, 128)

    def product(h, yy, er):
        e = (1 - zh) if er == 0 else zh
        return nn(a_ref[half(h), :], w_ref[:, rows(yy * 1024 + e * 512, 512)])

    low, high = pl.ds(0, 64), pl.ds(64, 64)
    right, left, opposite = dev(y=ring(y, 1)), dev(y=ring(y, 3)), dev(y=ring(y, 2))

    def y_products(h):
        for er in (0, 1):
            c = h * 2 + er
            ys[c, 0] = product(h, ring(y, 2), er).astype(WIRE)
            near = product(h, ring(y, 1), er)
            yf[c, 0] = near[0:64]
            ys[c, 1, high, :] = near[64:128].astype(WIRE)
            near = product(h, ring(y, 3), er)
            yf[c, 1] = near[64:128]
            ys[c, 1, low, :] = near[0:64].astype(WIRE)

    def y_send(c):
        go("y1", c * 6 + 0, ys.at[c, 0, low], yt.at[c, 0], right)
        go("y1", c * 6 + 1, ys.at[c, 0, high], yt.at[c, 1], left)
        go("y1", c * 6 + 2, ys.at[c, 1, high], yr.at[c, 0, high], right)
        go("y1", c * 6 + 3, ys.at[c, 1, low], yr.at[c, 1, low], left)

    def y_hop(c):
        got("y1", c * 6 + 0, yt.at[c, 0])
        ys[c, 2, low, :] = (yf[c, 0] + yt[c, 0].astype(F32)).astype(WIRE)
        go("y1", c * 6 + 4, ys.at[c, 2, low], yr.at[c, 0, low], right)
        got("y1", c * 6 + 1, yt.at[c, 1])
        ys[c, 2, high, :] = (yf[c, 1] + yt[c, 1].astype(F32)).astype(WIRE)
        go("y1", c * 6 + 5, ys.at[c, 2, high], yr.at[c, 1, high], left)

    def y_sum(c):
        got("y1", c * 6 + 2, yr.at[c, 0, high])
        got("y1", c * 6 + 3, yr.at[c, 1, low])
        got("y1", c * 6 + 4, yr.at[c, 0, low])
        got("y1", c * 6 + 5, yr.at[c, 1, high])
        return own[c] + yr[c, 0].astype(F32) + yr[c, 1].astype(F32)

    def z_send(h):
        zs[h] = y_sum(h * 2).astype(WIRE)
        go("z1", h, zs.at[h], zr.at[h], dev(zh=1 - zh))

    def squares(h):
        got("z1", h, zr.at[h])
        proj = own[h * 2 + 1] + zr[h].astype(F32)
        scaled = (r_ref[half(h), :].astype(F32) + proj) * gain_ref[...]
        sc[half(h), :] = scaled
        ssb[h, 0] = to_row(jnp.sum(scaled * scaled, axis=1, keepdims=True))
        for d, e in others:
            k = d * 2 + e
            go("ss", h * 7 + k - 1, ssb.at[h, 0], ssb.at[h, k], dev(y=ring(y, d), zh=(zh + e) % 2))

    def embed(h):
        for d, e in others[::-1]:
            k = d * 2 + e
            got("ss", h * 7 + k - 1, ssb.at[h, k])
        total = ssb[h, 0]
        for k in range(1, 8):
            total = total + ssb[h, k]
        inv = to_col(lax.rsqrt(total[0:1] + EPS))
        inv_s[half(h), :] = jnp.broadcast_to(inv, (128, 128))
        return (sc[half(h), :] * inv).astype(BF16)

    y_products(0)
    px[x] = jnp.broadcast_to(pos_ref[...], (8, 128))
    pl.semaphore_wait(barrier, len(peers))
    y_send(0)
    y_products(1)
    y_send(2)
    for d in (2, 1, 3):
        go("ps", d - 1, px.at[x], px.at[x], dev(x=ring(x, d)))
        go("ax", d - 1, a_ref, ax.at[rows(x * 256, 256)], dev(x=ring(x, d)))
    for h in (0, 1):
        for er in (0, 1):
            own[h * 2 + er] = product(h, y, er)
    y_hop(0)
    y_send(1)
    y_hop(2)
    y_send(3)
    ax[rows(x * 256, 256), :] = a_ref[...]

    for c in loads[6:]:
        c.wait()
    z_send(0)
    y_hop(1)
    z_send(1)
    y_hop(3)
    own[1] = y_sum(1)
    squares(0)
    own[3] = y_sum(3)
    squares(1)
    early = len(pending)
    settle(early - 14)
    emb = embed(0)
    q_at = rows(x * 128, 128)
    qx[q_at, :] = emb
    for d in (2, 1, 3):
        go("qx", d - 1, qx.at[q_at], qx.at[q_at], dev(x=ring(x, d)))
    emb = embed(1)
    a_at = rows((zl * 2 + core) * 128, 128)
    aa[a_at, :] = emb
    go("ac", 0, aa.at[a_at], aa.at[a_at], dev(core=1 - core))
    for d in (2, 1, 3):
        go("az", d - 1, aa.at[a_at], aa.at[a_at], dev(zl=ring(zl, d)))
    for d in (1, 3, 2):
        got("ps", d - 1, px.at[ring(x, -d)])
    for xx in range(4):
        pc[pl.ds(xx * 128, 128), :] = jnp.broadcast_to(
            to_col(px[xx].astype(F32)[0:1]), (128, 128)
        )
    for d in (1, 3, 2):
        got("qx", d - 1, qx.at[rows(ring(x, -d) * 128, 128)])

    def block(yy, e):
        return rows((yy * 2 + e) * 64, 64)

    mine, pair = block(y, zh), block(y, 1 - zh)

    def logit_send(t):
        zz = ring(zl, -t)
        if t:
            at = rows((zz * 2 + core) * 128, 128)
            got("az", t - 1, aa.at[at])
            go("ac", t, aa.at[at], aa.at[at], dev(core=1 - core))
        got("ac", t, aa.at[rows((zz * 2 + 1 - core) * 128, 128)])
        lg[t] = nt(qx[...], aa[rows(zz * 256, 256), :])
        for er in (0, 1):
            k = t * 12 + er * 6
            far, after, before = (logit_piece(t, er, d) for d in (2, 1, 3))
            last = t == 2
            go("ly", k + 0, far.at[top], lt.at[t, er, 0], opposite if last else right)
            go("ly", k + 1, far.at[end], lt.at[t, er, 1], opposite if last else left)
            if last:
                go("ly", k + 4, after.at[top], lr.at[t, er, 0, top], right)
                go("ly", k + 5, before.at[end], lr.at[t, er, 1, end], left)
            go("ly", k + 2, after.at[end], lr.at[t, er, 0, end], right)
            go("ly", k + 3, before.at[top], lr.at[t, er, 1, top], left)

    top, end = pl.ds(0, 32), pl.ds(32, 32)

    def logit_piece(t, er, d):
        return lg.at[t, block(ring(y, d), (1 - zh) if er == 0 else zh)]

    def logit_hop(t):
        for er in (0, 1):
            k = t * 12 + er * 6
            after, before = (logit_piece(t, er, d) for d in (1, 3))
            got("ly", k + 0, lt.at[t, er, 0])
            after[top, :] = after[top, :] + lt[t, er, 0]
            go("ly", k + 4, after.at[top], lr.at[t, er, 0, top], right)
            got("ly", k + 1, lt.at[t, er, 1])
            before[end, :] = before[end, :] + lt[t, er, 1]
            go("ly", k + 5, before.at[end], lr.at[t, er, 1, end], left)

    def logit_sum(t, er):
        k = t * 12 + er * 6
        got("ly", k + 2, lr.at[t, er, 0, end])
        got("ly", k + 3, lr.at[t, er, 1, top])
        got("ly", k + 4, lr.at[t, er, 0, top])
        got("ly", k + 5, lr.at[t, er, 1, end])
        part = lg[t, pair if er == 0 else mine, :] + lr[t, er, 0] + lr[t, er, 1]
        if t == 2:
            got("ly", k + 0, lt.at[t, er, 0])
            got("ly", k + 1, lt.at[t, er, 1])
            part = part + jnp.concatenate([lt[t, er, 0], lt[t, er, 1]], axis=0)
        return part

    def logit_pass(t):
        lzs[t] = logit_sum(t, 0)
        go("lz", t, lzs.at[t], lzr.at[t], dev(zh=1 - zh))

    lanes = lax.broadcasted_iota(jnp.int32, (128, 128), 1).astype(F32)

    def hits(t, at, c):
        first = (ring(zl, -t) * 1024 + x * 256 + c * 128).astype(F32)
        mark = pc[at, :] - first
        return lanes[0:mark.shape[0]] == mark

    def logit_done(t):
        part = logit_sum(t, 1)
        got("lz", t, lzr.at[t])
        logits = LOGIT_SCALE * (part + lzr[t])
        ex = jnp.exp(logits)
        ea[t, mine, :] = ex.astype(BF16)
        go("ez", t, ea.at[t, mine], ea.at[t, mine], dev(zh=1 - zh))
        if t != 2:
            exp_send(t, zh)
        hit = jnp.concatenate([hits(t, mine, 0), hits(t, mine, 1)], axis=1)
        sums_s[t] = jnp.concatenate(
            [
                jnp.sum(ex, axis=1, keepdims=True),
                jnp.sum(jnp.where(hit, logits, 0.0), axis=1, keepdims=True),
            ],
            axis=0,
        )

    def exp_send(t, e):
        part = ea.at[t, block(y, e)]
        go("ey", t * 6 + e, part, part, right)
        go("ey", t * 6 + 2 + e, part, part, left)
        go("ey", t * 6 + 4 + e, part, part, dev(y=ring(y, 2)))

    def exp_pass(t):
        got("ez", t, ea.at[t, pair])
        exp_send(t, 1 - zh)

    logit_send(0)
    logit_send(1)
    logit_hop(0)
    logit_send(3)
    logit_hop(1)
    logit_send(2)
    logit_pass(0)
    logit_hop(3)
    logit_pass(1)
    settle(early)
    logit_done(0)
    logit_pass(3)
    logit_done(1)
    exp_pass(0)
    logit_pass(2)
    logit_done(3)
    exp_pass(1)
    early = len(pending) - 24
    settle(early)
    logit_done(2)

    txb[0] = to_row(sums_s[0] + sums_s[1] + sums_s[2] + sums_s[3])
    for d in (2, 1, 3):
        go("tx", d - 1, txb.at[0], txb.at[d], dev(x=ring(x, d)))
    exp_send(2, zh)
    exp_pass(3)
    for d in (1, 3, 2):
        got("tx", d - 1, txb.at[d])
    td[j] = txb[0] + txb[1] + txb[2] + txb[3]
    for d, e in others:
        go("td", d * 2 + e - 1, td.at[j], td.at[j], dev(y=ring(y, d), zh=(zh + e) % 2))
    exp_pass(2)

    settle(early + 12)

    for d, e in others[::-1]:
        got("td", d * 2 + e - 1, td.at[ring(y, -d) * 2 + (zh + e) % 2])
    for xx in range(4):
        first, second = td[xx * 2][0:1], td[xx * 2 + 1][0:1]
        total = jnp.concatenate([first[:, 0:64], second[:, 0:64]], axis=1)
        top = jnp.concatenate([first[:, 64:128], second[:, 64:128]], axis=1)
        scale = LOGIT_SCALE / total
        at = pl.ds(xx * 128, 128)
        pos_s[0, at, :] = jnp.broadcast_to(to_col(scale), (128, 128))
        pos_s[1, at, :] = jnp.broadcast_to(
            to_col(-LOGIT_SCALE * ((total - jnp.exp(top)) / total)), (128, 128)
        )

    def score(t):
        for e in (0, 1):
            got("ey", t * 6 + e, ea.at[t, block(ring(y, 3), e)])
            got("ey", t * 6 + 2 + e, ea.at[t, block(ring(y, 1), e)])
            got("ey", t * 6 + 4 + e, ea.at[t, block(ring(y, 2), e)])
        for xx in range(4):
            at = pl.ds(xx * 128, 128)
            for c in (0, 1):
                part = pl.ds(c * 128, 128)
                rest = ea[t, at, part].astype(F32) * pos_s[0, at, :]
                sa[t, at, part] = jnp.where(
                    hits(t, at, c), pos_s[1, at, :], rest
                ).astype(BF16)

    def answers_part(t):
        gap[t] = tn(sa[t], qx[...])
        away = rows((1 - core) * 128, 128)
        go("gc", t, gap.at[t, away], gcr.at[t], dev(core=1 - core))

    def answers_sum(t):
        got("gc", t, gcr.at[t])
        both = gap[t, rows(core * 128, 128), :] + gcr[t]
        if t:
            gzs[t] = both.astype(GZ_WIRE)
            go("gz", t - 1, gzs.at[t], gzr.at[t - 1], dev(zl=ring(zl, -t)))
        else:
            ge[half(1), :] = both

    def queries_part(d):
        part = jnp.zeros((128, 512), F32)
        for t in range(4):
            left = sa[t, rows(ring(x, d) * 128, 128), :]
            part = part + nn(left, aa[rows(ring(zl, -t) * 256, 256), :])
        gqs[d] = part
        if d:
            go("gq", d - 1, gqs.at[d], gqr.at[d - 1], dev(x=ring(x, d)))

    score(2)
    answers_part(2)
    score(3)
    answers_part(3)
    answers_sum(2)
    score(1)
    answers_part(1)
    answers_sum(3)
    score(0)
    queries_part(2)
    answers_sum(1)
    queries_part(1)
    queries_part(3)
    answers_part(0)
    queries_part(0)
    answers_sum(0)

    def radial(h, g):
        at = half(h)
        ge[at, :] = g
        rb[h, 0] = to_row(jnp.sum(g * sc[at, :], axis=1, keepdims=True))
        for d, e in others:
            k = d * 2 + e
            go("rr", h * 7 + k - 1, rb.at[h, 0], rb.at[h, k], dev(y=ring(y, d), zh=(zh + e) % 2))

    def spread(h):
        at = half(h)
        tot = rb[h, 0]
        for d, e in others[::-1]:
            k = d * 2 + e
            got("rr", h * 7 + k - 1, rb.at[h, k])
        for k in range(1, 8):
            tot = tot + rb[h, k]
        rad = to_col(tot[0:1])
        iv = inv_s[at, 0:1]
        out = gain_ref[...] * (iv * ge[at, :] - (iv * iv * iv * rad) * sc[at, :])
        for c in (0, 1):
            gg[j, c, at, :] = out[:, c * 256:(c + 1) * 256].astype(BF16)
        for c in (0, 1):
            part = gg.at[j, c, at]
            go("gh", h * 2 + c, part, part, dev(zh=1 - zh))
        near(h, 0)
        rg_ref[at, :] = out

    def near(h, k):
        e = zh if k == 0 else 1 - zh
        for c in (0, 1):
            part = gg.at[y * 2 + e, c, half(h)]
            if k:
                got("gh", h * 2 + c, part)
            go("gy", h * 12 + k * 6 + c, part, part, right)
            go("gy", h * 12 + k * 6 + 2 + c, part, part, left)
            if straight(h, k):
                go("gy", h * 12 + k * 6 + 4 + c, part, part, dev(y=ring(y, 2)))

    def straight(h, k):
        return h == 1 and k == 1

    def hop(h, k):
        e = zh if k == 0 else 1 - zh
        part = gg.at[ring(y, 3) * 2 + e, 0, half(h)]
        got("gy", h * 12 + k * 6, part)
        go("gy", h * 12 + k * 6 + 4, part, part, right)
        part = gg.at[ring(y, 1) * 2 + e, 1, half(h)]
        got("gy", h * 12 + k * 6 + 3, part)
        go("gy", h * 12 + k * 6 + 5, part, part, left)

    def column_copy(h, t, k, c):
        e = zh if k == 0 else 1 - zh
        xx = e * 2 + c
        d = (xx - x + 4) % 4
        src = gg.at[ring(y, -t) * 2 + e, c, half(h)]
        dst = gx.at[t, rows(x * 256 + h * 128, 128)]
        n = t * 2 + h
        return d, src, dst, copy("gx", (n * 2 + k) * 2 + c, src, dst, dev(x=xx), n * 3 + d - 1)

    def columns(h, t, k):
        arrivals = {0: (), 1: ((1, 1),), 3: ((2, 0),), 2: ((4, 0), (5, 1))}[t]
        if straight(h, k):
            arrivals += {0: (), 1: ((0, 0),), 3: ((3, 1),), 2: ()}[t]
        for n, c in arrivals:
            e = zh if k == 0 else 1 - zh
            got("gy", h * 12 + k * 6 + n, gg.at[ring(y, -t) * 2 + e, c, half(h)])
        for c in (0, 1):
            d, src, dst, remote = column_copy(h, t, k, c)

            @pl.when(d > 0)
            def _():
                remote.start()

            @pl.when(d == 0)
            def _():
                dst[...] = src[...]

    early = len(pending)
    settle(early - 10)
    for d in (1, 3, 2):
        got("gq", d - 1, gqr.at[d - 1])
    radial(0, gqs[0] + gqr[0] + gqr[1] + gqr[2])
    for d in (1, 3, 2):
        got("gz", d - 1, gzr.at[d - 1])
    radial(1, ge[half(1), :] + gzr[0].astype(F32) + gzr[1].astype(F32) + gzr[2].astype(F32))
    spread(0)
    columns(0, 0, 0)
    spread(1)
    columns(1, 0, 0)
    hop(0, 0)
    columns(0, 1, 0)
    columns(0, 3, 0)
    hop(1, 0)
    columns(1, 1, 0)
    columns(1, 3, 0)
    settle(early)
    near(0, 1)
    columns(0, 0, 1)
    columns(0, 2, 0)
    hop(0, 1)
    columns(0, 1, 1)
    columns(0, 3, 1)
    columns(1, 2, 0)
    near(1, 1)
    columns(1, 0, 1)
    columns(0, 2, 1)

    for d in (1, 3, 2):
        got("ax", d - 1, ax.at[rows(ring(x, -d) * 256, 256)])

    def weight_part(t):
        for h in (0, 1):
            for d in (1, 3, 2):
                got("gx", (t * 2 + h) * 3 + d - 1,
                    gx.at[t, rows(ring(x, -d) * 256 + h * 128, 128)])
        part = tn(ax[...], gx[t])
        tb[t, 0] = part[:, 0:128]
        tb[t, 1] = part[:, 128:256]
        go("wc", t, tb.at[t, 1 - core], tcr.at[t], dev(core=1 - core))

    def weight_sum(t):
        got("wc", t, tcr.at[t])
        zz = ring(y, -t)
        d = (zz - zl + 4) % 4
        both = tb[t, core] + tcr[t]

        @pl.when(d > 0)
        def _():
            wzs[d - 1] = both.astype(WZ_WIRE)
            copy("wz", d - 1, wzs.at[d - 1], wzr.at[d - 1], dev(zl=zz)).start()

        @pl.when(d == 0)
        def _():
            wg_ref[...] = both

    columns(1, 1, 1)
    columns(1, 3, 1)
    weight_part(0)
    columns(1, 2, 1)
    weight_sum(0)
    weight_part(1)
    weight_part(3)
    weight_sum(1)
    weight_sum(3)

    weight_part(2)
    weight_sum(2)
    ag_ref[...] = jnp.zeros((256, 512), F32)
    for jj in range(8):
        for c in (0, 1):
            ag_ref[...] += nt(gg[jj, c], w_ref[:, pl.ds(jj * 512 + c * 256, 256)])
    losses = []
    for v in (td[x * 2][0:1], td[x * 2 + 1][0:1]):
        total, top = v[:, 0:64], v[:, 64:128]
        peak = jnp.exp(top)
        losses.append(
            jnp.where(
                total < 4.0 * peak, jnp.log1p((total - peak) / peak), jnp.log(total) - top
            )
        )
    loss_ref[...] = jnp.concatenate(losses, axis=1)
    settle(len(pending))
    for n in range(32):
        d, _, _, remote = column_copy(n // 16, n // 4 % 4, n // 2 % 2, n % 2)

        @pl.when(d > 0)
        def _():
            remote.wait_send()

    for d in (1, 3, 2):
        got("wz", d - 1, wzr.at[d - 1])
    wg_ref[...] += wzr[0].astype(F32) + wzr[1].astype(F32) + wzr[2].astype(F32)
    for d in (1, 2, 3):
        copy("wz", d - 1, wzs.at[d - 1], wzr.at[d - 1], dev(core=1 - core)).wait_send()


def hand_over(*refs):
    copies = [pltpu.make_async_copy(refs[k], refs[4 + k], refs[8].at[k]) for k in range(4)]
    for c in copies:
        c.start()
    for c in copies:
        c.wait()


def body(attn_out, residual, o_weight, norm_gain, positive):
    vmem = pl.BlockSpec(memory_space=pltpu.VMEM)
    shape = jax.ShapeDtypeStruct
    scratch = [
        ((256, 512), BF16), ((256, 512), BF16), ((512, 4096), BF16), ((1, 512), F32),
        ((1, 128), jnp.int32),
        ((4, 3, 128, 512), WIRE), ((4, 2, 64, 512), F32), ((4, 2, 64, 512), WIRE),
        ((4, 2, 128, 512), WIRE), ((4, 128, 512), F32),
        ((2, 128, 512), WIRE), ((2, 128, 512), WIRE), ((256, 512), F32), ((256, 128), F32),
        ((2, 8, 8, 128), F32),
        ((512, 512), BF16), ((1024, 512), BF16), ((4, 8, 128), jnp.int32), ((512, 128), F32),
        ((4, 512, 256), F32), ((4, 2, 2, 32, 256), F32), ((4, 2, 2, 64, 256), F32), ((4, 64, 256), F32), ((4, 64, 256), F32),
        ((2, 512, 128), F32), ((4, 128, 1), F32), ((4, 8, 128), F32), ((8, 8, 128), F32),
        ((4, 512, 256), BF16), ((4, 512, 256), BF16),
        ((4, 256, 512), F32), ((4, 128, 512), F32), ((4, 128, 512), GZ_WIRE),
        ((3, 128, 512), GZ_WIRE), ((4, 128, 512), F32), ((3, 128, 512), F32), ((256, 512), F32),
        ((2, 8, 8, 128), F32),
        ((8, 2, 256, 256), BF16), ((4, 1024, 256), BF16), ((1024, 512), BF16),
        ((4, 2, 512, 128), F32), ((4, 512, 128), F32), ((3, 512, 128), WZ_WIRE),
        ((3, 512, 128), WZ_WIRE),
    ]
    outs = (
        shape((1, 128), F32), shape((256, 512), F32), shape((256, 512), F32),
        shape((512, 128), F32),
    )
    made = pl.pallas_call(
        kernel,
        name="step",
        out_shape=tuple(pltpu.VMEM(v.shape, v.dtype) for v in outs),
        in_specs=[pl.BlockSpec(memory_space=pl.ANY)] * 5,
        out_specs=[vmem] * 4,
        scratch_shapes=[pltpu.VMEM(s, t) for s, t in scratch]
        + [pltpu.SemaphoreType.DMA((n,)) for n in (COUNT, COUNT, 8)],
        compiler_params=pltpu.CompilerParams(
            collective_id=0, has_side_effects=True, vmem_limit_bytes=56 * 1024 * 1024
        ),
    )(
        attn_out.reshape(256, 512), residual.reshape(256, 512), o_weight,
        norm_gain.reshape(1, 512), positive.reshape(1, 128),
    )
    loss, rg, ag, wg = pl.pallas_call(
        hand_over,
        name="hand_over",
        out_shape=outs,
        in_specs=[vmem] * 4,
        out_specs=[pl.BlockSpec(memory_space=pl.ANY)] * 4,
        scratch_shapes=[pltpu.SemaphoreType.DMA((4,))],
        compiler_params=pltpu.CompilerParams(vmem_limit_bytes=4 * 1024 * 1024),
    )(*made)
    return (
        loss.reshape(128), rg.reshape(2, 128, 512), ag.reshape(2, 128, 512), wg,
    )


def solution(mesh):
    placed = (P(None, "dp", "mp"), P(None, "dp", "mp"), P("mp", None), P("mp"), P("dp"))
    return jax.shard_map(
        body,
        mesh=mesh,
        in_specs=placed,
        out_specs=(P("dp"), P(None, "dp", "mp"), P(None, "dp", "mp"), P("mp", "dp")),
        check_vma=False,
    )
```
